256 devices in a mesh: bunch: 16 (over x, y), mp: 16 (over z, core).
Axes of the slice: x: 4, y: 4, z: 8, core: 2. Of those that a mesh axis runs over, the one named last changes fastest.
Arguments:
- phase_space: float32 [4, 256, 65536], P(None, 'bunch', 'mp')
- phase_advance: float32 [2, 256], P(None, 'bunch'), may hold values from 0.3 to 2.8
- centroid_history: float32 [2, 64, 256], P(None, None, 'bunch'), may hold values from -6 to 6
- lr_wake: float32 [16640], replicated, may hold values from -0.046875 to 0.046875
- sr_dipole: float32 [256, 256], replicated, may hold values from -24 to 24
- sr_quad: float32 [256, 256], replicated, may hold values from -24 to 24
- slice_ids: int32 [2, 256, 65536], P(None, 'bunch', 'mp'), may hold values from 0 to 255
Outputs:
- tracked: float32 [4, 256, 65536], P(None, 'bunch', 'mp')
- centroids: float32 [2, 2, 256], P(None, None, 'bunch')
The draws below stay inside these ranges and needn't reach their ends.
All inputs are finite; a program needn't handle non-finite values.
Results may differ from the reference program's by a relative error of at most 0.00019.
Values sent between devices are 32-bit elements; how exact they have to be, the bound alone decides.
A program may use at most 64 MiB of HBM per device.

```python
import jax
import jax.numpy as jnp
from jax import lax

SLICES = 256
HISTORY = 64
TURNS = 2
BUNCHES = 256
MACRO = 65536
LAGS = 16640


def draw_phase_space(key, part):
    key_offset = jax.random.fold_in(key, 11)
    key_noise = jax.random.fold_in(key, 12)
    offsets = jax.random.normal(key_offset, (4, BUNCHES, 1), jnp.float32)
    ramp_up = 0.5 + jnp.arange(MACRO, dtype=jnp.float32) / MACRO
    noise_part = 0.5 * jax.random.normal(key_noise, (4, BUNCHES, MACRO), jnp.float32)
    return offsets * ramp_up[None, None, :] + noise_part


def touch_ends(result, stream_key, smallest, high):
    longest = result.shape.index(max(result.shape))
    spots = []
    for shift in (0, 1):
        where = [jax.random.randint(jax.random.fold_in(stream_key, axis), (), 0, length) for axis, length in enumerate(result.shape)]
        where[longest] = (where[longest] + shift) % result.shape[longest]
        spots.append(tuple(where))
    return result.at[spots[0]].set(smallest).at[spots[1]].set(high)


def level_of(stream_key, extent, shards, least, top_value):
    factor_of, own = 1.0, jax.random.fold_in(stream_key, 6)
    for dim, parts in shards:
        steps = jnp.exp(jax.random.uniform(jax.random.fold_in(own, dim), (parts,), jnp.float32, least / len(shards), top_value / len(shards)))
        factor_of = factor_of * jnp.repeat(steps, extent[dim] // parts).reshape([-1 if axis == dim else 1 for axis in range(len(extent))])
    return factor_of


def scatter_about(stream_key, extent, deviation, most, cuts=(), kind=jnp.bfloat16):
    loudness = level_of(stream_key, extent, cuts, -0.22, 0.18) if cuts else 1.0
    entries = jax.random.normal(stream_key, extent, jnp.float32) * deviation * loudness
    return jnp.minimum(jnp.maximum(entries, -most), most).astype(kind)


def setup_inputs(seed: int = 0) -> dict:
    splits = jax.random.split(jax.random.key(seed), 8)
    phase_space = draw_phase_space(jax.random.fold_in(splits[7], 71), 0)
    phase_advance = jnp.clip(0.3 + 2.5 * jax.random.uniform(splits[1], (2, BUNCHES), jnp.float32) ** level_of(splits[1], (2, BUNCHES), ((1, 16),), -0.2, 0.2), 0.3, 2.8)
    centroid_history = scatter_about(splits[2], (2, HISTORY, BUNCHES), 1.0, 6.0, ((2, 16),), jnp.float32)
    lr_wake = scatter_about(splits[3], (LAGS,), LAGS ** -0.5, 0.046875, (), jnp.float32)
    sr_dipole = scatter_about(splits[4], (SLICES, SLICES), 4.0, 24.0, (), jnp.float32)
    sr_quad = scatter_about(splits[5], (SLICES, SLICES), 4.0, 24.0, (), jnp.float32)
    slice_ids = touch_ends(jax.random.randint(splits[6], (TURNS, BUNCHES, MACRO), 0, SLICES), jax.random.fold_in(splits[6], 1), 0, SLICES - 1).astype(jnp.int32)
    return {"phase_space": phase_space, "phase_advance": phase_advance, "centroid_history": centroid_history, "lr_wake": lr_wake, "sr_dipole": sr_dipole, "sr_quad": sr_quad, "slice_ids": slice_ids}


DETUNE = 0.02


def reference(phase_space, phase_advance, centroid_history, lr_wake, sr_dipole, sr_quad, slice_ids):
    highest = lax.Precision.HIGHEST
    all_bunches = phase_space.shape[1]
    macro_total = phase_space.shape[2]
    length = (HISTORY + 1) * all_bunches
    padded = jnp.concatenate([jnp.zeros((all_bunches,), jnp.float32), lr_wake])
    starts = jnp.arange(all_bunches, dtype=jnp.int32)
    windows = jax.vmap(lambda start_at: lax.dynamic_slice(padded, (start_at,), (length,)))(starts)
    history = centroid_history
    coords = phase_space
    centroid_rows = []
    offsets = (jnp.arange(all_bunches, dtype=jnp.int32) * SLICES)[:, None]
    segments_total = all_bunches * SLICES
    for turn_index in range(TURNS):
        slice_row = slice_ids[turn_index]
        segment = (slice_row + offsets).reshape(-1)
        counts = jax.ops.segment_sum(jnp.ones((segment.shape[0],), jnp.float32), segment, segments_total)
        sum_x = jax.ops.segment_sum(coords[0].reshape(-1), segment, segments_total)
        sum_y = jax.ops.segment_sum(coords[2].reshape(-1), segment, segments_total)
        density = counts.reshape(all_bunches, SLICES) / macro_total
        dipole = jnp.stack([sum_x, sum_y]).reshape(2, all_bunches, SLICES) / macro_total
        centroid = jnp.sum(dipole, axis=2)
        centroid_rows.append(centroid)
        dip_kick = jnp.einsum("pbj,ij->pbi", dipole, sr_dipole, precision=highest)
        quad_kick = jnp.einsum("bj,ij->bi", density, sr_quad, precision=highest)
        all_rows = jnp.concatenate([centroid[:, None, :], history], axis=1)[:, :, ::-1].reshape(2, length)
        far_kick = jnp.einsum("bk,pk->pb", windows, all_rows, precision=highest)
        slice_dip = jnp.take_along_axis(dip_kick, jnp.broadcast_to(slice_row[None], (2,) + slice_row.shape), axis=2)
        slice_quad = jnp.take_along_axis(quad_kick, slice_row, axis=1)
        coord_x, moment_x, coord_y, moment_y = coords[0], coords[1], coords[2], coords[3]
        moment_x = moment_x + slice_dip[0] + slice_quad * coord_x + far_kick[0][:, None]
        moment_y = moment_y + slice_dip[1] - slice_quad * coord_y + far_kick[1][:, None]
        action = coord_x * coord_x + moment_x * moment_x + coord_y * coord_y + moment_y * moment_y
        angle_x = phase_advance[0][:, None] + DETUNE * action
        angle_y = phase_advance[1][:, None] + DETUNE * action
        new_x = jnp.cos(angle_x) * coord_x + jnp.sin(angle_x) * moment_x
        new_mx = -jnp.sin(angle_x) * coord_x + jnp.cos(angle_x) * moment_x
        new_y = jnp.cos(angle_y) * coord_y + jnp.sin(angle_y) * moment_y
        new_my = -jnp.sin(angle_y) * coord_y + jnp.cos(angle_y) * moment_y
        coords = jnp.stack([new_x, new_mx, new_y, new_my])
        history = jnp.concatenate([centroid[:, None, :], history[:, :-1]], axis=1)
    return coords, jnp.stack(centroid_rows, axis=1)
```

```python
import functools

import jax
import jax.numpy as jnp
from jax import lax
from jax.experimental import pallas as pl
from jax.experimental.pallas import tpu as pltpu
from jax.sharding import PartitionSpec as P

SLICES = 256
TURNS = 2
DETUNE = 0.02
LANES = 128
COARSE, FINE = 8, 32
CHUNK = 512
GROUP = 8

F32, BF16, I32 = jnp.float32, jnp.bfloat16, jnp.int32
NT = (((1,), (1,)), ((), ()))
HIGHEST = lax.Precision.HIGHEST


def iota(shape, axis):
    return lax.broadcasted_iota(I32, shape, axis)


def gather_lanes(row, index):
    return jnp.take_along_axis(row, index, axis=1, mode="promise_in_bounds")


def two_pieces(v):
    high = v.astype(BF16).astype(F32)
    return high, v - high


def sin_cos(theta):
    n = jnp.round(theta * 0.6366197723675814)
    r = theta - n * 1.5703125
    r = r - n * 4.837512969970703e-4
    r = r - n * 7.549789948768648e-8
    r = jnp.clip(r, -0.8, 0.8)
    q = n.astype(I32)
    z = r * r
    s = r + r * z * (-1.6666654611e-1 + z * (8.3321608736e-3 + z * -1.9515295891e-4))
    c = 1.0 - 0.5 * z + z * z * (
        4.166664568298827e-2 + z * (-1.388731625493765e-3 + z * 2.443315711809948e-5)
    )
    odd = (q & 1) == 1
    sin, cos = jnp.where(odd, c, s), jnp.where(odd, s, c)
    sin = jnp.where((q & 2) == 2, -sin, sin)
    cos = jnp.where(((q + 1) & 2) == 2, -cos, cos)
    return sin, cos


def kernel(
    rings,
    phase_ref,
    advance_ref,
    hist_ref,
    wake_ref,
    dipole_ref,
    quad_ref,
    ids_ref,
    out_ref,
    cent_ref,
    msg,
    landed,
    far_src,
    far_all,
    tab_src,
    tab_all,
    spread,
    ext,
    toep0,
    rot,
    msg_send,
    msg_recv,
    far_send,
    far_recv,
    tab_send,
    tab_recv,
):
    n_bunch, n_mp = rings
    me_b, me_m = lax.axis_index("bunch"), lax.axis_index("mp")
    bunches, parts = phase_ref.shape[1], phase_ref.shape[2]
    scale = 1.0 / (parts * n_mp)

    barrier = pltpu.get_barrier_semaphore()

    def greet(k, _):
        pl.semaphore_signal(barrier, inc=1, device_id={"mp": lax.rem(me_m + k, n_mp)})
        pl.semaphore_signal(barrier, inc=1, device_id={"bunch": lax.rem(me_b + k, n_bunch)})
        return 0

    lax.fori_loop(1, 16, greet, 0)

    def msg_copy(turn, b):
        return pltpu.make_async_remote_copy(
            src_ref=msg.at[turn, b],
            dst_ref=landed.at[turn, me_m],
            send_sem=msg_send.at[turn, b],
            recv_sem=msg_recv.at[turn, me_m],
            device_id={"mp": b},
        )

    def msg_arrival(turn, sender):
        return pltpu.make_async_remote_copy(
            src_ref=msg.at[turn, sender],
            dst_ref=landed.at[turn, sender],
            send_sem=msg_send.at[turn, sender],
            recv_sem=msg_recv.at[turn, sender],
            device_id={"mp": sender},
        )

    def far_copy(kind, peer):
        return pltpu.make_async_remote_copy(
            src_ref=far_src.at[kind],
            dst_ref=far_all.at[kind, me_b],
            send_sem=far_send.at[kind, peer],
            recv_sem=far_recv.at[kind, me_b],
            device_id={"bunch": peer},
        )

    def far_arrival(kind, peer):
        return pltpu.make_async_remote_copy(
            src_ref=far_src.at[kind],
            dst_ref=far_all.at[kind, peer],
            send_sem=far_send.at[kind, peer],
            recv_sem=far_recv.at[kind, peer],
            device_id={"bunch": peer},
        )

    def tab_copy(turn, peer):
        return pltpu.make_async_remote_copy(
            src_ref=tab_src.at[turn],
            dst_ref=tab_all.at[turn, me_m],
            send_sem=tab_send.at[turn, peer],
            recv_sem=tab_recv.at[turn, me_m],
            device_id={"mp": peer},
        )

    def tab_arrival(turn, peer):
        return pltpu.make_async_remote_copy(
            src_ref=tab_src.at[turn],
            dst_ref=tab_all.at[turn, peer],
            send_sem=tab_send.at[turn, peer],
            recv_sem=tab_recv.at[turn, peer],
            device_id={"mp": peer},
        )

    def others(me, n, act):
        def step(k, _):
            act(lax.rem(me + k, n))
            return 0

        lax.fori_loop(1, n, step, 0)

    row8, lane8 = iota((8, LANES), 0), iota((8, LANES), 1)
    place = lax.rem(me_b, 8) * bunches

    share = hist_ref.shape[1] // n_mp
    own = jnp.concatenate(
        [hist_ref[0, pl.ds(me_m * share, share), :], hist_ref[1, pl.ds(me_m * share, share), :]], axis=0
    )
    own = jnp.concatenate([own, jnp.zeros((8, LANES - bunches), F32)], axis=1)
    own = pltpu.roll(own, place, 1)
    far_src[2] = own
    far_all[2, me_b] = own
    spread[...] = jnp.zeros_like(spread)

    def send_sums(turn, sums_x, sums_y):
        spread[0, pl.ds(place, bunches), :] = sums_x * scale
        spread[1, pl.ds(place, bunches), :] = sums_y * scale
        ones = jnp.ones((8, LANES), F32)
        row_x = lax.dot_general(ones, spread[0], NT, precision=HIGHEST, preferred_element_type=F32)
        row_y = lax.dot_general(ones, spread[1], NT, precision=HIGHEST, preferred_element_type=F32)
        tile = jnp.where(row8 == 0, row_x, row_y)
        far_src[turn] = tile
        far_all[turn, me_b] = tile

    def lane_sums(p):
        def step(c, acc):
            return acc + phase_ref[p, :, pl.ds(pl.multiple_of(c * LANES, LANES), LANES)]

        return lax.fori_loop(0, parts // LANES, step, jnp.zeros((bunches, LANES), F32), unroll=8)

    send_sums(0, lane_sums(0), lane_sums(2))

    diag = iota((bunches, LANES), 0) == iota((bunches, LANES), 1)
    for p in range(2):
        wide = jnp.concatenate([advance_ref[p : p + 1, :], jnp.zeros((1, LANES - bunches), F32)], axis=1)
        column = jnp.sum(jnp.where(diag, jnp.broadcast_to(wide, (bunches, LANES)), 0.0), axis=1, keepdims=True)
        sin, cos = sin_cos(jnp.broadcast_to(column, (bunches, LANES)))
        rot[2 * p] = cos
        rot[2 * p + 1] = sin

    pl.semaphore_wait(barrier, n_mp + n_bunch - 2)
    others(me_b, n_bunch, lambda peer: far_copy(2, peer).start())
    others(me_b, n_bunch, lambda peer: far_copy(0, peer).start())

    iota_c = iota((COARSE, CHUNK), 0)
    iota_f = iota((FINE, CHUNK), 0)
    own_lanes = lax.shift_right_logical(lane8, 5) == (row8 & 3)

    def bin_bunch(turn, source, b):
        acc = None
        for c in range(parts // CHUNK):
            at = pl.ds(c * CHUNK, CHUNK)
            ids = ids_ref[turn, pl.ds(b, 1), at]
            x = source[0, pl.ds(b, 1), at]
            y = source[2, pl.ds(b, 1), at]
            coarse = iota_c == lax.shift_right_logical(ids, 5)
            fine = jnp.where(iota_f == (ids & (FINE - 1)), 1.0, 0.0).astype(BF16)
            rows = [jnp.where(coarse, 1.0, 0.0)]
            for v in (*two_pieces(x), *two_pieces(y)):
                rows.append(jnp.where(coarse, jnp.broadcast_to(v, (COARSE, CHUNK)), 0.0))
            weighted = jnp.concatenate(rows, axis=0).astype(BF16)
            part = lax.dot_general(weighted, fine, NT, preferred_element_type=F32)
            acc = part if acc is None else acc + part
        tiles = []
        for v in (acc[8:16] + acc[16:24], acc[24:32] + acc[32:40], acc[0:8]):
            v = jnp.where(own_lanes, jnp.concatenate([v] * 4, axis=1), 0.0)
            v = v + pltpu.roll(v, 1, 0)
            tiles.append(v + pltpu.roll(v, 2, 0))
        last = row8 & 3
        tile = jnp.where(
            last == 3,
            tiles[0],
            jnp.where(last == 0, pltpu.roll(tiles[1], 1, 0), pltpu.roll(tiles[2], 2, 0)),
        )
        msg[turn, b] = tile * scale

    def finish(turn, b):
        row_x = jnp.broadcast_to(ext[turn, 0, pl.ds(b, 1), :], (8, LANES))
        row_y = jnp.broadcast_to(ext[turn, 1, pl.ds(b, 1), :], (8, LANES))
        tile = jnp.where(row8 == 2, row_x, jnp.where(row8 == 6, row_y, msg[turn, b]))
        msg[turn, b] = tile

    def toeplitz_rows(r, half, sub):
        d = place_all + sub * 8 + row8 - (LANES * half + lane8) - 1
        c = d & (SLICES - 1)
        index = c & (LANES - 1)
        low = jnp.broadcast_to(wake_ref[pl.ds(2 * r, 1), :], (8, LANES))
        high = jnp.broadcast_to(wake_ref[pl.ds(2 * r + 1, 1), :], (8, LANES))
        return jnp.where(c >= LANES, gather_lanes(high, index), gather_lanes(low, index)), d >= 0

    place_all = me_b * bunches

    def collected(kind):
        halves = []
        for half in range(2):
            total = far_all[kind, 8 * half]
            for k in range(1, 8):
                total = total + far_all[kind, 8 * half + k]
            halves.append(total)
        return halves

    def row_of(tile, k):
        return jnp.broadcast_to(tile[k : k + 1, :], (8, LANES))

    top = hist_ref.shape[1]

    def far_first():
        others(me_b, n_bunch, lambda peer: far_arrival(2, peer).wait_recv())
        others(me_b, n_bunch, lambda peer: far_arrival(0, peer).wait_recv())
        hist, cent = collected(2), collected(0)
        kept = jnp.where(me_m == n_mp - 1, 0.0, 1.0)
        for sub in range(2):
            at = pl.ds(8 * sub, 8)
            sums = [[jnp.zeros((8, LANES), F32) for _ in range(2)] for _ in range(2)]
            for half in range(2):
                g0, upper = toeplitz_rows(0, half, sub)
                g1, _ = toeplitz_rows(1, half, sub)
                u0 = jnp.where(upper, g0, 0.0)
                u1 = jnp.where(upper, g1, g0)
                toep0[half, at, :] = u0
                for p in range(2):
                    c = row_of(cent[half], p)
                    sums[0][p] = sums[0][p] + u0 * c
                    sums[1][p] = sums[1][p] + u1 * c
                first = me_m * share
                g = [
                    toeplitz_rows(jnp.minimum(first + k, top), half, sub)[0] for k in range(share + 2)
                ]
                for k in range(share):
                    near = jnp.where(upper, g[k + 1], g[k])
                    later = jnp.where(upper, g[k + 2], g[k + 1])
                    if k == share - 1:
                        later = later * kept
                    for p in range(2):
                        h = row_of(hist[half], p * share + k)
                        sums[0][p] = sums[0][p] + near * h
                        sums[1][p] = sums[1][p] + later * h
            for turn in range(2):
                for p in range(2):
                    ext[turn, p, at, :] = sums[turn][p]

    def far_second():
        others(me_b, n_bunch, lambda peer: far_arrival(1, peer).wait_recv())
        cent = collected(1)
        for sub in range(2):
            at = pl.ds(8 * sub, 8)
            for p in range(2):
                total = ext[1, p, at, :]
                for half in range(2):
                    total = total + toep0[half, at, :] * row_of(cent[half], p)
                ext[1, p, at, :] = total

    early = bunches // 2

    def one_turn(turn, source):
        def bin_early(k, _):
            bin_bunch(turn, source, lax.rem(me_m + 1 + k, n_mp))
            return 0

        lax.fori_loop(0, early, bin_early, 0)
        (far_first if turn == 0 else far_second)()

        def send_early(k, _):
            b = lax.rem(me_m + 1 + k, n_mp)
            finish(turn, b)
            msg_copy(turn, b).start()
            return 0

        lax.fori_loop(0, early, send_early, 0)

        def bin_late(k, _):
            b = lax.rem(me_m + 1 + k, n_mp)
            bin_bunch(turn, source, b)
            finish(turn, b)
            msg_copy(turn, b).start()
            return 0

        lax.fori_loop(early, bunches - 1, bin_late, 0)
        bin_bunch(turn, source, me_m)
        finish(turn, me_m)
        landed[turn, me_m] = msg[turn, me_m]

        others(me_m, n_mp, lambda peer: msg_arrival(turn, peer).wait_recv())
        total = landed[turn, 0]
        for k in range(1, 16):
            total = total + landed[turn, k]
        wide = jnp.concatenate([total, pltpu.roll(total, 4, 0)], axis=1)
        dip = lax.dot_general(wide, dipole_ref[...], NT, precision=HIGHEST, preferred_element_type=F32)
        quad = lax.dot_general(wide, quad_ref[...], NT, precision=HIGHEST, preferred_element_type=F32)
        moved = jnp.sum(wide, axis=1, keepdims=True)
        ext_sum = jnp.sum(total, axis=1, keepdims=True)
        low, high = dip[:, :LANES], dip[:, LANES:]
        far_x = jnp.broadcast_to(ext_sum[2:3], (1, LANES))
        far_y = jnp.broadcast_to(ext_sum[6:7], (1, LANES))
        tab_src[turn] = jnp.concatenate(
            [
                low[3:4] + far_x,
                high[3:4] + far_x,
                low[4:5] + far_y,
                high[4:5] + far_y,
                quad[5:6, :LANES],
                quad[5:6, LANES:],
                jnp.broadcast_to(moved[3:4], (1, LANES)),
                jnp.broadcast_to(moved[4:5], (1, LANES)),
            ],
            axis=0,
        )
        others(me_m, n_mp, lambda peer: tab_copy(turn, peer).start())
        tab_all[turn, me_m] = tab_src[turn]
        others(me_m, n_mp, lambda peer: tab_arrival(turn, peer).wait_recv())

        table = tab_all.at[turn]

        def column(k, first, count):
            return jnp.concatenate([table[first + n, k : k + 1, :] for n in range(count)], axis=0)

        for p in range(2):
            spot = jnp.where(diag, column(6 + p, 0, bunches), 0.0)
            cent_ref[p, turn : turn + 1, :] = jnp.sum(spot, axis=0, keepdims=True)[:, :bunches]

        sums = []
        for g in range(bunches // GROUP):
            at = pl.ds(g * GROUP, GROUP)
            rows = [column(k, g * GROUP, GROUP) for k in range(6)]
            cos_x, sin_x, cos_y, sin_y = (rot[k, at, :] for k in range(4))

            def kick(c, acc):
                lanes = pl.ds(pl.multiple_of(c * LANES, LANES), LANES)
                ids = ids_ref[turn, at, lanes]
                x, mx, y, my = (source[k, at, lanes] for k in range(4))
                index, upper = ids & (LANES - 1), ids >= LANES
                kx, ky, kq = (
                    jnp.where(upper, gather_lanes(rows[2 * k + 1], index), gather_lanes(rows[2 * k], index))
                    for k in range(3)
                )
                mx = mx + (kx + kq * x)
                my = my + (ky - kq * y)
                action = x * x + mx * mx + y * y + my * my
                sin, cos = sin_cos(DETUNE * action)
                x, mx = cos * x + sin * mx, cos * mx - sin * x
                y, my = cos * y + sin * my, cos * my - sin * y
                x, mx = cos_x * x + sin_x * mx, cos_x * mx - sin_x * x
                y, my = cos_y * y + sin_y * my, cos_y * my - sin_y * y
                out_ref[0, at, lanes] = x
                out_ref[1, at, lanes] = mx
                out_ref[2, at, lanes] = y
                out_ref[3, at, lanes] = my
                return acc[0] + x, acc[1] + y

            zero = jnp.zeros((GROUP, LANES), F32)
            sums.append(lax.fori_loop(0, parts // LANES, kick, (zero, zero), unroll=4))
        if turn == 0:
            send_sums(1, *(jnp.concatenate([s[p] for s in sums], axis=0) for p in range(2)))
            others(me_b, n_bunch, lambda peer: far_copy(1, peer).start())

    one_turn(0, phase_ref)
    one_turn(1, out_ref)

    for turn in range(TURNS):
        others(me_m, n_mp, lambda peer: msg_copy(turn, peer).wait_send())
        others(me_m, n_mp, lambda peer: tab_copy(turn, peer).wait_send())
    for kind in range(3):
        others(me_b, n_bunch, lambda peer: far_copy(kind, peer).wait_send())


def body(phase_space, phase_advance, centroid_history, lr_wake, sr_dipole, sr_quad, slice_ids):
    n_bunch, n_mp = lax.axis_size("bunch"), lax.axis_size("mp")
    bunches = phase_space.shape[1]
    vmem = pl.BlockSpec(memory_space=pltpu.VMEM)
    dma = pltpu.SemaphoreType.DMA
    return tuple(
        pl.pallas_call(
            functools.partial(kernel, (n_bunch, n_mp)),
            out_shape=(
                jax.ShapeDtypeStruct(phase_space.shape, F32),
                jax.ShapeDtypeStruct((2, TURNS, bunches), F32),
            ),
            in_specs=[vmem] * 7,
            out_specs=(vmem, vmem),
            scratch_shapes=[
                pltpu.VMEM((TURNS, bunches, 8, LANES), F32),
                pltpu.VMEM((TURNS, n_mp, 8, LANES), F32),
                pltpu.VMEM((3, 8, LANES), F32),
                pltpu.VMEM((3, n_bunch, 8, LANES), F32),
                pltpu.VMEM((TURNS, 8, LANES), F32),
                pltpu.VMEM((TURNS, n_mp, 8, LANES), F32),
                pltpu.VMEM((2, LANES, LANES), F32),
                pltpu.VMEM((TURNS, 2, bunches, LANES), F32),
                pltpu.VMEM((2, bunches, LANES), F32),
                pltpu.VMEM((4, bunches, LANES), F32),
                dma((TURNS, n_mp)),
                dma((TURNS, n_mp)),
                dma((3, n_bunch)),
                dma((3, n_bunch)),
                dma((TURNS, n_mp)),
                dma((TURNS, n_mp)),
            ],
            compiler_params=pltpu.CompilerParams(
                collective_id=0, has_side_effects=True, vmem_limit_bytes=32 << 20
            ),
            cost_estimate=pl.CostEstimate(
                flops=4 * 65536 * 256, bytes_accessed=3 << 20, transcendentals=0
            ),
        )(
            phase_space,
            phase_advance,
            centroid_history,
            lr_wake.reshape(-1, LANES),
            sr_dipole,
            sr_quad,
            slice_ids,
        )
    )


def solution(mesh):
    placed = (
        P(None, "bunch", "mp"),
        P(None, "bunch"),
        P(None, None, "bunch"),
        P(),
        P(),
        P(),
        P(None, "bunch", "mp"),
    )
    return jax.shard_map(
        body,
        mesh=mesh,
        in_specs=placed,
        out_specs=(P(None, "bunch", "mp"), P(None, None, "bunch")),
        check_vma=False,
    )
```

```python
import functools

import jax
import jax.numpy as jnp
from jax import lax
from jax.experimental import pallas as pl
from jax.experimental.pallas import tpu as pltpu
from jax.sharding import PartitionSpec as P

SLICES = 256
TURNS = 2
DETUNE = 0.02
LANES = 128
COARSE, FINE = 8, 32
CHUNK = 512
GROUP = 8
AT_ONCE = 4
WIDTH = 512
SPANS = 2

F32, BF16, I32 = jnp.float32, jnp.bfloat16, jnp.int32
NT = (((1,), (1,)), ((), ()))
HIGHEST = lax.Precision.HIGHEST


def iota(shape, axis):
    return lax.broadcasted_iota(I32, shape, axis)


def gather_lanes(row, index):
    return jnp.take_along_axis(row, index, axis=1, mode="promise_in_bounds")


def two_pieces(v):
    high = v.astype(BF16).astype(F32)
    return high, v - high


def sin_cos(theta):
    n = jnp.round(theta * 0.6366197723675814)
    r = theta - n * 1.5703125
    r = r - n * 4.837512969970703e-4
    r = r - n * 7.549789948768648e-8
    r = jnp.clip(r, -0.8, 0.8)
    q = n.astype(I32)
    z = r * r
    s = r + r * z * (-1.6666654611e-1 + z * (8.3321608736e-3 + z * -1.9515295891e-4))
    c = 1.0 - 0.5 * z + z * z * (
        4.166664568298827e-2 + z * (-1.388731625493765e-3 + z * 2.443315711809948e-5)
    )
    odd = (q & 1) == 1
    sin, cos = jnp.where(odd, c, s), jnp.where(odd, s, c)
    sin = jnp.where((q & 2) == 2, -sin, sin)
    cos = jnp.where(((q + 1) & 2) == 2, -cos, cos)
    return sin, cos


def turned(ids, coords, rows, rot):
    width = ids.shape[1]
    index, upper = ids & (LANES - 1), ids >= LANES

    def looked_up(k):
        pieces = []
        for c in range(width // LANES):
            at = slice(c * LANES, (c + 1) * LANES)
            low, high = gather_lanes(rows[2 * k], index[:, at]), gather_lanes(rows[2 * k + 1], index[:, at])
            pieces.append(jnp.where(upper[:, at], high, low))
        return jnp.concatenate(pieces, axis=1)

    x, mx, y, my = coords
    kx, ky, kq = looked_up(0), looked_up(1), looked_up(2)
    mx = mx + (kx + kq * x)
    my = my + (ky - kq * y)
    action = x * x + mx * mx + y * y + my * my
    sin, cos = sin_cos(DETUNE * action)
    cos_x, sin_x, cos_y, sin_y = (jnp.concatenate([r] * (width // LANES), axis=1) for r in rot)
    x, mx = cos * x + sin * mx, cos * mx - sin * x
    y, my = cos * y + sin * my, cos * my - sin * y
    x, mx = cos_x * x + sin_x * mx, cos_x * mx - sin_x * x
    y, my = cos_y * y + sin_y * my, cos_y * my - sin_y * y
    return x, mx, y, my


def track_kernel(
    rings,
    phase_hbm,
    advance_hbm,
    hist_hbm,
    wake_hbm,
    dipole_hbm,
    quad_hbm,
    ids_hbm,
    mid_ref,
    next_ids,
    rows_ref,
    rot,
    cent_ref,
    phase_ref,
    first_ids,
    advance_ref,
    hist_ref,
    wake_ref,
    dipole_ref,
    quad_ref,
    msg,
    landed,
    hist_src,
    hist_all,
    sum_src,
    sum_all,
    far_src,
    far_all,
    tab_src,
    tab_all,
    spread,
    ext,
    toep0,
    load,
    msg_send,
    msg_recv,
    hist_send,
    hist_recv,
    sum_send,
    sum_recv,
    far_send,
    far_recv,
    tab_send,
    tab_recv,
):
    n_bunch, n_mp = rings
    me_b, me_m = lax.axis_index("bunch"), lax.axis_index("mp")
    bunches, parts = mid_ref.shape[1], mid_ref.shape[2]
    turns_back = hist_ref.shape[2]
    share = turns_back // n_mp
    scale = 1.0 / (parts * n_mp)

    barrier = pltpu.get_barrier_semaphore()

    def greet(k, _):
        pl.semaphore_signal(barrier, inc=1, device_id={"mp": lax.rem(me_m + k, n_mp)})
        pl.semaphore_signal(barrier, inc=1, device_id={"bunch": lax.rem(me_b + k, n_bunch)})
        return 0

    lax.fori_loop(1, 16, greet, 0)

    loads = [
        pltpu.make_async_copy(source, target, load.at[k])
        for k, (source, target) in enumerate(
            (
                (phase_hbm.at[0], phase_ref.at[0]),
                (phase_hbm.at[2], phase_ref.at[2]),
                (ids_hbm.at[0], first_ids),
                (hist_hbm, hist_ref),
                (wake_hbm, wake_ref),
                (advance_hbm, advance_ref),
                (dipole_hbm, dipole_ref),
                (quad_hbm, quad_ref),
                (phase_hbm.at[1], phase_ref.at[1]),
                (phase_hbm.at[3], phase_ref.at[3]),
                (ids_hbm.at[1], next_ids),
            )
        )
    ]
    for copy in loads:
        copy.start()

    class Exchange:
        def __init__(self, axis, me, n, source, target, send, recv):
            self.axis, self.me, self.n = axis, me, n
            self.source, self.target, self.send, self.recv = source, target, send, recv

        def copy(self, peer, slot):
            return pltpu.make_async_remote_copy(
                src_ref=self.source,
                dst_ref=self.target.at[slot],
                send_sem=self.send.at[peer],
                recv_sem=self.recv.at[slot],
                device_id={self.axis: peer},
            )

        def each(self, act):
            def step(k, _):
                act(lax.rem(self.me + lax.rem(k + self.n // 2 - 1, self.n - 1) + 1, self.n))
                return 0

            lax.fori_loop(0, self.n - 1, step, 0)

        def start(self):
            self.each(lambda peer: self.copy(peer, self.me).start())

        def arrive(self):
            self.each(lambda peer: self.copy(peer, peer).wait_recv())

        def leave(self):
            self.each(lambda peer: self.copy(peer, self.me).wait_send())

    hist_x = Exchange("bunch", me_b, n_bunch, hist_src, hist_all, hist_send, hist_recv)
    sum_x = [
        Exchange("bunch", me_b, n_bunch, sum_src.at[t], sum_all.at[t], sum_send.at[t], sum_recv.at[t])
        for t in range(TURNS)
    ]
    far_x = [
        Exchange("mp", me_m, n_mp, far_src.at[t], far_all.at[t], far_send.at[t], far_recv.at[t])
        for t in range(TURNS)
    ]
    tab_x = [
        Exchange("mp", me_m, n_mp, tab_src.at[t], tab_all.at[t], tab_send.at[t], tab_recv.at[t])
        for t in range(TURNS)
    ]

    def msg_copy(turn, b, slot):
        return pltpu.make_async_remote_copy(
            src_ref=msg.at[turn, b],
            dst_ref=landed.at[turn, slot],
            send_sem=msg_send.at[turn, b],
            recv_sem=msg_recv.at[turn, slot],
            device_id={"mp": b},
        )

    row8, lane8 = iota((8, LANES), 0), iota((8, LANES), 1)
    place = lax.rem(me_b, 8) * bunches
    ones = jnp.ones((8, LANES), F32)

    def lane_row(block):
        return lax.dot_general(ones, block, NT, precision=HIGHEST, preferred_element_type=F32)

    spread[...] = jnp.zeros_like(spread)

    def send_sums(turn, sums_x, sums_y):
        spread[0, pl.ds(place, bunches), :] = sums_x * scale
        spread[1, pl.ds(place, bunches), :] = sums_y * scale
        rows = jnp.concatenate([lane_row(spread[0])[:1], lane_row(spread[1])[:1]], axis=0)
        sum_src[turn] = rows
        sum_all[turn, me_b] = rows
        sum_x[turn].start()

    def lane_sums(p):
        def step(c, acc):
            return acc + phase_ref[p, :, pl.ds(pl.multiple_of(c * LANES, LANES), LANES)]

        return lax.fori_loop(0, parts // LANES, step, jnp.zeros((bunches, LANES), F32), unroll=8)

    loads[3].wait()
    pick = iota((8, turns_back), 1) == me_m * share + (iota((8, turns_back), 0) & (share - 1))
    halves = iota((8, turns_back), 0) < share
    own = None
    for p in range(2):
        spread[p, pl.ds(place, bunches), :turns_back] = hist_ref[p]
        chosen = jnp.where(pick & (halves if p == 0 else ~halves), 1.0, 0.0)
        part = lax.dot_general(
            chosen, spread[p, :, :turns_back], NT, precision=HIGHEST, preferred_element_type=F32
        )
        own = part if own is None else own + part
    hist_src[...] = own
    hist_all[me_b] = own

    loads[0].wait()
    loads[1].wait()
    sums = (lane_sums(0), lane_sums(2))
    pl.semaphore_wait(barrier, n_mp + n_bunch - 2)
    send_sums(0, *sums)
    hist_x.start()
    loads[2].wait()

    iota_c = iota((COARSE, CHUNK), 0)
    iota_f = iota((FINE, CHUNK), 0)
    own_lanes = lax.shift_right_logical(lane8, 5) == (row8 & 3)

    def bin_bunch(ids_ref, source, b):
        acc = None
        for c in range(parts // CHUNK):
            at = pl.ds(c * CHUNK, CHUNK)
            ids = ids_ref[pl.ds(b, 1), at]
            x = source[0, pl.ds(b, 1), at]
            y = source[2, pl.ds(b, 1), at]
            coarse = iota_c == lax.shift_right_logical(ids, 5)
            fine = jnp.where(iota_f == (ids & (FINE - 1)), 1.0, 0.0).astype(BF16)
            rows = [jnp.where(coarse, 1.0, 0.0)]
            for v in (*two_pieces(x), *two_pieces(y)):
                rows.append(jnp.where(coarse, jnp.broadcast_to(v, (COARSE, CHUNK)), 0.0))
            weighted = jnp.concatenate(rows, axis=0).astype(BF16)
            part = lax.dot_general(weighted, fine, NT, preferred_element_type=F32)
            acc = part if acc is None else acc + part
        return acc

    def as_tile(acc):
        tiles = []
        for v in (acc[8:16] + acc[16:24], acc[24:32] + acc[32:40], acc[0:8]):
            v = jnp.where(own_lanes, jnp.concatenate([v] * 4, axis=1), 0.0)
            v = v + pltpu.roll(v, 1, 0)
            tiles.append(v + pltpu.roll(v, 2, 0))
        last = row8 & 3
        tile = jnp.where(
            last == 3,
            tiles[0],
            jnp.where(last == 0, pltpu.roll(tiles[1], 1, 0), pltpu.roll(tiles[2], 2, 0)),
        )
        return tile * scale

    chips, chip = n_mp // 2, lax.div(me_m, 2)
    core = lax.rem(me_m, 2)

    def owner(k):
        u, side = lax.div(k, 2), lax.rem(k, 2)
        reach = chips // 2 - lax.div(u + 1, 2)
        there = lax.rem(chip + reach * (2 * lax.rem(u, 2) - 1) + chips, chips)
        return there * 2 + lax.rem(core + 1 + side, 2)

    def bin_all(turn, ids_ref, source):
        def bin_some(first, count):
            owners = [owner(first + k) for k in range(count)]
            accs = [bin_bunch(ids_ref, source, b) for b in owners]
            return owners, [as_tile(acc) for acc in accs]

        def step(k, _):
            owners, tiles = bin_some(k * AT_ONCE, AT_ONCE)
            for b, tile in zip(owners, tiles):
                msg[turn, b] = tile
            for b in owners:
                msg_copy(turn, b, me_m).start()
            return 0

        lax.fori_loop(0, bunches // AT_ONCE - 1, step, 0)
        owners, tiles = bin_some(bunches - AT_ONCE, AT_ONCE)
        for b, tile in zip(owners[:-1], tiles[:-1]):
            msg[turn, b] = tile
        landed[turn, me_m] = tiles[-1]
        for b in owners[:-1]:
            msg_copy(turn, b, me_m).start()

    def others(act):
        def step(k, _):
            act(lax.rem(me_m + k, n_mp))
            return 0

        lax.fori_loop(1, n_mp, step, 0)

    def toeplitz_rows(r, half, sub):
        d = me_b * bunches + sub * 8 + row8 - (LANES * half + lane8) - 1
        c = d & (SLICES - 1)
        index = c & (LANES - 1)
        low = jnp.broadcast_to(wake_ref[pl.ds(2 * r, 1), :], (8, LANES))
        high = jnp.broadcast_to(wake_ref[pl.ds(2 * r + 1, 1), :], (8, LANES))
        return jnp.where(c >= LANES, gather_lanes(high, index), gather_lanes(low, index)), d >= 0

    def collected(ref):
        halves = []
        for half in range(2):
            total = ref[8 * half]
            for k in range(1, 8):
                total = total + ref[8 * half + k]
            halves.append(total)
        return halves

    def row_of(tile, k):
        return jnp.broadcast_to(tile[k : k + 1, :], (8, LANES))

    def send_far(turn):
        row = lane_row(ext[turn])[:1]
        far_src[turn] = row
        far_all[turn, me_m] = row
        far_x[turn].start()

    def far_first():
        loads[4].wait()
        sum_x[0].arrive()
        hist_x.arrive()
        hist, cent = collected(hist_all), collected(sum_all.at[0])
        kept = jnp.where(me_m == n_mp - 1, 0.0, 1.0)
        for sub in range(2):
            sums = [[jnp.zeros((8, LANES), F32) for _ in range(2)] for _ in range(2)]
            for half in range(2):
                g0, upper = toeplitz_rows(0, half, sub)
                g1, _ = toeplitz_rows(1, half, sub)
                u0 = jnp.where(upper, g0, 0.0)
                u1 = jnp.where(upper, g1, g0)
                toep0[half, pl.ds(8 * sub, 8), :] = u0
                for p in range(2):
                    c = row_of(cent[half], p)
                    sums[0][p] = sums[0][p] + u0 * c
                    sums[1][p] = sums[1][p] + u1 * c
                first = me_m * share
                g = [
                    toeplitz_rows(jnp.minimum(first + k, turns_back), half, sub)[0]
                    for k in range(share + 2)
                ]
                for k in range(share):
                    near = jnp.where(upper, g[k + 1], g[k])
                    later = jnp.where(upper, g[k + 2], g[k + 1])
                    if k == share - 1:
                        later = later * kept
                    for p in range(2):
                        h = row_of(hist[half], p * share + k)
                        sums[0][p] = sums[0][p] + near * h
                        sums[1][p] = sums[1][p] + later * h
            for turn in range(2):
                for p in range(2):
                    ext[turn, pl.ds(p * bunches + 8 * sub, 8), :] = sums[turn][p]
        send_far(0)

    def far_second():
        sum_x[1].arrive()
        cent = collected(sum_all.at[1])
        for sub in range(2):
            for p in range(2):
                at = pl.ds(p * bunches + 8 * sub, 8)
                total = ext[1, at, :]
                for half in range(2):
                    total = total + toep0[half, pl.ds(8 * sub, 8), :] * row_of(cent[half], p)
                ext[1, at, :] = total
        send_far(1)

    def kick_table(turn):
        others(lambda peer: msg_copy(turn, peer, peer).wait_recv())
        total = landed[turn, 0]
        for k in range(1, 16):
            total = total + landed[turn, k]
        wide = jnp.concatenate([total, pltpu.roll(total, 4, 0)], axis=1)
        dip = lax.dot_general(wide, dipole_ref[...], NT, precision=HIGHEST, preferred_element_type=F32)
        quad = lax.dot_general(wide, quad_ref[...], NT, precision=HIGHEST, preferred_element_type=F32)
        moved = jnp.sum(wide, axis=1, keepdims=True)
        low, high = dip[:, :LANES], dip[:, LANES:]
        tab_src[turn] = jnp.concatenate(
            [
                low[3:4],
                high[3:4],
                low[4:5],
                high[4:5],
                quad[5:6, :LANES],
                quad[5:6, LANES:],
                jnp.broadcast_to(moved[3:4], (1, LANES)),
                jnp.broadcast_to(moved[4:5], (1, LANES)),
            ],
            axis=0,
        )
        tab_x[turn].start()
        tab_all[turn, me_m] = tab_src[turn]

    full_row, full_lane = iota((bunches, LANES), 0), iota((bunches, LANES), 1)

    def lay_rows(turn):
        far_x[turn].arrive()
        total = far_all[turn, 0]
        for k in range(1, n_mp):
            total = total + far_all[turn, k]
        total = jnp.broadcast_to(total, (bunches, LANES))
        far = [
            jnp.sum(jnp.where(full_lane == full_row + p * bunches, total, 0.0), axis=1, keepdims=True)
            for p in range(2)
        ]
        tab_x[turn].arrive()

        def column(k):
            return jnp.concatenate([tab_all[turn, n, k : k + 1, :] for n in range(bunches)], axis=0)

        for k in range(6):
            row = column(k)
            rows_ref[k] = row + far[k // 2] if k < 4 else row
        for p in range(2):
            spot = jnp.where(full_row == full_lane, column(6 + p), 0.0)
            cent_ref[p, turn : turn + 1, :] = jnp.sum(spot, axis=0, keepdims=True)[:, :bunches]

    bin_all(0, first_ids, phase_ref)
    far_first()

    loads[5].wait()
    for p in range(2):
        wide = jnp.concatenate([advance_ref[p : p + 1, :], jnp.zeros((1, LANES - bunches), F32)], axis=1)
        wide = jnp.broadcast_to(wide, (bunches, LANES))
        column = jnp.sum(jnp.where(full_row == full_lane, wide, 0.0), axis=1, keepdims=True)
        sin, cos = sin_cos(jnp.broadcast_to(column, (bunches, LANES)))
        rot[2 * p] = cos
        rot[2 * p + 1] = sin

    loads[6].wait()
    loads[7].wait()
    kick_table(0)
    loads[8].wait()
    loads[9].wait()
    loads[10].wait()
    lay_rows(0)

    sums = []
    for g in range(bunches // GROUP):
        at = pl.ds(g * GROUP, GROUP)
        rows = [rows_ref[k, at, :] for k in range(6)]
        turn_by = [rot[k, at, :] for k in range(4)]

        def kick(c, acc):
            lanes = pl.ds(pl.multiple_of(c * WIDTH, WIDTH), WIDTH)
            new = turned(first_ids[at, lanes], [phase_ref[k, at, lanes] for k in range(4)], rows, turn_by)
            for k in range(4):
                mid_ref[k, at, lanes] = new[k]
            acc = list(acc)
            for s in range(WIDTH // LANES):
                cut = slice(s * LANES, (s + 1) * LANES)
                acc = [acc[0] + new[0][:, cut], acc[1] + new[2][:, cut]]
            return tuple(acc)

        zero = jnp.zeros((GROUP, LANES), F32)
        sums.append(lax.fori_loop(0, parts // WIDTH, kick, (zero, zero)))
    send_sums(1, *(jnp.concatenate([s[p] for s in sums], axis=0) for p in range(2)))

    bin_all(1, next_ids, mid_ref)
    kick_table(1)
    far_second()
    lay_rows(1)

    for turn in range(TURNS):
        others(lambda peer: msg_copy(turn, peer, me_m).wait_send())
        for exchange in (tab_x[turn], far_x[turn], sum_x[turn]):
            exchange.leave()
    hist_x.leave()


def last_kernel(mid_ref, ids_ref, rows_ref, rot, cent_in, out_hbm, cent_hbm, out_ref, cent_ref, sems):
    bunches, parts = mid_ref.shape[1], mid_ref.shape[2]
    cent_ref[...] = cent_in[...]
    copies = [pltpu.make_async_copy(cent_ref, cent_hbm, sems.at[0])]
    copies[0].start()
    span = parts // SPANS
    for g in range(bunches // GROUP):
        at = pl.ds(g * GROUP, GROUP)
        rows = [rows_ref[k, at, :] for k in range(6)]
        turn_by = [rot[k, at, :] for k in range(4)]
        for part in range(SPANS):

            def kick(c, _):
                lanes = pl.ds(pl.multiple_of(part * span + c * WIDTH, WIDTH), WIDTH)
                new = turned(ids_ref[at, lanes], [mid_ref[k, at, lanes] for k in range(4)], rows, turn_by)
                for k in range(4):
                    out_ref[k, at, lanes] = new[k]
                return 0

            lax.fori_loop(0, span // WIDTH, kick, 0)
            block = (slice(None), at, pl.ds(part * span, span))
            copies.append(
                pltpu.make_async_copy(out_ref.at[block], out_hbm.at[block], sems.at[len(copies)])
            )
            copies[-1].start()
    for copy in copies:
        copy.wait()


def body(phase_space, phase_advance, centroid_history, lr_wake, sr_dipole, sr_quad, slice_ids):
    n_bunch, n_mp = lax.axis_size("bunch"), lax.axis_size("mp")
    bunches, parts = phase_space.shape[1:]
    turns_back = centroid_history.shape[1]
    wake_rows = lr_wake.shape[0] // LANES
    vmem, hbm = pl.BlockSpec(memory_space=pltpu.VMEM), pl.BlockSpec(memory_space=pltpu.HBM)
    dma = pltpu.SemaphoreType.DMA

    def held(*shape, dtype=F32):
        return pltpu.VMEM(shape, dtype)

    cent_shape = jax.ShapeDtypeStruct((2, TURNS, bunches), F32)
    state = pl.pallas_call(
        functools.partial(track_kernel, (n_bunch, n_mp)),
        out_shape=(
            jax.ShapeDtypeStruct(phase_space.shape, F32),
            jax.ShapeDtypeStruct((bunches, parts), I32),
            jax.ShapeDtypeStruct((6, bunches, LANES), F32),
            jax.ShapeDtypeStruct((4, bunches, LANES), F32),
            cent_shape,
        ),
        in_specs=[hbm] * 7,
        out_specs=(vmem,) * 5,
        scratch_shapes=[
            held(4, bunches, parts),
            held(bunches, parts, dtype=I32),
            held(2, bunches),
            held(2, bunches, turns_back),
            held(wake_rows, LANES),
            held(SLICES, SLICES),
            held(SLICES, SLICES),
            held(TURNS, bunches, 8, LANES),
            held(TURNS, n_mp, 8, LANES),
            held(8, LANES),
            held(n_bunch, 8, LANES),
            held(TURNS, 2, LANES),
            held(TURNS, n_bunch, 2, LANES),
            held(TURNS, 1, LANES),
            held(TURNS, n_mp, 1, LANES),
            held(TURNS, 8, LANES),
            held(TURNS, n_mp, 8, LANES),
            held(2, LANES, LANES),
            held(TURNS, LANES, LANES),
            held(2, bunches, LANES),
            dma((11,)),
            dma((TURNS, n_mp)),
            dma((TURNS, n_mp)),
            dma((n_bunch,)),
            dma((n_bunch,)),
            dma((TURNS, n_bunch)),
            dma((TURNS, n_bunch)),
            dma((TURNS, n_mp)),
            dma((TURNS, n_mp)),
            dma((TURNS, n_mp)),
            dma((TURNS, n_mp)),
        ],
        compiler_params=pltpu.CompilerParams(
            collective_id=0, has_side_effects=True, vmem_limit_bytes=40 << 20
        ),
        cost_estimate=pl.CostEstimate(flops=4 * 65536 * 256, bytes_accessed=3 << 20, transcendentals=0),
        name="track",
    )(
        *(
            pltpu.with_memory_space_constraint(a, pltpu.HBM)
            for a in (
                phase_space,
                phase_advance,
                jnp.transpose(centroid_history, (0, 2, 1)),
                lr_wake.reshape(-1, LANES),
                sr_dipole,
                sr_quad,
                slice_ids,
            )
        )
    )
    return tuple(
        pl.pallas_call(
            last_kernel,
            out_shape=(jax.ShapeDtypeStruct(phase_space.shape, F32), cent_shape),
            in_specs=[vmem] * 5,
            out_specs=(hbm, hbm),
            scratch_shapes=[
                held(*phase_space.shape),
                held(2, TURNS, bunches),
                dma((1 + SPANS * bunches // GROUP,)),
            ],
            compiler_params=pltpu.CompilerParams(vmem_limit_bytes=16 << 20),
            cost_estimate=pl.CostEstimate(flops=100 * 65536, bytes_accessed=1 << 20, transcendentals=0),
            name="last",
        )(*state)
    )


def solution(mesh):
    placed = (
        P(None, "bunch", "mp"),
        P(None, "bunch"),
        P(None, None, "bunch"),
        P(),
        P(),
        P(),
        P(None, "bunch", "mp"),
    )
    return jax.shard_map(
        body,
        mesh=mesh,
        in_specs=placed,
        out_specs=(P(None, "bunch", "mp"), P(None, None, "bunch")),
        check_vma=False,
    )
```

```python
import functools

import jax
import jax.numpy as jnp
from jax import lax
from jax.experimental import pallas as pl
from jax.experimental.pallas import tpu as pltpu
from jax.sharding import PartitionSpec as P

SLICES = 256
TURNS = 2
DETUNE = 0.02
LANES = 128
COARSE, FINE = 8, 32
CHUNK = 512
GROUP = 8
AT_ONCE = 8
WIDTH = 512
SPANS = 2

F32, BF16, I32 = jnp.float32, jnp.bfloat16, jnp.int32
NT = (((1,), (1,)), ((), ()))
HIGHEST = lax.Precision.HIGHEST


def iota(shape, axis):
    return lax.broadcasted_iota(I32, shape, axis)


def gather_lanes(row, index):
    return jnp.take_along_axis(row, index, axis=1, mode="promise_in_bounds")


def two_pieces(v):
    high = v.astype(BF16).astype(F32)
    return high, v - high


def sin_cos(theta):
    n = jnp.round(theta * 0.6366197723675814)
    r = theta - n * 1.5703125
    r = r - n * 4.837512969970703e-4
    r = r - n * 7.549789948768648e-8
    r = jnp.clip(r, -0.8, 0.8)
    q = n.astype(I32)
    z = r * r
    s = r + r * z * (-1.6666654611e-1 + z * (8.3321608736e-3 + z * -1.9515295891e-4))
    c = 1.0 - 0.5 * z + z * z * (
        4.166664568298827e-2 + z * (-1.388731625493765e-3 + z * 2.443315711809948e-5)
    )
    odd = (q & 1) == 1
    sin, cos = jnp.where(odd, c, s), jnp.where(odd, s, c)
    sin = jnp.where((q & 2) == 2, -sin, sin)
    cos = jnp.where(((q + 1) & 2) == 2, -cos, cos)
    return sin, cos


def turned(ids, coords, rows, rot):
    width = ids.shape[1]
    index, upper = ids & (LANES - 1), ids >= LANES

    def looked_up(k):
        pieces = []
        for c in range(width // LANES):
            at = slice(c * LANES, (c + 1) * LANES)
            low, high = gather_lanes(rows[2 * k], index[:, at]), gather_lanes(rows[2 * k + 1], index[:, at])
            pieces.append(jnp.where(upper[:, at], high, low))
        return jnp.concatenate(pieces, axis=1)

    x, mx, y, my = coords
    kx, ky, kq = looked_up(0), looked_up(1), looked_up(2)
    mx = mx + (kx + kq * x)
    my = my + (ky - kq * y)
    action = x * x + mx * mx + y * y + my * my
    sin, cos = sin_cos(DETUNE * action)
    cos_x, sin_x, cos_y, sin_y = (jnp.concatenate([r] * (width // LANES), axis=1) for r in rot)
    x, mx = cos * x + sin * mx, cos * mx - sin * x
    y, my = cos * y + sin * my, cos * my - sin * y
    x, mx = cos_x * x + sin_x * mx, cos_x * mx - sin_x * x
    y, my = cos_y * y + sin_y * my, cos_y * my - sin_y * y
    return x, mx, y, my


def track_kernel(
    rings,
    phase_hbm,
    advance_hbm,
    hist_hbm,
    wake_hbm,
    dipole_hbm,
    quad_hbm,
    ids_hbm,
    mid_ref,
    next_ids,
    rows_ref,
    rot,
    cent_ref,
    phase_ref,
    first_ids,
    advance_ref,
    hist_ref,
    wake_ref,
    dipole_ref,
    quad_ref,
    msg,
    landed,
    hist_src,
    hist_all,
    sum_src,
    sum_all,
    far_src,
    far_all,
    tab_src,
    tab_all,
    ext,
    toep,
    load,
    msg_send,
    msg_recv,
    hist_send,
    hist_recv,
    sum_send,
    sum_recv,
    far_send,
    far_recv,
    tab_send,
    tab_recv,
):
    n_bunch, n_mp = rings
    me_b, me_m = lax.axis_index("bunch"), lax.axis_index("mp")
    bunches, parts = mid_ref.shape[1], mid_ref.shape[2]
    turns_back = hist_ref.shape[2]
    share = turns_back // n_mp
    scale = 1.0 / (parts * n_mp)

    barrier = pltpu.get_barrier_semaphore()

    def greet(k, _):
        pl.semaphore_signal(barrier, inc=1, device_id={"mp": lax.rem(me_m + k, n_mp)})
        pl.semaphore_signal(barrier, inc=1, device_id={"bunch": lax.rem(me_b + k, n_bunch)})
        return 0

    lax.fori_loop(1, 16, greet, 0)

    loads = [
        pltpu.make_async_copy(source, target, load.at[k])
        for k, (source, target) in enumerate(
            (
                (phase_hbm.at[0], phase_ref.at[0]),
                (phase_hbm.at[2], phase_ref.at[2]),
                (ids_hbm.at[0], first_ids),
                (hist_hbm, hist_ref),
                (wake_hbm, wake_ref),
                (advance_hbm, advance_ref),
                (dipole_hbm, dipole_ref),
                (quad_hbm, quad_ref),
                (phase_hbm.at[1], phase_ref.at[1]),
                (phase_hbm.at[3], phase_ref.at[3]),
                (ids_hbm.at[1], next_ids),
            )
        )
    ]
    for copy in loads:
        copy.start()

    def by_reach(n, step):
        return sorted(range(1, n), key=lambda k: -min(k // step, (n - k) // step))

    class Exchange:
        def __init__(self, axis, me, offsets, source, target, send, recv):
            self.axis, self.me, self.offsets = axis, me, offsets
            self.source, self.target, self.send, self.recv = source, target, send, recv

        def start(self):
            for k in self.offsets:
                pltpu.make_async_remote_copy(
                    src_ref=self.source,
                    dst_ref=self.target.at[self.me],
                    send_sem=self.send,
                    recv_sem=self.recv,
                    device_id={self.axis: lax.rem(self.me + k, len(self.offsets) + 1)},
                ).start()

        def all_of_them(self):
            block = self.target.at[pl.ds(0, len(self.offsets))]
            return pltpu.make_async_remote_copy(
                src_ref=block,
                dst_ref=block,
                send_sem=self.send,
                recv_sem=self.recv,
                device_id={self.axis: lax.rem(self.me + 1, len(self.offsets) + 1)},
            )

        def arrive(self):
            self.all_of_them().wait_recv()

        def leave(self):
            self.all_of_them().wait_send()

    across, along = by_reach(n_bunch, 1), by_reach(n_mp, 2)
    hist_x = Exchange("bunch", me_b, across, hist_src, hist_all, hist_send, hist_recv)
    sum_x = [
        Exchange("bunch", me_b, across, sum_src.at[t], sum_all.at[t], sum_send.at[t], sum_recv.at[t])
        for t in range(TURNS)
    ]
    far_x = [
        Exchange("mp", me_m, along, far_src.at[t], far_all.at[t], far_send.at[t], far_recv.at[t])
        for t in range(TURNS)
    ]
    tab_x = [
        Exchange("mp", me_m, along, tab_src.at[t], tab_all.at[t], tab_send.at[t], tab_recv.at[t])
        for t in range(TURNS)
    ]
    msg_x = [
        Exchange("mp", me_m, along, None, landed.at[t], msg_send.at[t], msg_recv.at[t]) for t in range(TURNS)
    ]

    def send_msg(turn, b):
        pltpu.make_async_remote_copy(
            src_ref=msg.at[turn, b],
            dst_ref=landed.at[turn, me_m],
            send_sem=msg_send.at[turn],
            recv_sem=msg_recv.at[turn],
            device_id={"mp": b},
        ).start()

    row8, lane8 = iota((8, LANES), 0), iota((8, LANES), 1)
    place = lax.rem(me_b, 8) * bunches

    def pieces(block):
        parts = []
        for _ in range(3):
            parts.append(block.astype(BF16))
            block = block - parts[-1].astype(F32)
        return jnp.concatenate(parts, axis=1)

    def to_lanes(chosen, block):
        rows = lax.dot_general(
            jnp.concatenate([chosen.astype(BF16)] * 3, axis=1), pieces(block), NT, preferred_element_type=F32
        )
        return jnp.concatenate([rows, jnp.zeros((16, LANES - block.shape[0]), F32)], axis=1)

    def send_sums(turn, sums_x, sums_y):
        both = to_lanes(jnp.ones((16, LANES), F32), jnp.concatenate([sums_x, sums_y], axis=0) * scale)[:8]
        x = pltpu.roll(jnp.where(lane8 < bunches, both, 0.0), place, 1)
        y = jnp.where((lane8 >= bunches) & (lane8 < 2 * bunches), both, 0.0)
        y = pltpu.roll(y, lax.rem(place + LANES - bunches, LANES), 1)
        rows = jnp.where(row8 == 0, x, y)[:2]
        sum_src[turn] = rows
        sum_all[turn, me_b] = rows
        sum_x[turn].start()

    def lane_sums(p):
        def step(c, acc):
            return acc + phase_ref[p, :, pl.ds(pl.multiple_of(c * LANES, LANES), LANES)]

        return lax.fori_loop(0, parts // LANES, step, jnp.zeros((bunches, LANES), F32), unroll=8)

    def send_history():
        loads[3].wait()
        r, c = iota((16, 2 * turns_back), 0), iota((16, 2 * turns_back), 1)
        chosen = jnp.where(c == (r // share) * turns_back + me_m * share + (r & (share - 1)), 1.0, 0.0)
        own = to_lanes(chosen, jnp.concatenate([hist_ref[0], hist_ref[1]], axis=1))[:8]
        own = pltpu.roll(own, place, 1)
        hist_src[...] = own
        hist_all[me_b] = own
        hist_x.start()

    loads[0].wait()
    loads[1].wait()
    loads[2].wait()

    iota_c = iota((COARSE, CHUNK), 0)
    iota_f = iota((FINE, CHUNK), 0)
    own_lanes = lax.shift_right_logical(lane8, 5) == (row8 & 3)

    def bin_bunch(ids_ref, source, b):
        acc = None
        for c in range(parts // CHUNK):
            at = pl.ds(c * CHUNK, CHUNK)
            ids = ids_ref[pl.ds(b, 1), at]
            x = source[0, pl.ds(b, 1), at]
            y = source[2, pl.ds(b, 1), at]
            coarse = iota_c == lax.shift_right_logical(ids, 5)
            fine = jnp.where(iota_f == (ids & (FINE - 1)), 1.0, 0.0).astype(BF16)
            rows = [jnp.where(coarse, 1.0, 0.0)]
            for v in (*two_pieces(x), *two_pieces(y)):
                rows.append(jnp.where(coarse, jnp.broadcast_to(v, (COARSE, CHUNK)), 0.0))
            weighted = jnp.concatenate(rows, axis=0).astype(BF16)
            part = lax.dot_general(weighted, fine, NT, preferred_element_type=F32)
            acc = part if acc is None else acc + part
        return acc

    def as_tile(acc):
        tiles = []
        for v in (acc[8:16] + acc[16:24], acc[24:32] + acc[32:40], acc[0:8]):
            v = jnp.where(own_lanes, jnp.concatenate([v] * 4, axis=1), 0.0)
            v = v + pltpu.roll(v, 1, 0)
            tiles.append(v + pltpu.roll(v, 2, 0))
        last = row8 & 3
        tile = jnp.where(
            last == 3,
            tiles[0],
            jnp.where(last == 0, pltpu.roll(tiles[1], 1, 0), pltpu.roll(tiles[2], 2, 0)),
        )
        return tile * scale

    chips, chip = n_mp // 2, lax.div(me_m, 2)
    core = lax.rem(me_m, 2)

    def owner(k):
        u, side = k // 2, k % 2
        reach = (chips // 2 - (u + 1) // 2) * (2 * (u % 2) - 1)
        there = lax.rem(chip + reach + chips, chips)
        return there * 2 + lax.rem(core + 1 + side, 2)

    def bin_all(turn, ids_ref, source, between):
        for first in range(0, bunches, AT_ONCE):
            owners = [owner(first + k) for k in range(AT_ONCE)]
            tiles = [as_tile(bin_bunch(ids_ref, source, b)) for b in owners]
            if first == 0:
                between()
            if first + AT_ONCE == bunches:
                landed[turn, me_m] = tiles[-1]
                owners = owners[:-1]
            for b, tile in zip(owners, tiles):
                msg[turn, b] = tile
            for b in owners:
                send_msg(turn, b)

    def toeplitz_rows(r, half, sub):
        d = me_b * bunches + sub * 8 + row8 - (LANES * half + lane8) - 1
        c = d & (SLICES - 1)
        index = c & (LANES - 1)
        low = jnp.broadcast_to(wake_ref[pl.ds(2 * r, 1), :], (8, LANES))
        high = jnp.broadcast_to(wake_ref[pl.ds(2 * r + 1, 1), :], (8, LANES))
        return jnp.where(c >= LANES, gather_lanes(high, index), gather_lanes(low, index)), d >= 0

    def collected(ref):
        halves = []
        for half in range(2):
            total = ref[8 * half]
            for k in range(1, 8):
                total = total + ref[8 * half + k]
            halves.append(total)
        return halves

    def row_of(tile, k):
        return jnp.broadcast_to(tile[k : k + 1, :], (8, LANES))

    def send_far(turn):
        row = to_lanes(jnp.ones((16, LANES), F32), ext[turn])[:1]
        far_src[turn] = row
        far_all[turn, me_m] = row
        far_x[turn].start()

    def lay_wake():
        loads[4].wait()
        kept = jnp.where(me_m == n_mp - 1, 0.0, 1.0)
        first = me_m * share
        for sub in range(2):
            at = pl.ds(8 * sub, 8)
            for half in range(2):
                g0, upper = toeplitz_rows(0, half, sub)
                g1, _ = toeplitz_rows(1, half, sub)
                toep[0, half, at, :] = jnp.where(upper, g0, 0.0)
                toep[1, half, at, :] = jnp.where(upper, g1, g0)
                g = [
                    toeplitz_rows(jnp.minimum(first + k, turns_back), half, sub)[0]
                    for k in range(share + 2)
                ]
                for k in range(share + 1):
                    near = jnp.where(upper, g[k + 1], g[k])
                    toep[2 + k, half, at, :] = near
                toep[2 + share + 1, half, at, :] = near * kept

    def far_first():
        sum_x[0].arrive()
        hist_x.arrive()
        hist, cent = collected(hist_all), collected(sum_all.at[0])
        for sub in range(2):
            at = pl.ds(8 * sub, 8)
            sums = [[jnp.zeros((8, LANES), F32) for _ in range(2)] for _ in range(2)]
            for half in range(2):
                u = [toep[k, half, at, :] for k in range(share + 4)]
                for p in range(2):
                    c = row_of(cent[half], p)
                    sums[0][p] = sums[0][p] + u[0] * c
                    sums[1][p] = sums[1][p] + u[1] * c
                for k in range(share):
                    for p in range(2):
                        h = row_of(hist[half], p * share + k)
                        sums[0][p] = sums[0][p] + u[2 + k] * h
                        later = u[3 + k] if k < share - 1 else u[3 + share]
                        sums[1][p] = sums[1][p] + later * h
            for turn in range(2):
                for p in range(2):
                    ext[turn, pl.ds(p * bunches + 8 * sub, 8), :] = sums[turn][p]
        send_far(0)

    def far_second():
        sum_x[1].arrive()
        cent = collected(sum_all.at[1])
        for sub in range(2):
            for p in range(2):
                at = pl.ds(p * bunches + 8 * sub, 8)
                total = ext[1, at, :]
                for half in range(2):
                    total = total + toep[0, half, pl.ds(8 * sub, 8), :] * row_of(cent[half], p)
                ext[1, at, :] = total
        send_far(1)

    def kick_table(turn):
        msg_x[turn].arrive()
        total = landed[turn, 0]
        for k in range(1, 16):
            total = total + landed[turn, k]
        wide = jnp.concatenate([total, pltpu.roll(total, 4, 0)], axis=1)
        dip = lax.dot_general(wide, dipole_ref[...], NT, precision=HIGHEST, preferred_element_type=F32)
        quad = lax.dot_general(wide, quad_ref[...], NT, precision=HIGHEST, preferred_element_type=F32)
        moved = jnp.sum(wide, axis=1, keepdims=True)
        low, high = dip[:, :LANES], dip[:, LANES:]
        tab_src[turn] = jnp.concatenate(
            [
                low[3:4],
                high[3:4],
                low[4:5],
                high[4:5],
                quad[5:6, :LANES],
                quad[5:6, LANES:],
                jnp.broadcast_to(moved[3:4], (1, LANES)),
                jnp.broadcast_to(moved[4:5], (1, LANES)),
            ],
            axis=0,
        )
        tab_x[turn].start()
        tab_all[turn, me_m] = tab_src[turn]

    full_row, full_lane = iota((bunches, LANES), 0), iota((bunches, LANES), 1)

    def lay_rows(turn):
        far_x[turn].arrive()
        total = far_all[turn, 0]
        for k in range(1, n_mp):
            total = total + far_all[turn, k]
        total = jnp.broadcast_to(total, (bunches, LANES))
        far = [
            jnp.sum(jnp.where(full_lane == full_row + p * bunches, total, 0.0), axis=1, keepdims=True)
            for p in range(2)
        ]
        tab_x[turn].arrive()

        def column(k):
            return jnp.concatenate([tab_all[turn, n, k : k + 1, :] for n in range(bunches)], axis=0)

        for k in range(6):
            row = column(k)
            rows_ref[k] = row + far[k // 2] if k < 4 else row
        for p in range(2):
            spot = jnp.where(full_row == full_lane, column(6 + p), 0.0)
            cent_ref[p, turn : turn + 1, :] = jnp.sum(spot, axis=0, keepdims=True)[:, :bunches]

    def first_sends():
        pl.semaphore_wait(barrier, n_mp + n_bunch - 2)
        send_sums(0, lane_sums(0), lane_sums(2))
        send_history()

    bin_all(0, first_ids, phase_ref, first_sends)
    lay_wake()

    loads[5].wait()
    for p in range(2):
        wide = jnp.concatenate([advance_ref[p : p + 1, :], jnp.zeros((1, LANES - bunches), F32)], axis=1)
        wide = jnp.broadcast_to(wide, (bunches, LANES))
        column = jnp.sum(jnp.where(full_row == full_lane, wide, 0.0), axis=1, keepdims=True)
        sin, cos = sin_cos(jnp.broadcast_to(column, (bunches, LANES)))
        rot[2 * p] = cos
        rot[2 * p + 1] = sin

    loads[6].wait()
    loads[7].wait()
    kick_table(0)
    far_first()
    loads[8].wait()
    loads[9].wait()
    loads[10].wait()
    lay_rows(0)

    sums = []
    for g in range(bunches // GROUP):
        at = pl.ds(g * GROUP, GROUP)
        rows = [rows_ref[k, at, :] for k in range(6)]
        turn_by = [rot[k, at, :] for k in range(4)]

        def kick(c, acc):
            lanes = pl.ds(pl.multiple_of(c * WIDTH, WIDTH), WIDTH)
            new = turned(first_ids[at, lanes], [phase_ref[k, at, lanes] for k in range(4)], rows, turn_by)
            for k in range(4):
                mid_ref[k, at, lanes] = new[k]
            acc = list(acc)
            for s in range(WIDTH // LANES):
                cut = slice(s * LANES, (s + 1) * LANES)
                acc = [acc[0] + new[0][:, cut], acc[1] + new[2][:, cut]]
            return tuple(acc)

        zero = jnp.zeros((GROUP, LANES), F32)
        sums.append(lax.fori_loop(0, parts // WIDTH, kick, (zero, zero), unroll=4))
    send_sums(1, *(jnp.concatenate([s[p] for s in sums], axis=0) for p in range(2)))

    bin_all(1, next_ids, mid_ref, lambda: None)
    kick_table(1)
    far_second()
    lay_rows(1)

    for turn in range(TURNS):
        for exchange in (msg_x[turn], tab_x[turn], far_x[turn], sum_x[turn]):
            exchange.leave()
    hist_x.leave()


def last_kernel(mid_ref, ids_ref, rows_ref, rot, cent_in, out_hbm, cent_hbm, out_ref, cent_ref, sems):
    bunches, parts = mid_ref.shape[1], mid_ref.shape[2]
    cent_ref[...] = cent_in[...]
    copies = [pltpu.make_async_copy(cent_ref, cent_hbm, sems.at[0])]
    copies[0].start()
    span = parts // SPANS
    for g in range(bunches // GROUP):
        at = pl.ds(g * GROUP, GROUP)
        rows = [rows_ref[k, at, :] for k in range(6)]
        turn_by = [rot[k, at, :] for k in range(4)]
        for part in range(SPANS):

            def kick(c, _):
                lanes = pl.ds(pl.multiple_of(part * span + c * WIDTH, WIDTH), WIDTH)
                new = turned(ids_ref[at, lanes], [mid_ref[k, at, lanes] for k in range(4)], rows, turn_by)
                for k in range(4):
                    out_ref[k, at, lanes] = new[k]
                return 0

            lax.fori_loop(0, span // WIDTH, kick, 0, unroll=4)
            block = (slice(None), at, pl.ds(part * span, span))
            copies.append(
                pltpu.make_async_copy(out_ref.at[block], out_hbm.at[block], sems.at[len(copies)])
            )
            copies[-1].start()
    for copy in copies:
        copy.wait()


def body(phase_space, phase_advance, centroid_history, lr_wake, sr_dipole, sr_quad, slice_ids):
    n_bunch, n_mp = lax.axis_size("bunch"), lax.axis_size("mp")
    bunches, parts = phase_space.shape[1:]
    turns_back = centroid_history.shape[1]
    wake_rows = lr_wake.shape[0] // LANES
    vmem, hbm = pl.BlockSpec(memory_space=pltpu.VMEM), pl.BlockSpec(memory_space=pltpu.HBM)
    dma = pltpu.SemaphoreType.DMA

    def held(*shape, dtype=F32):
        return pltpu.VMEM(shape, dtype)

    cent_shape = jax.ShapeDtypeStruct((2, TURNS, bunches), F32)
    state = pl.pallas_call(
        functools.partial(track_kernel, (n_bunch, n_mp)),
        out_shape=(
            jax.ShapeDtypeStruct(phase_space.shape, F32),
            jax.ShapeDtypeStruct((bunches, parts), I32),
            jax.ShapeDtypeStruct((6, bunches, LANES), F32),
            jax.ShapeDtypeStruct((4, bunches, LANES), F32),
            cent_shape,
        ),
        in_specs=[hbm] * 7,
        out_specs=(vmem,) * 5,
        scratch_shapes=[
            held(4, bunches, parts),
            held(bunches, parts, dtype=I32),
            held(2, bunches),
            held(2, bunches, turns_back),
            held(wake_rows, LANES),
            held(SLICES, SLICES),
            held(SLICES, SLICES),
            held(TURNS, bunches, 8, LANES),
            held(TURNS, n_mp, 8, LANES),
            held(8, LANES),
            held(n_bunch, 8, LANES),
            held(TURNS, 2, LANES),
            held(TURNS, n_bunch, 2, LANES),
            held(TURNS, 1, LANES),
            held(TURNS, n_mp, 1, LANES),
            held(TURNS, 8, LANES),
            held(TURNS, n_mp, 8, LANES),
            held(TURNS, 2 * bunches, LANES),
            held(4 + turns_back // n_mp, 2, bunches, LANES),
            dma((11,)),
            dma((TURNS,)),
            dma((TURNS,)),
            dma,
            dma,
            dma((TURNS,)),
            dma((TURNS,)),
            dma((TURNS,)),
            dma((TURNS,)),
            dma((TURNS,)),
            dma((TURNS,)),
        ],
        compiler_params=pltpu.CompilerParams(
            collective_id=0, has_side_effects=True, vmem_limit_bytes=40 << 20
        ),
        cost_estimate=pl.CostEstimate(flops=4 * 65536 * 256, bytes_accessed=3 << 20, transcendentals=0),
        name="track",
    )(
        *(
            pltpu.with_memory_space_constraint(a, pltpu.HBM)
            for a in (
                phase_space,
                phase_advance,
                jnp.transpose(centroid_history, (0, 2, 1)),
                lr_wake.reshape(-1, LANES),
                sr_dipole,
                sr_quad,
                slice_ids,
            )
        )
    )
    return tuple(
        pl.pallas_call(
            last_kernel,
            out_shape=(jax.ShapeDtypeStruct(phase_space.shape, F32), cent_shape),
            in_specs=[vmem] * 5,
            out_specs=(hbm, hbm),
            scratch_shapes=[
                held(*phase_space.shape),
                held(2, TURNS, bunches),
                dma((1 + SPANS * bunches // GROUP,)),
            ],
            compiler_params=pltpu.CompilerParams(vmem_limit_bytes=16 << 20),
            cost_estimate=pl.CostEstimate(flops=100 * 65536, bytes_accessed=1 << 20, transcendentals=0),
            name="last",
        )(*state)
    )


def solution(mesh):
    placed = (
        P(None, "bunch", "mp"),
        P(None, "bunch"),
        P(None, None, "bunch"),
        P(),
        P(),
        P(),
        P(None, "bunch", "mp"),
    )
    return jax.shard_map(
        body,
        mesh=mesh,
        in_specs=placed,
        out_specs=(P(None, "bunch", "mp"), P(None, None, "bunch")),
        check_vma=False,
    )
```

```python
import functools

import jax
import jax.numpy as jnp
from jax import lax
from jax.experimental import pallas as pl
from jax.experimental.pallas import tpu as pltpu
from jax.sharding import PartitionSpec as P

SLICES = 256
TURNS = 2
DETUNE = 0.02
LANES = 128
COARSE, FINE = 8, 32
CHUNK = 512
GROUP = 8
AT_ONCE = 8
WIDTH = 512
SPANS = 2

F32, BF16, I32 = jnp.float32, jnp.bfloat16, jnp.int32
NT = (((1,), (1,)), ((), ()))
HIGHEST = lax.Precision.HIGHEST


def iota(shape, axis):
    return lax.broadcasted_iota(I32, shape, axis)


def gather_lanes(row, index):
    return jnp.take_along_axis(row, index, axis=1, mode="promise_in_bounds")


def two_pieces(v):
    high = v.astype(BF16).astype(F32)
    return high, v - high


def sin_cos(theta):
    n = jnp.round(theta * 0.6366197723675814)
    r = theta - n * 1.5703125
    r = r - n * 4.837512969970703e-4
    r = r - n * 7.549789948768648e-8
    r = jnp.clip(r, -0.8, 0.8)
    q = n.astype(I32)
    z = r * r
    s = r + r * z * (-1.6666654611e-1 + z * (8.3321608736e-3 + z * -1.9515295891e-4))
    c = 1.0 - 0.5 * z + z * z * (
        4.166664568298827e-2 + z * (-1.388731625493765e-3 + z * 2.443315711809948e-5)
    )
    odd = (q & 1) == 1
    sin, cos = jnp.where(odd, c, s), jnp.where(odd, s, c)
    sin = jnp.where((q & 2) == 2, -sin, sin)
    cos = jnp.where(((q + 1) & 2) == 2, -cos, cos)
    return sin, cos


def turned(ids, coords, rows, rot):
    width = ids.shape[1]
    index, upper = ids & (LANES - 1), ids >= LANES

    def looked_up(k):
        pieces = []
        for c in range(width // LANES):
            at = slice(c * LANES, (c + 1) * LANES)
            low, high = gather_lanes(rows[2 * k], index[:, at]), gather_lanes(rows[2 * k + 1], index[:, at])
            pieces.append(jnp.where(upper[:, at], high, low))
        return jnp.concatenate(pieces, axis=1)

    x, mx, y, my = coords
    kx, ky, kq = looked_up(0), looked_up(1), looked_up(2)
    mx = mx + (kx + kq * x)
    my = my + (ky - kq * y)
    action = x * x + mx * mx + y * y + my * my
    sin, cos = sin_cos(DETUNE * action)
    cos_x, sin_x, cos_y, sin_y = (jnp.concatenate([r] * (width // LANES), axis=1) for r in rot)
    x, mx = cos * x + sin * mx, cos * mx - sin * x
    y, my = cos * y + sin * my, cos * my - sin * y
    x, mx = cos_x * x + sin_x * mx, cos_x * mx - sin_x * x
    y, my = cos_y * y + sin_y * my, cos_y * my - sin_y * y
    return x, mx, y, my


def track_kernel(
    rings,
    phase_hbm,
    advance_hbm,
    hist_hbm,
    wake_hbm,
    dipole_hbm,
    quad_hbm,
    ids_hbm,
    mid_ref,
    next_ids,
    rows_ref,
    rot,
    cent_ref,
    phase_ref,
    first_ids,
    advance_ref,
    hist_ref,
    wake_ref,
    dipole_ref,
    quad_ref,
    msg,
    landed,
    hist_src,
    hist_all,
    sum_src,
    sum_all,
    far_src,
    far_all,
    tab_src,
    tab_all,
    ext,
    toep,
    partial,
    split,
    load,
    msg_send,
    msg_recv,
    hist_send,
    hist_recv,
    sum_send,
    sum_recv,
    far_send,
    far_recv,
    tab_send,
    tab_recv,
):
    n_bunch, n_mp = rings
    me_b, me_m = lax.axis_index("bunch"), lax.axis_index("mp")
    bunches, parts = mid_ref.shape[1], mid_ref.shape[2]
    turns_back = hist_ref.shape[2]
    share = turns_back // n_mp
    scale = 1.0 / (parts * n_mp)

    loads = [
        pltpu.make_async_copy(source, target, load.at[k])
        for k, (source, target) in enumerate(
            (
                (phase_hbm.at[0], phase_ref.at[0]),
                (phase_hbm.at[2], phase_ref.at[2]),
                (ids_hbm.at[0], first_ids),
                (hist_hbm, hist_ref),
                (wake_hbm, wake_ref),
                (advance_hbm, advance_ref),
                (dipole_hbm, dipole_ref),
                (quad_hbm, quad_ref),
                (phase_hbm.at[1], phase_ref.at[1]),
                (phase_hbm.at[3], phase_ref.at[3]),
                (ids_hbm.at[1], next_ids),
            )
        )
    ]
    for copy in loads:
        copy.start()

    barrier = pltpu.get_barrier_semaphore()
    for k in range(1, n_mp):
        pl.semaphore_signal(barrier, inc=1, device_id={"mp": lax.rem(me_m + k, n_mp)})
    for k in range(1, n_bunch):
        pl.semaphore_signal(barrier, inc=1, device_id={"bunch": lax.rem(me_b + k, n_bunch)})

    def by_reach(n, step):
        return sorted(range(1, n), key=lambda k: -min(k // step, (n - k) // step))

    class Exchange:
        def __init__(self, axis, me, offsets, source, target, send, recv):
            self.axis, self.me, self.offsets = axis, me, offsets
            self.source, self.target, self.send, self.recv = source, target, send, recv

        def start(self):
            for k in self.offsets:
                pltpu.make_async_remote_copy(
                    src_ref=self.source,
                    dst_ref=self.target.at[self.me],
                    send_sem=self.send,
                    recv_sem=self.recv,
                    device_id={self.axis: lax.rem(self.me + k, len(self.offsets) + 1)},
                ).start()

        def all_of_them(self):
            block = self.target.at[pl.ds(0, len(self.offsets))]
            return pltpu.make_async_remote_copy(
                src_ref=block,
                dst_ref=block,
                send_sem=self.send,
                recv_sem=self.recv,
                device_id={self.axis: lax.rem(self.me + 1, len(self.offsets) + 1)},
            )

        def arrive(self):
            self.all_of_them().wait_recv()

        def leave(self):
            self.all_of_them().wait_send()

    across, along = by_reach(n_bunch, 1), by_reach(n_mp, 2)
    hist_x = Exchange("bunch", me_b, across, hist_src, hist_all, hist_send, hist_recv)
    sum_x = [
        Exchange("bunch", me_b, across, sum_src.at[t], sum_all.at[t], sum_send.at[t], sum_recv.at[t])
        for t in range(TURNS)
    ]
    far_x = [
        Exchange("mp", me_m, along, far_src.at[t], far_all.at[t], far_send.at[t], far_recv.at[t])
        for t in range(TURNS)
    ]
    tab_x = [
        Exchange("mp", me_m, along, tab_src.at[t], tab_all.at[t], tab_send.at[t], tab_recv.at[t])
        for t in range(TURNS)
    ]
    msg_x = [
        Exchange("mp", me_m, along, None, landed.at[t], msg_send.at[t], msg_recv.at[t]) for t in range(TURNS)
    ]

    def send_msg(turn, b):
        pltpu.make_async_remote_copy(
            src_ref=msg.at[turn, b],
            dst_ref=landed.at[turn, me_m],
            send_sem=msg_send.at[turn],
            recv_sem=msg_recv.at[turn],
            device_id={"mp": b},
        ).start()

    row8, lane8 = iota((8, LANES), 0), iota((8, LANES), 1)
    place = lax.rem(me_b, 8) * bunches

    def pieces(block):
        parts = []
        for _ in range(3):
            parts.append(block.astype(BF16))
            block = block - parts[-1].astype(F32)
        return jnp.concatenate(parts, axis=1)

    def to_lanes(chosen, block):
        rows = lax.dot_general(
            jnp.concatenate([chosen.astype(BF16)] * 3, axis=1), pieces(block), NT, preferred_element_type=F32
        )
        return jnp.concatenate([rows, jnp.zeros((16, LANES - block.shape[0]), F32)], axis=1)

    def send_sums(turn, sums_x, sums_y):
        both = to_lanes(jnp.ones((16, LANES), F32), jnp.concatenate([sums_x, sums_y], axis=0) * scale)[:8]
        partial[turn] = pltpu.roll(both, 2 * bunches, 1)[:1]
        x = pltpu.roll(jnp.where(lane8 < bunches, both, 0.0), place, 1)
        y = jnp.where((lane8 >= bunches) & (lane8 < 2 * bunches), both, 0.0)
        y = pltpu.roll(y, lax.rem(place + LANES - bunches, LANES), 1)
        rows = jnp.where(row8 == 0, x, y)[:2]
        sum_src[turn] = rows
        sum_all[turn, me_b] = rows
        sum_x[turn].start()

    def lane_sums(p):
        def step(c, acc):
            return acc + phase_ref[p, :, pl.ds(pl.multiple_of(c * LANES, LANES), LANES)]

        return lax.fori_loop(0, parts // LANES, step, jnp.zeros((bunches, LANES), F32), unroll=8)

    def send_history():
        loads[3].wait()
        r, c = iota((16, 2 * turns_back), 0), iota((16, 2 * turns_back), 1)
        chosen = jnp.where(c == (r // share) * turns_back + me_m * share + (r & (share - 1)), 1.0, 0.0)
        own = to_lanes(chosen, jnp.concatenate([hist_ref[0], hist_ref[1]], axis=1))[:8]
        own = pltpu.roll(own, place, 1)
        hist_src[...] = own
        hist_all[me_b] = own
        hist_x.start()

    loads[0].wait()
    loads[1].wait()
    loads[2].wait()

    iota_c = iota((COARSE, CHUNK), 0)
    iota_f = iota((FINE, CHUNK), 0)
    own_lanes = lax.shift_right_logical(lane8, 5) == lax.shift_right_logical(row8, 1)

    def bin_bunch(ids_ref, source, b):
        acc = None
        for c in range(parts // CHUNK):
            at = pl.ds(c * CHUNK, CHUNK)
            ids = ids_ref[pl.ds(b, 1), at]
            x = source[0, pl.ds(b, 1), at]
            y = source[2, pl.ds(b, 1), at]
            coarse = iota_c == ((lax.shift_right_logical(ids, 4) & 6) | lax.shift_right_logical(ids, 7))
            fine = jnp.where(iota_f == (ids & (FINE - 1)), 1.0, 0.0).astype(BF16)
            rows = [jnp.where(coarse, 1.0, 0.0)]
            for v in (*two_pieces(x), *two_pieces(y)):
                rows.append(jnp.where(coarse, jnp.broadcast_to(v, (COARSE, CHUNK)), 0.0))
            weighted = jnp.concatenate(rows, axis=0).astype(BF16)
            part = lax.dot_general(weighted, fine, NT, preferred_element_type=F32)
            acc = part if acc is None else acc + part
        return acc

    def as_tile(acc):
        tiles = []
        for v in (acc[8:16] + acc[16:24], acc[24:32] + acc[32:40], acc[0:8]):
            v = jnp.where(own_lanes, jnp.concatenate([v] * 4, axis=1), 0.0)
            v = v + pltpu.roll(v, 2, 0)
            tiles.append(v + pltpu.roll(v, 4, 0))
        tile = jnp.where(row8 < 2, tiles[0], jnp.where(row8 < 4, tiles[1], tiles[2]))
        return (tile * scale)[:6]

    chips, chip = n_mp // 2, lax.div(me_m, 2)
    core = lax.rem(me_m, 2)

    def owner(k):
        u, side = k // 2, k % 2
        reach = (chips // 2 - (u + 1) // 2) * (2 * (u % 2) - 1)
        there = lax.rem(chip + reach + chips, chips)
        return there * 2 + lax.rem(core + 1 + side, 2)

    def bin_all(turn, ids_ref, source, before, after):
        for first in range(0, bunches, AT_ONCE):
            owners = [owner(first + k) for k in range(AT_ONCE)]
            tiles = [as_tile(bin_bunch(ids_ref, source, b)) for b in owners]
            if first == 0:
                before()
            if first + AT_ONCE == bunches:
                landed[turn, me_m] = tiles[-1]
                owners = owners[:-1]
            for b, tile in zip(owners, tiles):
                msg[turn, b] = tile
            for b in owners:
                send_msg(turn, b)
            if first == 0:
                after()

    def toeplitz_rows(r, half, sub):
        d = me_b * bunches + sub * 8 + row8 - (LANES * half + lane8) - 1
        c = d & (SLICES - 1)
        index = c & (LANES - 1)
        low = jnp.broadcast_to(wake_ref[pl.ds(2 * r, 1), :], (8, LANES))
        high = jnp.broadcast_to(wake_ref[pl.ds(2 * r + 1, 1), :], (8, LANES))
        return jnp.where(c >= LANES, gather_lanes(high, index), gather_lanes(low, index)), d >= 0

    def collected(ref):
        halves = []
        for half in range(2):
            total = ref[8 * half]
            for k in range(1, 8):
                total = total + ref[8 * half + k]
            halves.append(total)
        return halves

    def row_of(tile, k):
        return jnp.broadcast_to(tile[k : k + 1, :], (8, LANES))

    def send_far(turn):
        row = to_lanes(jnp.ones((16, LANES), F32), ext[turn])[:1] + partial[turn]
        far_src[turn] = row
        far_all[turn, me_m] = row
        far_x[turn].start()

    def lay_wake():
        loads[4].wait()
        kept = jnp.where(me_m == n_mp - 1, 0.0, 1.0)
        first = me_m * share
        for sub in range(2):
            at = pl.ds(8 * sub, 8)
            for half in range(2):
                g0, upper = toeplitz_rows(0, half, sub)
                g1, _ = toeplitz_rows(1, half, sub)
                toep[0, half, at, :] = jnp.where(upper, g0, 0.0)
                toep[1, half, at, :] = jnp.where(upper, g1, g0)
                g = [
                    toeplitz_rows(jnp.minimum(first + k, turns_back), half, sub)[0]
                    for k in range(share + 2)
                ]
                for k in range(share + 1):
                    near = jnp.where(upper, g[k + 1], g[k])
                    toep[2 + k, half, at, :] = near
                toep[2 + share + 1, half, at, :] = near * kept

    def far_first():
        sum_x[0].arrive()
        hist_x.arrive()
        hist, cent = collected(hist_all), collected(sum_all.at[0])
        for sub in range(2):
            at = pl.ds(8 * sub, 8)
            sums = [[jnp.zeros((8, LANES), F32) for _ in range(2)] for _ in range(2)]
            for half in range(2):
                u = [toep[k, half, at, :] for k in range(share + 4)]
                for p in range(2):
                    c = row_of(cent[half], p)
                    sums[0][p] = sums[0][p] + u[0] * c
                    sums[1][p] = sums[1][p] + u[1] * c
                for k in range(share):
                    for p in range(2):
                        h = row_of(hist[half], p * share + k)
                        sums[0][p] = sums[0][p] + u[2 + k] * h
                        later = u[3 + k] if k < share - 1 else u[3 + share]
                        sums[1][p] = sums[1][p] + later * h
            for turn in range(2):
                for p in range(2):
                    ext[turn, pl.ds(p * bunches + 8 * sub, 8), :] = sums[turn][p]
        send_far(0)

    def far_second():
        sum_x[1].arrive()
        cent = collected(sum_all.at[1])
        for sub in range(2):
            for p in range(2):
                at = pl.ds(p * bunches + 8 * sub, 8)
                total = ext[1, at, :]
                for half in range(2):
                    total = total + toep[0, half, pl.ds(8 * sub, 8), :] * row_of(cent[half], p)
                ext[1, at, :] = total
        send_far(1)

    def kick_table(turn):
        msg_x[turn].arrive()
        total = landed[turn, 0]
        for k in range(1, 16):
            total = total + landed[turn, k]
        total = jnp.concatenate([total, jnp.zeros((2, LANES), F32)], axis=0)
        wide = jnp.concatenate([total, pltpu.roll(total, 7, 0)], axis=1)
        stack = []
        for _ in range(3):
            stack.append(wide.astype(BF16).astype(F32))
            wide = wide - stack[-1]
        stack = jnp.concatenate(stack, axis=0).astype(BF16)

        def product(which):
            out = None
            for k in reversed(range(3)):
                part = jnp.dot(stack, split[which, k], preferred_element_type=F32)
                for n in reversed(range(3 - k)):
                    block = part[8 * n : 8 * n + 8]
                    out = block if out is None else out + block
            return out

        dip, quad = product(0), product(1)
        low, high = dip[:, :LANES], dip[:, LANES:]
        tab_src[turn] = jnp.concatenate(
            [low[0:1], high[0:1], low[2:3], high[2:3], quad[4:5, :LANES], quad[4:5, LANES:]], axis=0
        )
        tab_x[turn].start()
        tab_all[turn, me_m] = tab_src[turn]

    full_row, full_lane = iota((bunches, LANES), 0), iota((bunches, LANES), 1)

    def lay_rows(turn):
        far_x[turn].arrive()
        total = far_all[turn, 0]
        for k in range(1, n_mp):
            total = total + far_all[turn, k]
        for p in range(2):
            cent_ref[p, turn : turn + 1, :] = pltpu.roll(total, LANES - (2 + p) * bunches, 1)[:, :bunches]
        total = jnp.broadcast_to(total, (bunches, LANES))
        far = [
            jnp.sum(jnp.where(full_lane == full_row + p * bunches, total, 0.0), axis=1, keepdims=True)
            for p in range(2)
        ]
        tab_x[turn].arrive()

        def column(k):
            return jnp.concatenate([tab_all[turn, n, k : k + 1, :] for n in range(bunches)], axis=0)

        for k in range(6):
            row = column(k)
            rows_ref[k] = row + far[k // 2] if k < 4 else row

    def first_sends():
        send_sums(0, lane_sums(0), lane_sums(2))
        send_history()

    bin_all(0, first_ids, phase_ref, lambda: pl.semaphore_wait(barrier, n_mp + n_bunch - 2), first_sends)
    lay_wake()

    loads[5].wait()
    for p in range(2):
        wide = jnp.concatenate([advance_ref[p : p + 1, :], jnp.zeros((1, LANES - bunches), F32)], axis=1)
        wide = jnp.broadcast_to(wide, (bunches, LANES))
        column = jnp.sum(jnp.where(full_row == full_lane, wide, 0.0), axis=1, keepdims=True)
        sin, cos = sin_cos(jnp.broadcast_to(column, (bunches, LANES)))
        rot[2 * p] = cos
        rot[2 * p + 1] = sin

    for k, ref in enumerate((dipole_ref, quad_ref)):
        loads[6 + k].wait()
        rest = jnp.transpose(ref[...])
        for n in range(3):
            piece = rest.astype(BF16)
            split[k, n] = piece
            rest = rest - piece.astype(F32)
    kick_table(0)
    far_first()
    loads[8].wait()
    loads[9].wait()
    loads[10].wait()
    lay_rows(0)

    sums = []
    for g in range(bunches // GROUP):
        at = pl.ds(g * GROUP, GROUP)
        rows = [rows_ref[k, at, :] for k in range(6)]
        turn_by = [rot[k, at, :] for k in range(4)]

        def kick(c, acc):
            lanes = pl.ds(pl.multiple_of(c * WIDTH, WIDTH), WIDTH)
            new = turned(first_ids[at, lanes], [phase_ref[k, at, lanes] for k in range(4)], rows, turn_by)
            for k in range(4):
                mid_ref[k, at, lanes] = new[k]
            acc = list(acc)
            for s in range(WIDTH // LANES):
                cut = slice(s * LANES, (s + 1) * LANES)
                acc = [acc[0] + new[0][:, cut], acc[1] + new[2][:, cut]]
            return tuple(acc)

        zero = jnp.zeros((GROUP, LANES), F32)
        sums.append(lax.fori_loop(0, parts // WIDTH, kick, (zero, zero), unroll=8))
    sums = [jnp.concatenate([s[p] for s in sums], axis=0) for p in range(2)]
    bin_all(1, next_ids, mid_ref, lambda: None, lambda: send_sums(1, *sums))
    kick_table(1)
    far_second()
    lay_rows(1)

    for turn in range(TURNS):
        for exchange in (msg_x[turn], tab_x[turn], far_x[turn], sum_x[turn]):
            exchange.leave()
    hist_x.leave()


def last_kernel(mid_ref, ids_ref, rows_ref, rot, cent_in, out_hbm, cent_hbm, out_ref, cent_ref, sems):
    bunches, parts = mid_ref.shape[1], mid_ref.shape[2]
    cent_ref[...] = cent_in[...]
    copies = [pltpu.make_async_copy(cent_ref, cent_hbm, sems.at[0])]
    copies[0].start()
    span = parts // SPANS
    for g in range(bunches // GROUP):
        at = pl.ds(g * GROUP, GROUP)
        rows = [rows_ref[k, at, :] for k in range(6)]
        turn_by = [rot[k, at, :] for k in range(4)]
        for part in range(SPANS):

            def kick(c, _):
                lanes = pl.ds(pl.multiple_of(part * span + c * WIDTH, WIDTH), WIDTH)
                new = turned(ids_ref[at, lanes], [mid_ref[k, at, lanes] for k in range(4)], rows, turn_by)
                for k in range(4):
                    out_ref[k, at, lanes] = new[k]
                return 0

            lax.fori_loop(0, span // WIDTH, kick, 0, unroll=4)
            block = (slice(None), at, pl.ds(part * span, span))
            copies.append(
                pltpu.make_async_copy(out_ref.at[block], out_hbm.at[block], sems.at[len(copies)])
            )
            copies[-1].start()
    for copy in copies:
        copy.wait()


def body(phase_space, phase_advance, centroid_history, lr_wake, sr_dipole, sr_quad, slice_ids):
    n_bunch, n_mp = lax.axis_size("bunch"), lax.axis_size("mp")
    bunches, parts = phase_space.shape[1:]
    turns_back = centroid_history.shape[1]
    wake_rows = lr_wake.shape[0] // LANES
    vmem, hbm = pl.BlockSpec(memory_space=pltpu.VMEM), pl.BlockSpec(memory_space=pltpu.HBM)
    dma = pltpu.SemaphoreType.DMA

    def held(*shape, dtype=F32):
        return pltpu.VMEM(shape, dtype)

    cent_shape = jax.ShapeDtypeStruct((2, TURNS, bunches), F32)
    state = pl.pallas_call(
        functools.partial(track_kernel, (n_bunch, n_mp)),
        out_shape=(
            jax.ShapeDtypeStruct(phase_space.shape, F32),
            jax.ShapeDtypeStruct((bunches, parts), I32),
            jax.ShapeDtypeStruct((6, bunches, LANES), F32),
            jax.ShapeDtypeStruct((4, bunches, LANES), F32),
            cent_shape,
        ),
        in_specs=[hbm] * 7,
        out_specs=(vmem,) * 5,
        scratch_shapes=[
            held(4, bunches, parts),
            held(bunches, parts, dtype=I32),
            held(2, bunches),
            held(2, bunches, turns_back),
            held(wake_rows, LANES),
            held(SLICES, SLICES),
            held(SLICES, SLICES),
            held(TURNS, bunches, 6, LANES),
            held(TURNS, n_mp, 6, LANES),
            held(8, LANES),
            held(n_bunch, 8, LANES),
            held(TURNS, 2, LANES),
            held(TURNS, n_bunch, 2, LANES),
            held(TURNS, 1, LANES),
            held(TURNS, n_mp, 1, LANES),
            held(TURNS, 6, LANES),
            held(TURNS, n_mp, 6, LANES),
            held(TURNS, 2 * bunches, LANES),
            held(4 + turns_back // n_mp, 2, bunches, LANES),
            held(TURNS, 1, LANES),
            held(2, 3, SLICES, SLICES, dtype=BF16),
            dma((11,)),
            dma((TURNS,)),
            dma((TURNS,)),
            dma,
            dma,
            dma((TURNS,)),
            dma((TURNS,)),
            dma((TURNS,)),
            dma((TURNS,)),
            dma((TURNS,)),
            dma((TURNS,)),
        ],
        compiler_params=pltpu.CompilerParams(
            collective_id=0, has_side_effects=True, vmem_limit_bytes=40 << 20
        ),
        cost_estimate=pl.CostEstimate(flops=4 * 65536 * 256, bytes_accessed=3 << 20, transcendentals=0),
        name="track",
    )(
        *(
            pltpu.with_memory_space_constraint(a, pltpu.HBM)
            for a in (
                phase_space,
                phase_advance,
                jnp.transpose(centroid_history, (0, 2, 1)),
                lr_wake.reshape(-1, LANES),
                sr_dipole,
                sr_quad,
                slice_ids,
            )
        )
    )
    return tuple(
        pl.pallas_call(
            last_kernel,
            out_shape=(jax.ShapeDtypeStruct(phase_space.shape, F32), cent_shape),
            in_specs=[vmem] * 5,
            out_specs=(hbm, hbm),
            scratch_shapes=[
                held(*phase_space.shape),
                held(2, TURNS, bunches),
                dma((1 + SPANS * bunches // GROUP,)),
            ],
            compiler_params=pltpu.CompilerParams(vmem_limit_bytes=16 << 20),
            cost_estimate=pl.CostEstimate(flops=100 * 65536, bytes_accessed=1 << 20, transcendentals=0),
            name="last",
        )(*state)
    )


def solution(mesh):
    placed = (
        P(None, "bunch", "mp"),
        P(None, "bunch"),
        P(None, None, "bunch"),
        P(),
        P(),
        P(),
        P(None, "bunch", "mp"),
    )
    return jax.shard_map(
        body,
        mesh=mesh,
        in_specs=placed,
        out_specs=(P(None, "bunch", "mp"), P(None, None, "bunch")),
        check_vma=False,
    )
```

```python
import functools

import jax
import jax.numpy as jnp
from jax import lax
from jax.experimental import pallas as pl
from jax.experimental.pallas import tpu as pltpu
from jax.sharding import PartitionSpec as P

SLICES = 256
TURNS = 2
DETUNE = 0.02
LANES = 128
COARSE, FINE = 8, 32
CHUNK = 512
GROUP = 8
BLOCKS = (6, 10)
WIDTH = 512
SPANS = 2

F32, BF16, I32 = jnp.float32, jnp.bfloat16, jnp.int32
NT = (((1,), (1,)), ((), ()))
HIGHEST = lax.Precision.HIGHEST


def iota(shape, axis):
    return lax.broadcasted_iota(I32, shape, axis)


def gather_lanes(row, index):
    return jnp.take_along_axis(row, index, axis=1, mode="promise_in_bounds")


def two_pieces(v):
    high = v.astype(BF16).astype(F32)
    return high, v - high


def sin_cos(theta):
    n = jnp.round(theta * 0.6366197723675814)
    r = theta - n * 1.5703125
    r = r - n * 4.837512969970703e-4
    r = r - n * 7.549789948768648e-8
    r = jnp.clip(r, -0.8, 0.8)
    q = n.astype(I32)
    z = r * r
    s = r + r * z * (-1.6666654611e-1 + z * (8.3321608736e-3 + z * -1.9515295891e-4))
    c = 1.0 - 0.5 * z + z * z * (
        4.166664568298827e-2 + z * (-1.388731625493765e-3 + z * 2.443315711809948e-5)
    )
    odd = (q & 1) == 1
    sin, cos = jnp.where(odd, c, s), jnp.where(odd, s, c)
    sin = jnp.where((q & 2) == 2, -sin, sin)
    cos = jnp.where(((q + 1) & 2) == 2, -cos, cos)
    return sin, cos


def turned(ids, coords, rows, rot):
    width = ids.shape[1]
    index, upper = ids & (LANES - 1), ids >= LANES

    def looked_up(k):
        pieces = []
        for c in range(width // LANES):
            at = slice(c * LANES, (c + 1) * LANES)
            low, high = gather_lanes(rows[2 * k], index[:, at]), gather_lanes(rows[2 * k + 1], index[:, at])
            pieces.append(jnp.where(upper[:, at], high, low))
        return jnp.concatenate(pieces, axis=1)

    x, mx, y, my = coords
    kx, ky, kq = looked_up(0), looked_up(1), looked_up(2)
    mx = mx + (kx + kq * x)
    my = my + (ky - kq * y)
    action = x * x + mx * mx + y * y + my * my
    sin, cos = sin_cos(DETUNE * action)
    cos_x, sin_x, cos_y, sin_y = (jnp.concatenate([r] * (width // LANES), axis=1) for r in rot)
    x, mx = cos * x + sin * mx, cos * mx - sin * x
    y, my = cos * y + sin * my, cos * my - sin * y
    x, mx = cos_x * x + sin_x * mx, cos_x * mx - sin_x * x
    y, my = cos_y * y + sin_y * my, cos_y * my - sin_y * y
    return x, mx, y, my


def track_kernel(
    rings,
    phase_hbm,
    advance_hbm,
    hist_hbm,
    wake_hbm,
    dipole_hbm,
    quad_hbm,
    ids_hbm,
    mid_ref,
    next_ids,
    rows_ref,
    rot,
    cent_ref,
    phase_ref,
    first_ids,
    advance_ref,
    hist_ref,
    wake_ref,
    dipole_ref,
    quad_ref,
    msg,
    landed,
    hist_src,
    hist_all,
    sum_src,
    sum_all,
    tab_src,
    tab_all,
    ext,
    toep,
    partial,
    split,
    load,
    msg_send,
    msg_recv,
    sum_send,
    sum_recv,
    tab_send,
    tab_recv,
):
    n_bunch, n_mp = rings
    me_b, me_m = lax.axis_index("bunch"), lax.axis_index("mp")
    bunches, parts = mid_ref.shape[1], mid_ref.shape[2]
    turns_back = hist_ref.shape[2]
    share = turns_back // n_mp
    scale = 1.0 / (parts * n_mp)

    def by_reach(n, step):
        return sorted(range(1, n), key=lambda k: -min(k // step, (n - k) // step))

    across, along = by_reach(n_bunch, 1), by_reach(n_mp, 2)
    barrier = pltpu.get_barrier_semaphore()
    for k, n in zip(along, across):
        pl.semaphore_signal(barrier, inc=1, device_id={"mp": lax.rem(me_m + k, n_mp)})
        pl.semaphore_signal(barrier, inc=1, device_id={"bunch": lax.rem(me_b + n, n_bunch)})

    loads = [
        pltpu.make_async_copy(source, target, load.at[k])
        for k, (source, target) in enumerate(
            (
                (phase_hbm.at[0], phase_ref.at[0]),
                (phase_hbm.at[2], phase_ref.at[2]),
                (ids_hbm.at[0], first_ids),
                (hist_hbm, hist_ref),
                (wake_hbm, wake_ref),
                (advance_hbm, advance_ref),
                (dipole_hbm, dipole_ref),
                (quad_hbm, quad_ref),
                (phase_hbm.at[1], phase_ref.at[1]),
                (phase_hbm.at[3], phase_ref.at[3]),
                (ids_hbm.at[1], next_ids),
            )
        )
    ]
    for copy in loads:
        copy.start()

    class Exchange:
        def __init__(self, axis, me, offsets, source, target, send, recv):
            self.axis, self.me, self.offsets = axis, me, offsets
            self.source, self.target, self.send, self.recv = source, target, send, recv

        def start(self):
            for k in self.offsets:
                pltpu.make_async_remote_copy(
                    src_ref=self.source,
                    dst_ref=self.target.at[self.me],
                    send_sem=self.send,
                    recv_sem=self.recv,
                    device_id={self.axis: lax.rem(self.me + k, len(self.offsets) + 1)},
                ).start()

        def all_of_them(self):
            block = self.target.at[pl.ds(0, len(self.offsets))]
            return pltpu.make_async_remote_copy(
                src_ref=block,
                dst_ref=block,
                send_sem=self.send,
                recv_sem=self.recv,
                device_id={self.axis: lax.rem(self.me + 1, len(self.offsets) + 1)},
            )

        def arrive(self):
            self.all_of_them().wait_recv()

        def leave(self):
            self.all_of_them().wait_send()

    sum_x = [
        Exchange("bunch", me_b, across, source, target, sum_send.at[t], sum_recv.at[t])
        for t, (source, target) in enumerate(((hist_src, hist_all), (sum_src, sum_all)))
    ]
    tab_x = [
        Exchange("mp", me_m, along, tab_src.at[t], tab_all.at[t], tab_send.at[t], tab_recv.at[t])
        for t in range(TURNS)
    ]
    msg_x = [
        Exchange("mp", me_m, along, None, landed.at[t], msg_send.at[t], msg_recv.at[t]) for t in range(TURNS)
    ]

    def send_msg(turn, b):
        pltpu.make_async_remote_copy(
            src_ref=msg.at[turn, b],
            dst_ref=landed.at[turn, me_m],
            send_sem=msg_send.at[turn],
            recv_sem=msg_recv.at[turn],
            device_id={"mp": b},
        ).start()

    row8, lane8 = iota((8, LANES), 0), iota((8, LANES), 1)
    place = lax.rem(me_b, 8) * bunches

    def pieces(block):
        parts = []
        for _ in range(3):
            parts.append(block.astype(BF16))
            block = block - parts[-1].astype(F32)
        return jnp.concatenate(parts, axis=1)

    def to_lanes(chosen, block):
        rows = lax.dot_general(
            jnp.concatenate([chosen.astype(BF16)] * 3, axis=1), pieces(block), NT, preferred_element_type=F32
        )
        return jnp.concatenate([rows, jnp.zeros((16, LANES - block.shape[0]), F32)], axis=1)

    def sum_rows(turn, sums_x, sums_y):
        both = to_lanes(jnp.ones((16, LANES), F32), jnp.concatenate([sums_x, sums_y], axis=0) * scale)[:8]
        partial[turn] = pltpu.roll(both, 2 * bunches, 1)[:1]
        x = pltpu.roll(jnp.where(lane8 < bunches, both, 0.0), place, 1)
        y = jnp.where((lane8 >= bunches) & (lane8 < 2 * bunches), both, 0.0)
        y = pltpu.roll(y, lax.rem(place + LANES - bunches, LANES), 1)
        rows = jnp.where(row8 == 0, x, y)[:2]
        return rows

    def lane_sums(p):
        def step(c, acc):
            return acc + phase_ref[p, :, pl.ds(pl.multiple_of(c * LANES, LANES), LANES)]

        return lax.fori_loop(0, parts // LANES, step, jnp.zeros((bunches, LANES), F32), unroll=8)

    loads[3].wait()
    r, c = iota((16, 2 * turns_back), 0), iota((16, 2 * turns_back), 1)
    chosen = jnp.where(c == (r // share) * turns_back + me_m * share + (r & (share - 1)), 1.0, 0.0)
    own = to_lanes(chosen, jnp.concatenate([hist_ref[0], hist_ref[1]], axis=1))[: 2 * share]
    own = pltpu.roll(own, place, 1)

    loads[0].wait()
    loads[1].wait()
    own = jnp.concatenate([own, sum_rows(0, lane_sums(0), lane_sums(2))], axis=0)
    hist_src[...] = own
    hist_all[me_b] = own
    loads[2].wait()

    iota_c = iota((COARSE, CHUNK), 0)
    iota_f = iota((FINE, CHUNK), 0)
    own_lanes = lax.shift_right_logical(lane8, 5) == lax.shift_right_logical(row8, 1)

    def bin_bunch(ids_ref, source, b):
        acc = None
        for c in range(parts // CHUNK):
            at = pl.ds(c * CHUNK, CHUNK)
            ids = ids_ref[pl.ds(b, 1), at]
            x = source[0, pl.ds(b, 1), at]
            y = source[2, pl.ds(b, 1), at]
            coarse = iota_c == ((lax.shift_right_logical(ids, 4) & 6) | lax.shift_right_logical(ids, 7))
            fine = jnp.where(iota_f == (ids & (FINE - 1)), 1.0, 0.0).astype(BF16)
            rows = [jnp.where(coarse, 1.0, 0.0)]
            for v in (*two_pieces(x), *two_pieces(y)):
                rows.append(jnp.where(coarse, jnp.broadcast_to(v, (COARSE, CHUNK)), 0.0))
            weighted = jnp.concatenate(rows, axis=0).astype(BF16)
            part = lax.dot_general(weighted, fine, NT, preferred_element_type=F32)
            acc = part if acc is None else acc + part
        return acc

    def as_tile(acc):
        tiles = []
        for v in (acc[8:16] + acc[16:24], acc[24:32] + acc[32:40], acc[0:8]):
            v = jnp.where(own_lanes, jnp.concatenate([v] * 4, axis=1), 0.0)
            v = v + pltpu.roll(v, 2, 0)
            tiles.append(v + pltpu.roll(v, 4, 0))
        tile = jnp.where(row8 < 2, tiles[0], jnp.where(row8 < 4, tiles[1], tiles[2]))
        return (tile * scale)[:6]

    chips, chip = n_mp // 2, lax.div(me_m, 2)
    core = lax.rem(me_m, 2)

    def owner(k):
        u, side = k // 2, k % 2
        reach = (chips // 2 - (u + 1) // 2) * (2 * (u % 2) - 1)
        there = lax.rem(chip + reach + chips, chips)
        return there * 2 + lax.rem(core + 1 + side, 2)

    def bin_block(turn, ids_ref, source, first, count):
        owners = [owner(first + k) for k in range(count)]
        tiles = [as_tile(bin_bunch(ids_ref, source, b)) for b in owners]
        if first + count == bunches:
            landed[turn, me_m] = tiles[-1]
            owners = owners[:-1]
        for b, tile in zip(owners, tiles):
            msg[turn, b] = tile
        return owners

    def send_all(turn, owners):
        for b in owners:
            send_msg(turn, b)

    def toeplitz_rows(r, half, sub):
        d = me_b * bunches + sub * 8 + row8 - (LANES * half + lane8) - 1
        c = d & (SLICES - 1)
        index = c & (LANES - 1)
        low = jnp.broadcast_to(wake_ref[pl.ds(2 * r, 1), :], (8, LANES))
        high = jnp.broadcast_to(wake_ref[pl.ds(2 * r + 1, 1), :], (8, LANES))
        return jnp.where(c >= LANES, gather_lanes(high, index), gather_lanes(low, index)), d >= 0

    def collected(ref):
        halves = []
        for half in range(2):
            total = ref[8 * half]
            for k in range(1, 8):
                total = total + ref[8 * half + k]
            halves.append(total)
        return halves

    def row_of(tile, k):
        return jnp.broadcast_to(tile[k : k + 1, :], (8, LANES))

    def far_row(turn):
        return to_lanes(jnp.ones((16, LANES), F32), ext[turn])[:1] + partial[turn]

    def lay_wake():
        loads[4].wait()
        kept = jnp.where(me_m == n_mp - 1, 0.0, 1.0)
        first = me_m * share
        for sub in range(2):
            at = pl.ds(8 * sub, 8)
            for half in range(2):
                g0, upper = toeplitz_rows(0, half, sub)
                g1, _ = toeplitz_rows(1, half, sub)
                toep[0, half, at, :] = jnp.where(upper, g0, 0.0)
                toep[1, half, at, :] = jnp.where(upper, g1, g0)
                g = [
                    toeplitz_rows(jnp.minimum(first + k, turns_back), half, sub)[0]
                    for k in range(share + 2)
                ]
                for k in range(share + 1):
                    near = jnp.where(upper, g[k + 1], g[k])
                    toep[2 + k, half, at, :] = near
                toep[2 + share + 1, half, at, :] = near * kept

    def far_first():
        sum_x[0].arrive()
        hist = cent = collected(hist_all)
        for sub in range(2):
            at = pl.ds(8 * sub, 8)
            sums = [[jnp.zeros((8, LANES), F32) for _ in range(2)] for _ in range(2)]
            for half in range(2):
                u = [toep[k, half, at, :] for k in range(share + 4)]
                for p in range(2):
                    c = row_of(cent[half], 2 * share + p)
                    sums[0][p] = sums[0][p] + u[0] * c
                    sums[1][p] = sums[1][p] + u[1] * c
                for k in range(share):
                    for p in range(2):
                        h = row_of(hist[half], p * share + k)
                        sums[0][p] = sums[0][p] + u[2 + k] * h
                        later = u[3 + k] if k < share - 1 else u[3 + share]
                        sums[1][p] = sums[1][p] + later * h
            for turn in range(2):
                for p in range(2):
                    ext[turn, pl.ds(p * bunches + 8 * sub, 8), :] = sums[turn][p]
        tab_src[0, 6:7, :] = far_row(0)

    def far_second():
        sum_x[1].arrive()
        cent = collected(sum_all)
        for sub in range(2):
            for p in range(2):
                at = pl.ds(p * bunches + 8 * sub, 8)
                total = ext[1, at, :]
                for half in range(2):
                    total = total + toep[0, half, pl.ds(8 * sub, 8), :] * row_of(cent[half], p)
                ext[1, at, :] = total
        tab_src[1, 6:7, :] = far_row(1)

    def kick_table(turn):
        msg_x[turn].arrive()
        total = landed[turn, 0]
        for k in range(1, 16):
            total = total + landed[turn, k]
        total = jnp.concatenate([total, jnp.zeros((2, LANES), F32)], axis=0)
        wide = jnp.concatenate([total, pltpu.roll(total, 7, 0)], axis=1)
        stack = []
        for _ in range(3):
            stack.append(wide.astype(BF16).astype(F32))
            wide = wide - stack[-1]
        stack = jnp.concatenate(stack, axis=0).astype(BF16)

        def product(which):
            out = None
            for k in reversed(range(3)):
                part = jnp.dot(stack, split[which, k], preferred_element_type=F32)
                for n in reversed(range(3 - k)):
                    block = part[8 * n : 8 * n + 8]
                    out = block if out is None else out + block
            return out

        dip, quad = product(0), product(1)
        low, high = dip[:, :LANES], dip[:, LANES:]
        tab_src[turn, :6, :] = jnp.concatenate(
            [low[0:1], high[0:1], low[2:3], high[2:3], quad[4:5, :LANES], quad[4:5, LANES:]], axis=0
        )
        tab_x[turn].start()
        tab_all[turn, me_m] = tab_src[turn]

    full_row, full_lane = iota((bunches, LANES), 0), iota((bunches, LANES), 1)

    def lay_rows(turn):
        tab_x[turn].arrive()
        total = tab_all[turn, 0, 6:7, :]
        for k in range(1, n_mp):
            total = total + tab_all[turn, k, 6:7, :]
        for p in range(2):
            cent_ref[p, turn : turn + 1, :] = pltpu.roll(total, LANES - (2 + p) * bunches, 1)[:, :bunches]
        total = jnp.broadcast_to(total, (bunches, LANES))
        far = [
            jnp.sum(jnp.where(full_lane == full_row + p * bunches, total, 0.0), axis=1, keepdims=True)
            for p in range(2)
        ]

        def column(k):
            return jnp.concatenate([tab_all[turn, n, k : k + 1, :] for n in range(bunches)], axis=0)

        for k in range(6):
            row = column(k)
            rows_ref[k] = row + far[k // 2] if k < 4 else row

    half = bunches // 2
    owners = bin_block(0, first_ids, phase_ref, 0, half) + bin_block(0, first_ids, phase_ref, half, half)
    pl.semaphore_wait(barrier, n_mp + n_bunch - 2)
    send_all(0, owners[:half])
    sum_x[0].start()
    send_all(0, owners[half:])
    lay_wake()

    loads[5].wait()
    for p in range(2):
        wide = jnp.concatenate([advance_ref[p : p + 1, :], jnp.zeros((1, LANES - bunches), F32)], axis=1)
        wide = jnp.broadcast_to(wide, (bunches, LANES))
        column = jnp.sum(jnp.where(full_row == full_lane, wide, 0.0), axis=1, keepdims=True)
        sin, cos = sin_cos(jnp.broadcast_to(column, (bunches, LANES)))
        rot[2 * p] = cos
        rot[2 * p + 1] = sin

    for k, ref in enumerate((dipole_ref, quad_ref)):
        loads[6 + k].wait()
        rest = jnp.transpose(ref[...])
        for n in range(3):
            piece = rest.astype(BF16)
            split[k, n] = piece
            rest = rest - piece.astype(F32)
    far_first()
    kick_table(0)
    loads[8].wait()
    loads[9].wait()
    loads[10].wait()
    lay_rows(0)

    sums = []
    for g in range(bunches // GROUP):
        at = pl.ds(g * GROUP, GROUP)
        rows = [rows_ref[k, at, :] for k in range(6)]
        turn_by = [rot[k, at, :] for k in range(4)]

        def kick(c, acc):
            lanes = pl.ds(pl.multiple_of(c * WIDTH, WIDTH), WIDTH)
            new = turned(first_ids[at, lanes], [phase_ref[k, at, lanes] for k in range(4)], rows, turn_by)
            for k in range(4):
                mid_ref[k, at, lanes] = new[k]
            acc = list(acc)
            for s in range(WIDTH // LANES):
                cut = slice(s * LANES, (s + 1) * LANES)
                acc = [acc[0] + new[0][:, cut], acc[1] + new[2][:, cut]]
            return tuple(acc)

        zero = jnp.zeros((GROUP, LANES), F32)
        sums.append(lax.fori_loop(0, parts // WIDTH, kick, (zero, zero), unroll=8))
    sums = [jnp.concatenate([s[p] for s in sums], axis=0) for p in range(2)]
    rows = sum_rows(1, *sums)
    sum_src[...] = rows
    sum_all[me_b] = rows
    sum_x[1].start()
    first = 0
    for count in BLOCKS:
        send_all(1, bin_block(1, next_ids, mid_ref, first, count))
        first += count
    far_second()
    kick_table(1)
    lay_rows(1)

    for turn in range(TURNS):
        for exchange in (msg_x[turn], tab_x[turn], sum_x[turn]):
            exchange.leave()


def last_kernel(mid_ref, ids_ref, rows_ref, rot, cent_in, out_hbm, cent_hbm, out_ref, cent_ref, sems):
    bunches, parts = mid_ref.shape[1], mid_ref.shape[2]
    cent_ref[...] = cent_in[...]
    copies = [pltpu.make_async_copy(cent_ref, cent_hbm, sems.at[0])]
    copies[0].start()
    span = parts // SPANS
    for g in range(bunches // GROUP):
        at = pl.ds(g * GROUP, GROUP)
        rows = [rows_ref[k, at, :] for k in range(6)]
        turn_by = [rot[k, at, :] for k in range(4)]
        for part in range(SPANS):

            def kick(c, _):
                lanes = pl.ds(pl.multiple_of(part * span + c * WIDTH, WIDTH), WIDTH)
                new = turned(ids_ref[at, lanes], [mid_ref[k, at, lanes] for k in range(4)], rows, turn_by)
                for k in range(4):
                    out_ref[k, at, lanes] = new[k]
                return 0

            lax.fori_loop(0, span // WIDTH, kick, 0, unroll=4)
            block = (slice(None), at, pl.ds(part * span, span))
            copies.append(
                pltpu.make_async_copy(out_ref.at[block], out_hbm.at[block], sems.at[len(copies)])
            )
            copies[-1].start()
    for copy in copies:
        copy.wait()


def body(phase_space, phase_advance, centroid_history, lr_wake, sr_dipole, sr_quad, slice_ids):
    n_bunch, n_mp = lax.axis_size("bunch"), lax.axis_size("mp")
    bunches, parts = phase_space.shape[1:]
    turns_back = centroid_history.shape[1]
    wake_rows = lr_wake.shape[0] // LANES
    vmem, hbm = pl.BlockSpec(memory_space=pltpu.VMEM), pl.BlockSpec(memory_space=pltpu.HBM)
    dma = pltpu.SemaphoreType.DMA

    def held(*shape, dtype=F32):
        return pltpu.VMEM(shape, dtype)

    cent_shape = jax.ShapeDtypeStruct((2, TURNS, bunches), F32)
    state = pl.pallas_call(
        functools.partial(track_kernel, (n_bunch, n_mp)),
        out_shape=(
            jax.ShapeDtypeStruct(phase_space.shape, F32),
            jax.ShapeDtypeStruct((bunches, parts), I32),
            jax.ShapeDtypeStruct((6, bunches, LANES), F32),
            jax.ShapeDtypeStruct((4, bunches, LANES), F32),
            cent_shape,
        ),
        in_specs=[hbm] * 7,
        out_specs=(vmem,) * 5,
        scratch_shapes=[
            held(4, bunches, parts),
            held(bunches, parts, dtype=I32),
            held(2, bunches),
            held(2, bunches, turns_back),
            held(wake_rows, LANES),
            held(SLICES, SLICES),
            held(SLICES, SLICES),
            held(TURNS, bunches, 6, LANES),
            held(TURNS, n_mp, 6, LANES),
            held(2 + 2 * turns_back // n_mp, LANES),
            held(n_bunch, 2 + 2 * turns_back // n_mp, LANES),
            held(2, LANES),
            held(n_bunch, 2, LANES),
            held(TURNS, 7, LANES),
            held(TURNS, n_mp, 7, LANES),
            held(TURNS, 2 * bunches, LANES),
            held(4 + turns_back // n_mp, 2, bunches, LANES),
            held(TURNS, 1, LANES),
            held(2, 3, SLICES, SLICES, dtype=BF16),
            dma((11,)),
            dma((TURNS,)),
            dma((TURNS,)),
            dma((TURNS,)),
            dma((TURNS,)),
            dma((TURNS,)),
            dma((TURNS,)),
        ],
        compiler_params=pltpu.CompilerParams(
            collective_id=0, has_side_effects=True, vmem_limit_bytes=40 << 20
        ),
        cost_estimate=pl.CostEstimate(flops=4 * 65536 * 256, bytes_accessed=3 << 20, transcendentals=0),
        name="track",
    )(
        *(
            pltpu.with_memory_space_constraint(a, pltpu.HBM)
            for a in (
                phase_space,
                phase_advance,
                jnp.transpose(centroid_history, (0, 2, 1)),
                lr_wake.reshape(-1, LANES),
                sr_dipole,
                sr_quad,
                slice_ids,
            )
        )
    )
    return tuple(
        pl.pallas_call(
            last_kernel,
            out_shape=(jax.ShapeDtypeStruct(phase_space.shape, F32), cent_shape),
            in_specs=[vmem] * 5,
            out_specs=(hbm, hbm),
            scratch_shapes=[
                held(*phase_space.shape),
                held(2, TURNS, bunches),
                dma((1 + SPANS * bunches // GROUP,)),
            ],
            compiler_params=pltpu.CompilerParams(vmem_limit_bytes=16 << 20),
            cost_estimate=pl.CostEstimate(flops=100 * 65536, bytes_accessed=1 << 20, transcendentals=0),
            name="last",
        )(*state)
    )


def solution(mesh):
    placed = (
        P(None, "bunch", "mp"),
        P(None, "bunch"),
        P(None, None, "bunch"),
        P(),
        P(),
        P(),
        P(None, "bunch", "mp"),
    )
    return jax.shard_map(
        body,
        mesh=mesh,
        in_specs=placed,
        out_specs=(P(None, "bunch", "mp"), P(None, None, "bunch")),
        check_vma=False,
    )
```

```python
import functools

import jax
import jax.numpy as jnp
from jax import lax
from jax.experimental import pallas as pl
from jax.experimental.pallas import tpu as pltpu
from jax.sharding import PartitionSpec as P

SLICES = 256
TURNS = 2
DETUNE = 0.02
LANES = 128
COARSE, FINE = 8, 32
CHUNK = 512
GROUP = 8
BLOCKS = (8, 8)
WIDTH = 512
SPANS = 2

F32, BF16, I32 = jnp.float32, jnp.bfloat16, jnp.int32
NT = (((1,), (1,)), ((), ()))
HIGHEST = lax.Precision.HIGHEST


def iota(shape, axis):
    return lax.broadcasted_iota(I32, shape, axis)


def gather_lanes(row, index):
    return jnp.take_along_axis(row, index, axis=1, mode="promise_in_bounds")


def two_pieces(v):
    high = v.astype(BF16).astype(F32)
    return high, v - high


def sin_cos(theta):
    n = jnp.round(theta * 0.6366197723675814)
    r = theta - n * 1.5703125
    r = r - n * 4.837512969970703e-4
    r = r - n * 7.549789948768648e-8
    r = jnp.clip(r, -0.8, 0.8)
    q = n.astype(I32)
    z = r * r
    s = r + r * z * (-1.6666654611e-1 + z * (8.3321608736e-3 + z * -1.9515295891e-4))
    c = 1.0 - 0.5 * z + z * z * (
        4.166664568298827e-2 + z * (-1.388731625493765e-3 + z * 2.443315711809948e-5)
    )
    odd = (q & 1) == 1
    sin, cos = jnp.where(odd, c, s), jnp.where(odd, s, c)
    sin = jnp.where((q & 2) == 2, -sin, sin)
    cos = jnp.where(((q + 1) & 2) == 2, -cos, cos)
    return sin, cos


def turned(ids, coords, rows, rot):
    width = ids.shape[1]
    index, upper = ids & (LANES - 1), ids >= LANES

    def looked_up(k):
        pieces = []
        for c in range(width // LANES):
            at = slice(c * LANES, (c + 1) * LANES)
            low, high = gather_lanes(rows[2 * k], index[:, at]), gather_lanes(rows[2 * k + 1], index[:, at])
            pieces.append(jnp.where(upper[:, at], high, low))
        return jnp.concatenate(pieces, axis=1)

    x, mx, y, my = coords
    kx, ky, kq = looked_up(0), looked_up(1), looked_up(2)
    mx = mx + (kx + kq * x)
    my = my + (ky - kq * y)
    action = x * x + mx * mx + y * y + my * my
    sin, cos = sin_cos(DETUNE * action)
    cos_x, sin_x, cos_y, sin_y = (jnp.concatenate([r] * (width // LANES), axis=1) for r in rot)
    x, mx = cos * x + sin * mx, cos * mx - sin * x
    y, my = cos * y + sin * my, cos * my - sin * y
    x, mx = cos_x * x + sin_x * mx, cos_x * mx - sin_x * x
    y, my = cos_y * y + sin_y * my, cos_y * my - sin_y * y
    return x, mx, y, my


def track_kernel(
    rings,
    phase_hbm,
    advance_hbm,
    hist_hbm,
    wake_hbm,
    dipole_hbm,
    quad_hbm,
    ids_hbm,
    mid_ref,
    next_ids,
    rows_ref,
    rot,
    cent_ref,
    phase_ref,
    first_ids,
    advance_ref,
    hist_ref,
    wake_ref,
    dipole_ref,
    quad_ref,
    msg,
    landed,
    hist_src,
    hist_all,
    sum_src,
    sum_all,
    tab_src,
    tab_all,
    ext,
    toep,
    partial,
    split,
    load,
    msg_send,
    msg_recv,
    sum_send,
    sum_recv,
    tab_send,
    tab_recv,
):
    n_bunch, n_mp = rings
    me_b, me_m = lax.axis_index("bunch"), lax.axis_index("mp")
    bunches, parts = mid_ref.shape[1], mid_ref.shape[2]
    turns_back = hist_ref.shape[2]
    share = turns_back // n_mp
    scale = 1.0 / (parts * n_mp)

    def by_reach(n, step):
        return sorted(range(1, n), key=lambda k: -min(k // step, (n - k) // step))

    across, along = by_reach(n_bunch, 1), by_reach(n_mp, 2)
    barrier = pltpu.get_barrier_semaphore()
    for k, n in zip(along, across):
        pl.semaphore_signal(barrier, inc=1, device_id={"mp": lax.rem(me_m + k, n_mp)})
        pl.semaphore_signal(barrier, inc=1, device_id={"bunch": lax.rem(me_b + n, n_bunch)})

    loads = [
        pltpu.make_async_copy(source, target, load.at[k])
        for k, (source, target) in enumerate(
            (
                (phase_hbm.at[0], phase_ref.at[0]),
                (phase_hbm.at[2], phase_ref.at[2]),
                (ids_hbm.at[0], first_ids),
                (hist_hbm, hist_ref),
                (wake_hbm, wake_ref),
                (advance_hbm, advance_ref),
                (dipole_hbm, dipole_ref),
                (quad_hbm, quad_ref),
                (phase_hbm.at[1], phase_ref.at[1]),
                (phase_hbm.at[3], phase_ref.at[3]),
                (ids_hbm.at[1], next_ids),
            )
        )
    ]
    for copy in loads:
        copy.start()

    class Exchange:
        def __init__(self, axis, me, offsets, source, target, send, recv):
            self.axis, self.me, self.offsets = axis, me, offsets
            self.source, self.target, self.send, self.recv = source, target, send, recv

        def start(self):
            for k in self.offsets:
                pltpu.make_async_remote_copy(
                    src_ref=self.source,
                    dst_ref=self.target.at[self.me],
                    send_sem=self.send,
                    recv_sem=self.recv,
                    device_id={self.axis: lax.rem(self.me + k, len(self.offsets) + 1)},
                ).start()

        def all_of_them(self):
            block = self.target.at[pl.ds(0, len(self.offsets))]
            return pltpu.make_async_remote_copy(
                src_ref=block,
                dst_ref=block,
                send_sem=self.send,
                recv_sem=self.recv,
                device_id={self.axis: lax.rem(self.me + 1, len(self.offsets) + 1)},
            )

        def arrive(self):
            self.all_of_them().wait_recv()

        def leave(self):
            self.all_of_them().wait_send()

    sum_x = [
        Exchange("bunch", me_b, across, source, target, sum_send.at[t], sum_recv.at[t])
        for t, (source, target) in enumerate(((hist_src, hist_all), (sum_src, sum_all)))
    ]
    tab_x = [
        Exchange("mp", me_m, along, tab_src.at[t], tab_all.at[t], tab_send.at[t], tab_recv.at[t])
        for t in range(TURNS)
    ]
    msg_x = [
        Exchange("mp", me_m, along, None, landed.at[t], msg_send.at[t], msg_recv.at[t]) for t in range(TURNS)
    ]

    def send_msg(turn, b):
        pltpu.make_async_remote_copy(
            src_ref=msg.at[turn, b],
            dst_ref=landed.at[turn, me_m],
            send_sem=msg_send.at[turn],
            recv_sem=msg_recv.at[turn],
            device_id={"mp": b},
        ).start()

    row8, lane8 = iota((8, LANES), 0), iota((8, LANES), 1)
    place = lax.rem(me_b, 8) * bunches

    def pieces(block):
        parts = []
        for _ in range(3):
            parts.append(block.astype(BF16))
            block = block - parts[-1].astype(F32)
        return jnp.concatenate(parts, axis=1)

    def to_lanes(chosen, block):
        rows = lax.dot_general(
            jnp.concatenate([chosen.astype(BF16)] * 3, axis=1), pieces(block), NT, preferred_element_type=F32
        )
        return jnp.concatenate([rows, jnp.zeros((16, LANES - block.shape[0]), F32)], axis=1)

    def sum_rows(turn, sums_x, sums_y):
        both = to_lanes(jnp.ones((16, LANES), F32), jnp.concatenate([sums_x, sums_y], axis=0) * scale)[:8]
        partial[turn] = pltpu.roll(both, 2 * bunches, 1)[:1]
        x = pltpu.roll(jnp.where(lane8 < bunches, both, 0.0), place, 1)
        y = jnp.where((lane8 >= bunches) & (lane8 < 2 * bunches), both, 0.0)
        y = pltpu.roll(y, lax.rem(place + LANES - bunches, LANES), 1)
        rows = jnp.where(row8 == 0, x, y)[:2]
        return rows

    def lane_sums(p):
        def step(c, acc):
            return acc + phase_ref[p, :, pl.ds(pl.multiple_of(c * LANES, LANES), LANES)]

        return lax.fori_loop(0, parts // LANES, step, jnp.zeros((bunches, LANES), F32), unroll=8)

    loads[3].wait()
    r, c = iota((16, 2 * turns_back), 0), iota((16, 2 * turns_back), 1)
    chosen = jnp.where(c == (r // share) * turns_back + me_m * share + (r & (share - 1)), 1.0, 0.0)
    own = to_lanes(chosen, jnp.concatenate([hist_ref[0], hist_ref[1]], axis=1))[: 2 * share]
    own = pltpu.roll(own, place, 1)

    loads[0].wait()
    loads[1].wait()
    loads[2].wait()

    iota_c = iota((COARSE, CHUNK), 0)
    iota_f = iota((FINE, CHUNK), 0)
    own_lanes = lax.shift_right_logical(lane8, 5) == lax.shift_right_logical(row8, 1)

    def bin_bunch(ids_ref, source, b):
        acc = None
        for c in range(parts // CHUNK):
            at = pl.ds(c * CHUNK, CHUNK)
            ids = ids_ref[pl.ds(b, 1), at]
            x = source[0, pl.ds(b, 1), at]
            y = source[2, pl.ds(b, 1), at]
            coarse = iota_c == ((lax.shift_right_logical(ids, 4) & 6) | lax.shift_right_logical(ids, 7))
            fine = jnp.where(iota_f == (ids & (FINE - 1)), 1.0, 0.0).astype(BF16)
            rows = [jnp.where(coarse, 1.0, 0.0)]
            for v in (*two_pieces(x), *two_pieces(y)):
                rows.append(jnp.where(coarse, jnp.broadcast_to(v, (COARSE, CHUNK)), 0.0))
            weighted = jnp.concatenate(rows, axis=0).astype(BF16)
            part = lax.dot_general(weighted, fine, NT, preferred_element_type=F32)
            acc = part if acc is None else acc + part
        return acc

    def as_tile(acc):
        tiles = []
        for v in (acc[8:16] + acc[16:24], acc[24:32] + acc[32:40], acc[0:8]):
            v = jnp.where(own_lanes, jnp.concatenate([v] * 4, axis=1), 0.0)
            v = v + pltpu.roll(v, 2, 0)
            tiles.append(v + pltpu.roll(v, 4, 0))
        tile = jnp.where(row8 < 2, tiles[0], jnp.where(row8 < 4, tiles[1], tiles[2]))
        return (tile * scale)[:6]

    chips, chip = n_mp // 2, lax.div(me_m, 2)
    core = lax.rem(me_m, 2)

    def owner(k):
        u, side = k // 2, k % 2
        reach = (chips // 2 - (u + 1) // 2) * (2 * (u % 2) - 1)
        there = lax.rem(chip + reach + chips, chips)
        return there * 2 + lax.rem(core + 1 + side, 2)

    def bin_block(turn, ids_ref, source, first, count):
        owners = [owner(first + k) for k in range(count)]
        tiles = [as_tile(bin_bunch(ids_ref, source, b)) for b in owners]
        if first + count == bunches:
            landed[turn, me_m] = tiles[-1]
            owners = owners[:-1]
        for b, tile in zip(owners, tiles):
            msg[turn, b] = tile
        return owners

    def send_all(turn, owners):
        for b in owners:
            send_msg(turn, b)

    def toeplitz_rows(r, half, sub):
        d = me_b * bunches + sub * 8 + row8 - (LANES * half + lane8) - 1
        c = d & (SLICES - 1)
        index = c & (LANES - 1)
        low = jnp.broadcast_to(wake_ref[pl.ds(2 * r, 1), :], (8, LANES))
        high = jnp.broadcast_to(wake_ref[pl.ds(2 * r + 1, 1), :], (8, LANES))
        return jnp.where(c >= LANES, gather_lanes(high, index), gather_lanes(low, index)), d >= 0

    def collected(ref):
        halves = []
        for half in range(2):
            total = ref[8 * half]
            for k in range(1, 8):
                total = total + ref[8 * half + k]
            halves.append(total)
        return halves

    def row_of(tile, k):
        return jnp.broadcast_to(tile[k : k + 1, :], (8, LANES))

    def far_row(turn):
        return to_lanes(jnp.ones((16, LANES), F32), ext[turn])[:1] + partial[turn]

    def lay_wake():
        loads[4].wait()
        kept = jnp.where(me_m == n_mp - 1, 0.0, 1.0)
        first = me_m * share
        for sub in range(2):
            at = pl.ds(8 * sub, 8)
            for half in range(2):
                g0, upper = toeplitz_rows(0, half, sub)
                g1, _ = toeplitz_rows(1, half, sub)
                toep[0, half, at, :] = jnp.where(upper, g0, 0.0)
                toep[1, half, at, :] = jnp.where(upper, g1, g0)
                g = [
                    toeplitz_rows(jnp.minimum(first + k, turns_back), half, sub)[0]
                    for k in range(share + 2)
                ]
                for k in range(share + 1):
                    near = jnp.where(upper, g[k + 1], g[k])
                    toep[2 + k, half, at, :] = near
                toep[2 + share + 1, half, at, :] = near * kept

    def far_first():
        sum_x[0].arrive()
        tiles = collected(hist_all)
        for sub in range(2):
            at = pl.ds(8 * sub, 8)
            for p in range(2):
                total = jnp.zeros((8, LANES), F32)
                for half in range(2):
                    total = total + toep[0, half, at, :] * row_of(tiles[half], 2 * share + p)
                    for k in range(share):
                        total = total + toep[2 + k, half, at, :] * row_of(tiles[half], p * share + k)
                ext[0, pl.ds(p * bunches + 8 * sub, 8), :] = total
        tab_src[0, 6:7, :] = far_row(0)
        return tiles

    def far_later(tiles):
        for sub in range(2):
            at = pl.ds(8 * sub, 8)
            for p in range(2):
                total = jnp.zeros((8, LANES), F32)
                for half in range(2):
                    total = total + toep[1, half, at, :] * row_of(tiles[half], 2 * share + p)
                    for k in range(share):
                        later = toep[3 + k if k < share - 1 else 3 + share, half, at, :]
                        total = total + later * row_of(tiles[half], p * share + k)
                ext[1, pl.ds(p * bunches + 8 * sub, 8), :] = total

    def far_second():
        sum_x[1].arrive()
        cent = collected(sum_all)
        for sub in range(2):
            for p in range(2):
                at = pl.ds(p * bunches + 8 * sub, 8)
                total = ext[1, at, :]
                for half in range(2):
                    total = total + toep[0, half, pl.ds(8 * sub, 8), :] * row_of(cent[half], p)
                ext[1, at, :] = total
        tab_src[1, 6:7, :] = far_row(1)

    def kick_table(turn):
        msg_x[turn].arrive()
        total = landed[turn, 0]
        for k in range(1, 16):
            total = total + landed[turn, k]
        total = jnp.concatenate([total, jnp.zeros((2, LANES), F32)], axis=0)
        wide = jnp.concatenate([total, pltpu.roll(total, 7, 0)], axis=1)
        stack = []
        for _ in range(3):
            stack.append(wide.astype(BF16).astype(F32))
            wide = wide - stack[-1]
        stack = jnp.concatenate(stack, axis=0).astype(BF16)

        def product(which):
            out = None
            for k in reversed(range(3)):
                part = jnp.dot(stack, split[which, k], preferred_element_type=F32)
                for n in reversed(range(3 - k)):
                    block = part[8 * n : 8 * n + 8]
                    out = block if out is None else out + block
            return out

        dip, quad = product(0), product(1)
        low, high = dip[:, :LANES], dip[:, LANES:]
        tab_src[turn, :6, :] = jnp.concatenate(
            [low[0:1], high[0:1], low[2:3], high[2:3], quad[4:5, :LANES], quad[4:5, LANES:]], axis=0
        )
        tab_x[turn].start()
        tab_all[turn, me_m] = tab_src[turn]

    full_row, full_lane = iota((bunches, LANES), 0), iota((bunches, LANES), 1)

    def lay_rows(turn):
        tab_x[turn].arrive()
        total = tab_all[turn, 0, 6:7, :]
        for k in range(1, n_mp):
            total = total + tab_all[turn, k, 6:7, :]
        for p in range(2):
            cent_ref[p, turn : turn + 1, :] = pltpu.roll(total, LANES - (2 + p) * bunches, 1)[:, :bunches]
        total = jnp.broadcast_to(total, (bunches, LANES))
        far = [
            jnp.sum(jnp.where(full_lane == full_row + p * bunches, total, 0.0), axis=1, keepdims=True)
            for p in range(2)
        ]

        def column(k):
            return jnp.concatenate([tab_all[turn, n, k : k + 1, :] for n in range(bunches)], axis=0)

        for k in range(6):
            row = column(k)
            rows_ref[k] = row + far[k // 2] if k < 4 else row

    half = bunches // 2
    first_sums = (lane_sums(0), lane_sums(2))
    owners = bin_block(0, first_ids, phase_ref, 0, half)
    own = jnp.concatenate([own, sum_rows(0, *first_sums)], axis=0)
    hist_src[...] = own
    hist_all[me_b] = own
    owners = owners + bin_block(0, first_ids, phase_ref, half, half)
    pl.semaphore_wait(barrier, n_mp + n_bunch - 2)
    send_all(0, owners[:half])
    sum_x[0].start()
    send_all(0, owners[half:])
    lay_wake()

    loads[5].wait()
    for p in range(2):
        wide = jnp.concatenate([advance_ref[p : p + 1, :], jnp.zeros((1, LANES - bunches), F32)], axis=1)
        wide = jnp.broadcast_to(wide, (bunches, LANES))
        column = jnp.sum(jnp.where(full_row == full_lane, wide, 0.0), axis=1, keepdims=True)
        sin, cos = sin_cos(jnp.broadcast_to(column, (bunches, LANES)))
        rot[2 * p] = cos
        rot[2 * p + 1] = sin

    for k, ref in enumerate((dipole_ref, quad_ref)):
        loads[6 + k].wait()
        rest = jnp.transpose(ref[...])
        for n in range(3):
            piece = rest.astype(BF16)
            split[k, n] = piece
            rest = rest - piece.astype(F32)
    tiles = far_first()
    kick_table(0)
    far_later(tiles)
    loads[8].wait()
    loads[9].wait()
    loads[10].wait()
    lay_rows(0)

    sums = []
    for g in range(bunches // GROUP):
        at = pl.ds(g * GROUP, GROUP)
        rows = [rows_ref[k, at, :] for k in range(6)]
        turn_by = [rot[k, at, :] for k in range(4)]

        def kick(c, acc):
            lanes = pl.ds(pl.multiple_of(c * WIDTH, WIDTH), WIDTH)
            new = turned(first_ids[at, lanes], [phase_ref[k, at, lanes] for k in range(4)], rows, turn_by)
            for k in range(4):
                mid_ref[k, at, lanes] = new[k]
            acc = list(acc)
            for s in range(WIDTH // LANES):
                cut = slice(s * LANES, (s + 1) * LANES)
                acc = [acc[0] + new[0][:, cut], acc[1] + new[2][:, cut]]
            return tuple(acc)

        zero = jnp.zeros((GROUP, LANES), F32)
        sums.append(lax.fori_loop(0, parts // WIDTH, kick, (zero, zero), unroll=8))
    sums = [jnp.concatenate([s[p] for s in sums], axis=0) for p in range(2)]
    rows = sum_rows(1, *sums)
    sum_src[...] = rows
    sum_all[me_b] = rows
    sum_x[1].start()
    first = 0
    for count in BLOCKS:
        send_all(1, bin_block(1, next_ids, mid_ref, first, count))
        first += count
    far_second()
    kick_table(1)
    lay_rows(1)

    for turn in range(TURNS):
        for exchange in (msg_x[turn], tab_x[turn], sum_x[turn]):
            exchange.leave()


def last_kernel(mid_ref, ids_ref, rows_ref, rot, cent_in, out_hbm, cent_hbm, out_ref, cent_ref, sems):
    bunches, parts = mid_ref.shape[1], mid_ref.shape[2]
    cent_ref[...] = cent_in[...]
    copies = [pltpu.make_async_copy(cent_ref, cent_hbm, sems.at[0])]
    copies[0].start()
    span = parts // SPANS
    for g in range(bunches // GROUP):
        at = pl.ds(g * GROUP, GROUP)
        rows = [rows_ref[k, at, :] for k in range(6)]
        turn_by = [rot[k, at, :] for k in range(4)]
        for part in range(SPANS):

            def kick(c, _):
                lanes = pl.ds(pl.multiple_of(part * span + c * WIDTH, WIDTH), WIDTH)
                new = turned(ids_ref[at, lanes], [mid_ref[k, at, lanes] for k in range(4)], rows, turn_by)
                for k in range(4):
                    out_ref[k, at, lanes] = new[k]
                return 0

            lax.fori_loop(0, span // WIDTH, kick, 0, unroll=4)
            block = (slice(None), at, pl.ds(part * span, span))
            copies.append(
                pltpu.make_async_copy(out_ref.at[block], out_hbm.at[block], sems.at[len(copies)])
            )
            copies[-1].start()
    for copy in copies:
        copy.wait()


def body(phase_space, phase_advance, centroid_history, lr_wake, sr_dipole, sr_quad, slice_ids):
    n_bunch, n_mp = lax.axis_size("bunch"), lax.axis_size("mp")
    bunches, parts = phase_space.shape[1:]
    turns_back = centroid_history.shape[1]
    wake_rows = lr_wake.shape[0] // LANES
    vmem, hbm = pl.BlockSpec(memory_space=pltpu.VMEM), pl.BlockSpec(memory_space=pltpu.HBM)
    dma = pltpu.SemaphoreType.DMA

    def held(*shape, dtype=F32):
        return pltpu.VMEM(shape, dtype)

    cent_shape = jax.ShapeDtypeStruct((2, TURNS, bunches), F32)
    state = pl.pallas_call(
        functools.partial(track_kernel, (n_bunch, n_mp)),
        out_shape=(
            jax.ShapeDtypeStruct(phase_space.shape, F32),
            jax.ShapeDtypeStruct((bunches, parts), I32),
            jax.ShapeDtypeStruct((6, bunches, LANES), F32),
            jax.ShapeDtypeStruct((4, bunches, LANES), F32),
            cent_shape,
        ),
        in_specs=[hbm] * 7,
        out_specs=(vmem,) * 5,
        scratch_shapes=[
            held(4, bunches, parts),
            held(bunches, parts, dtype=I32),
            held(2, bunches),
            held(2, bunches, turns_back),
            held(wake_rows, LANES),
            held(SLICES, SLICES),
            held(SLICES, SLICES),
            held(TURNS, bunches, 6, LANES),
            held(TURNS, n_mp, 6, LANES),
            held(2 + 2 * turns_back // n_mp, LANES),
            held(n_bunch, 2 + 2 * turns_back // n_mp, LANES),
            held(2, LANES),
            held(n_bunch, 2, LANES),
            held(TURNS, 7, LANES),
            held(TURNS, n_mp, 7, LANES),
            held(TURNS, 2 * bunches, LANES),
            held(4 + turns_back // n_mp, 2, bunches, LANES),
            held(TURNS, 1, LANES),
            held(2, 3, SLICES, SLICES, dtype=BF16),
            dma((11,)),
            dma((TURNS,)),
            dma((TURNS,)),
            dma((TURNS,)),
            dma((TURNS,)),
            dma((TURNS,)),
            dma((TURNS,)),
        ],
        compiler_params=pltpu.CompilerParams(
            collective_id=0, has_side_effects=True, vmem_limit_bytes=40 << 20
        ),
        cost_estimate=pl.CostEstimate(flops=4 * 65536 * 256, bytes_accessed=3 << 20, transcendentals=0),
        name="track",
    )(
        *(
            pltpu.with_memory_space_constraint(a, pltpu.HBM)
            for a in (
                phase_space,
                phase_advance,
                jnp.transpose(centroid_history, (0, 2, 1)),
                lr_wake.reshape(-1, LANES),
                sr_dipole,
                sr_quad,
                slice_ids,
            )
        )
    )
    return tuple(
        pl.pallas_call(
            last_kernel,
            out_shape=(jax.ShapeDtypeStruct(phase_space.shape, F32), cent_shape),
            in_specs=[vmem] * 5,
            out_specs=(hbm, hbm),
            scratch_shapes=[
                held(*phase_space.shape),
                held(2, TURNS, bunches),
                dma((1 + SPANS * bunches // GROUP,)),
            ],
            compiler_params=pltpu.CompilerParams(vmem_limit_bytes=16 << 20),
            cost_estimate=pl.CostEstimate(flops=100 * 65536, bytes_accessed=1 << 20, transcendentals=0),
            name="last",
        )(*state)
    )


def solution(mesh):
    placed = (
        P(None, "bunch", "mp"),
        P(None, "bunch"),
        P(None, None, "bunch"),
        P(),
        P(),
        P(),
        P(None, "bunch", "mp"),
    )
    return jax.shard_map(
        body,
        mesh=mesh,
        in_specs=placed,
        out_specs=(P(None, "bunch", "mp"), P(None, None, "bunch")),
        check_vma=False,
    )
```

```python
import functools

import jax
import jax.numpy as jnp
from jax import lax
from jax.experimental import pallas as pl
from jax.experimental.pallas import tpu as pltpu
from jax.sharding import PartitionSpec as P

SLICES = 256
TURNS = 2
DETUNE = 0.02
LANES = 128
COARSE, FINE = 8, 32
CHUNK = 512
GROUP = 8
BLOCKS = (8, 8)
WIDTH = 512
SPANS = 2

F32, BF16, I32 = jnp.float32, jnp.bfloat16, jnp.int32
NT = (((1,), (1,)), ((), ()))
HIGHEST = lax.Precision.HIGHEST


def iota(shape, axis):
    return lax.broadcasted_iota(I32, shape, axis)


def gather_lanes(row, index):
    return jnp.take_along_axis(row, index, axis=1, mode="promise_in_bounds")


def two_pieces(v):
    high = v.astype(BF16).astype(F32)
    return high, v - high


def sin_cos(theta):
    n = jnp.round(theta * 0.6366197723675814)
    r = theta - n * 1.5703125
    r = r - n * 4.837512969970703e-4
    r = r - n * 7.549789948768648e-8
    r = jnp.clip(r, -0.8, 0.8)
    q = n.astype(I32)
    z = r * r
    s = r + r * z * (-1.6666654611e-1 + z * (8.3321608736e-3 + z * -1.9515295891e-4))
    c = 1.0 - 0.5 * z + z * z * (
        4.166664568298827e-2 + z * (-1.388731625493765e-3 + z * 2.443315711809948e-5)
    )
    odd = (q & 1) == 1
    sin, cos = jnp.where(odd, c, s), jnp.where(odd, s, c)
    sin = jnp.where((q & 2) == 2, -sin, sin)
    cos = jnp.where(((q + 1) & 2) == 2, -cos, cos)
    return sin, cos


def turned(ids, coords, rows, rot):
    width = ids.shape[1]
    index, upper = ids & (LANES - 1), ids >= LANES

    def looked_up(k):
        pieces = []
        for c in range(width // LANES):
            at = slice(c * LANES, (c + 1) * LANES)
            low, high = gather_lanes(rows[2 * k], index[:, at]), gather_lanes(rows[2 * k + 1], index[:, at])
            pieces.append(jnp.where(upper[:, at], high, low))
        return jnp.concatenate(pieces, axis=1)

    x, mx, y, my = coords
    kx, ky, kq = looked_up(0), looked_up(1), looked_up(2)
    mx = mx + (kx + kq * x)
    my = my + (ky - kq * y)
    action = x * x + mx * mx + y * y + my * my
    sin, cos = sin_cos(DETUNE * action)
    cos_x, sin_x, cos_y, sin_y = (jnp.concatenate([r] * (width // LANES), axis=1) for r in rot)
    x, mx = cos * x + sin * mx, cos * mx - sin * x
    y, my = cos * y + sin * my, cos * my - sin * y
    x, mx = cos_x * x + sin_x * mx, cos_x * mx - sin_x * x
    y, my = cos_y * y + sin_y * my, cos_y * my - sin_y * y
    return x, mx, y, my


def track_kernel(
    rings,
    phase_hbm,
    advance_hbm,
    hist_hbm,
    wake_hbm,
    dipole_hbm,
    quad_hbm,
    ids_hbm,
    mid_ref,
    next_ids,
    rows_ref,
    rot,
    cent_ref,
    phase_ref,
    first_ids,
    advance_ref,
    hist_ref,
    wake_ref,
    dipole_ref,
    quad_ref,
    msg,
    landed,
    hist_src,
    hist_all,
    sum_src,
    sum_all,
    tab_src,
    tab_all,
    ext,
    toep,
    partial,
    split,
    load,
    msg_send,
    msg_recv,
    sum_send,
    sum_recv,
    tab_send,
    tab_recv,
):
    n_bunch, n_mp = rings
    me_b, me_m = lax.axis_index("bunch"), lax.axis_index("mp")
    bunches, parts = mid_ref.shape[1], mid_ref.shape[2]
    turns_back = hist_ref.shape[2]
    share = turns_back // n_mp
    scale = 1.0 / (parts * n_mp)

    def by_reach(n, step):
        return sorted(range(1, n), key=lambda k: -min(k // step, (n - k) // step))

    across, along = by_reach(n_bunch, 1), by_reach(n_mp, 2)
    loads = [
        pltpu.make_async_copy(source, target, load.at[k])
        for k, (source, target) in enumerate(
            (
                (phase_hbm.at[0], phase_ref.at[0]),
                (phase_hbm.at[2], phase_ref.at[2]),
                (ids_hbm.at[0], first_ids),
                (hist_hbm, hist_ref),
                (wake_hbm, wake_ref),
                (advance_hbm, advance_ref),
                (dipole_hbm, dipole_ref),
                (quad_hbm, quad_ref),
                (phase_hbm.at[1], phase_ref.at[1]),
                (phase_hbm.at[3], phase_ref.at[3]),
                (ids_hbm.at[1], next_ids),
            )
        )
    ]
    for copy in loads[:4]:
        copy.start()

    barrier = pltpu.get_barrier_semaphore()
    for k, n in zip(along, across):
        pl.semaphore_signal(barrier, inc=1, device_id={"mp": lax.rem(me_m + k, n_mp)})
        pl.semaphore_signal(barrier, inc=1, device_id={"bunch": lax.rem(me_b + n, n_bunch)})

    for copy in loads[4:]:
        copy.start()

    class Exchange:
        def __init__(self, axis, me, offsets, source, target, send, recv):
            self.axis, self.me, self.offsets = axis, me, offsets
            self.source, self.target, self.send, self.recv = source, target, send, recv

        def start(self):
            for k in self.offsets:
                pltpu.make_async_remote_copy(
                    src_ref=self.source,
                    dst_ref=self.target.at[self.me],
                    send_sem=self.send,
                    recv_sem=self.recv,
                    device_id={self.axis: lax.rem(self.me + k, len(self.offsets) + 1)},
                ).start()

        def all_of_them(self):
            block = self.target.at[pl.ds(0, len(self.offsets))]
            return pltpu.make_async_remote_copy(
                src_ref=block,
                dst_ref=block,
                send_sem=self.send,
                recv_sem=self.recv,
                device_id={self.axis: lax.rem(self.me + 1, len(self.offsets) + 1)},
            )

        def arrive(self):
            self.all_of_them().wait_recv()

        def leave(self):
            self.all_of_them().wait_send()

    sum_x = [
        Exchange("bunch", me_b, across, source, target, sum_send.at[t], sum_recv.at[t])
        for t, (source, target) in enumerate(((hist_src, hist_all), (sum_src, sum_all)))
    ]
    tab_x = [
        Exchange("mp", me_m, along, tab_src.at[t], tab_all.at[t], tab_send.at[t], tab_recv.at[t])
        for t in range(TURNS)
    ]
    msg_x = [
        Exchange("mp", me_m, along, None, landed.at[t], msg_send.at[t], msg_recv.at[t]) for t in range(TURNS)
    ]

    def send_msg(turn, b):
        pltpu.make_async_remote_copy(
            src_ref=msg.at[turn, b],
            dst_ref=landed.at[turn, me_m],
            send_sem=msg_send.at[turn],
            recv_sem=msg_recv.at[turn],
            device_id={"mp": b},
        ).start()

    row8, lane8 = iota((8, LANES), 0), iota((8, LANES), 1)
    place = lax.rem(me_b, 8) * bunches

    def pieces(block):
        parts = []
        for _ in range(3):
            parts.append(block.astype(BF16))
            block = block - parts[-1].astype(F32)
        return jnp.concatenate(parts, axis=1)

    def to_lanes(chosen, block):
        rows = lax.dot_general(
            jnp.concatenate([chosen.astype(BF16)] * 3, axis=1), pieces(block), NT, preferred_element_type=F32
        )
        return jnp.concatenate([rows, jnp.zeros((16, LANES - block.shape[0]), F32)], axis=1)

    def sum_rows(turn, sums_x, sums_y):
        both = to_lanes(jnp.ones((16, LANES), F32), jnp.concatenate([sums_x, sums_y], axis=0) * scale)[:8]
        partial[turn] = pltpu.roll(both, 2 * bunches, 1)[:1]
        x = pltpu.roll(jnp.where(lane8 < bunches, both, 0.0), place, 1)
        y = jnp.where((lane8 >= bunches) & (lane8 < 2 * bunches), both, 0.0)
        y = pltpu.roll(y, lax.rem(place + LANES - bunches, LANES), 1)
        rows = jnp.where(row8 == 0, x, y)[:2]
        return rows

    def lane_sums(p):
        def step(c, acc):
            return acc + phase_ref[p, :, pl.ds(pl.multiple_of(c * LANES, LANES), LANES)]

        return lax.fori_loop(0, parts // LANES, step, jnp.zeros((bunches, LANES), F32), unroll=8)

    loads[3].wait()
    r, c = iota((16, 2 * turns_back), 0), iota((16, 2 * turns_back), 1)
    chosen = jnp.where(c == (r // share) * turns_back + me_m * share + (r & (share - 1)), 1.0, 0.0)
    own = to_lanes(chosen, jnp.concatenate([hist_ref[0], hist_ref[1]], axis=1))[: 2 * share]
    own = pltpu.roll(own, place, 1)

    loads[0].wait()
    loads[1].wait()
    loads[2].wait()

    iota_c = iota((COARSE, CHUNK), 0)
    iota_f = iota((FINE, CHUNK), 0)
    own_lanes = lax.shift_right_logical(lane8, 5) == lax.shift_right_logical(row8, 1)

    def bin_bunch(ids_ref, source, b):
        acc = None
        for c in range(parts // CHUNK):
            at = pl.ds(c * CHUNK, CHUNK)
            ids = ids_ref[pl.ds(b, 1), at]
            x = source[0, pl.ds(b, 1), at]
            y = source[2, pl.ds(b, 1), at]
            coarse = iota_c == ((lax.shift_right_logical(ids, 4) & 6) | lax.shift_right_logical(ids, 7))
            fine = jnp.where(iota_f == (ids & (FINE - 1)), 1.0, 0.0).astype(BF16)
            rows = [jnp.where(coarse, 1.0, 0.0)]
            for v in (*two_pieces(x), *two_pieces(y)):
                rows.append(jnp.where(coarse, jnp.broadcast_to(v, (COARSE, CHUNK)), 0.0))
            weighted = jnp.concatenate(rows, axis=0).astype(BF16)
            part = lax.dot_general(weighted, fine, NT, preferred_element_type=F32)
            acc = part if acc is None else acc + part
        return acc

    def as_tile(acc):
        tiles = []
        for v in (acc[8:16] + acc[16:24], acc[24:32] + acc[32:40], acc[0:8]):
            v = jnp.where(own_lanes, jnp.concatenate([v] * 4, axis=1), 0.0)
            v = v + pltpu.roll(v, 2, 0)
            tiles.append(v + pltpu.roll(v, 4, 0))
        tile = jnp.where(row8 < 2, tiles[0], jnp.where(row8 < 4, tiles[1], tiles[2]))
        return (tile * scale)[:6]

    chips, chip = n_mp // 2, lax.div(me_m, 2)
    core = lax.rem(me_m, 2)

    def owner(k):
        u, side = k // 2, k % 2
        reach = (chips // 2 - (u + 1) // 2) * (2 * (u % 2) - 1)
        there = lax.rem(chip + reach + chips, chips)
        return there * 2 + lax.rem(core + 1 + side, 2)

    def bin_block(turn, ids_ref, source, first, count):
        owners = [owner(first + k) for k in range(count)]
        tiles = [as_tile(bin_bunch(ids_ref, source, b)) for b in owners]
        if first + count == bunches:
            landed[turn, me_m] = tiles[-1]
            owners = owners[:-1]
        for b, tile in zip(owners, tiles):
            msg[turn, b] = tile
        return owners

    def send_all(turn, owners):
        for b in owners:
            send_msg(turn, b)

    def toeplitz_rows(r, half, sub):
        d = me_b * bunches + sub * 8 + row8 - (LANES * half + lane8) - 1
        c = d & (SLICES - 1)
        index = c & (LANES - 1)
        low = jnp.broadcast_to(wake_ref[pl.ds(2 * r, 1), :], (8, LANES))
        high = jnp.broadcast_to(wake_ref[pl.ds(2 * r + 1, 1), :], (8, LANES))
        return jnp.where(c >= LANES, gather_lanes(high, index), gather_lanes(low, index)), d >= 0

    def collected(ref):
        halves = []
        for half in range(2):
            total = ref[8 * half]
            for k in range(1, 8):
                total = total + ref[8 * half + k]
            halves.append(total)
        return halves

    def row_of(tile, k):
        return jnp.broadcast_to(tile[k : k + 1, :], (8, LANES))

    def far_row(turn):
        return to_lanes(jnp.ones((16, LANES), F32), ext[turn])[:1] + partial[turn]

    def lay_wake():
        loads[4].wait()
        kept = jnp.where(me_m == n_mp - 1, 0.0, 1.0)
        first = me_m * share
        for sub in range(2):
            at = pl.ds(8 * sub, 8)
            for half in range(2):
                g0, upper = toeplitz_rows(0, half, sub)
                g1, _ = toeplitz_rows(1, half, sub)
                toep[0, half, at, :] = jnp.where(upper, g0, 0.0)
                toep[1, half, at, :] = jnp.where(upper, g1, g0)
                g = [
                    toeplitz_rows(jnp.minimum(first + k, turns_back), half, sub)[0]
                    for k in range(share + 2)
                ]
                for k in range(share + 1):
                    near = jnp.where(upper, g[k + 1], g[k])
                    toep[2 + k, half, at, :] = near
                toep[2 + share + 1, half, at, :] = near * kept

    def far_first():
        sum_x[0].arrive()
        tiles = collected(hist_all)
        for sub in range(2):
            at = pl.ds(8 * sub, 8)
            for p in range(2):
                total = jnp.zeros((8, LANES), F32)
                for half in range(2):
                    total = total + toep[0, half, at, :] * row_of(tiles[half], 2 * share + p)
                    for k in range(share):
                        total = total + toep[2 + k, half, at, :] * row_of(tiles[half], p * share + k)
                ext[0, pl.ds(p * bunches + 8 * sub, 8), :] = total
        tab_src[0, 6:7, :] = far_row(0)
        return tiles

    def far_later(tiles):
        for sub in range(2):
            at = pl.ds(8 * sub, 8)
            for p in range(2):
                total = jnp.zeros((8, LANES), F32)
                for half in range(2):
                    total = total + toep[1, half, at, :] * row_of(tiles[half], 2 * share + p)
                    for k in range(share):
                        later = toep[3 + k if k < share - 1 else 3 + share, half, at, :]
                        total = total + later * row_of(tiles[half], p * share + k)
                ext[1, pl.ds(p * bunches + 8 * sub, 8), :] = total

    def far_second():
        sum_x[1].arrive()
        cent = collected(sum_all)
        for sub in range(2):
            for p in range(2):
                at = pl.ds(p * bunches + 8 * sub, 8)
                total = ext[1, at, :]
                for half in range(2):
                    total = total + toep[0, half, pl.ds(8 * sub, 8), :] * row_of(cent[half], p)
                ext[1, at, :] = total
        tab_src[1, 6:7, :] = far_row(1)

    def kick_table(turn):
        msg_x[turn].arrive()
        total = landed[turn, 0]
        for k in range(1, 16):
            total = total + landed[turn, k]
        total = jnp.concatenate([total, jnp.zeros((2, LANES), F32)], axis=0)
        wide = jnp.concatenate([total, pltpu.roll(total, 7, 0)], axis=1)
        stack = []
        for _ in range(3):
            stack.append(wide.astype(BF16).astype(F32))
            wide = wide - stack[-1]
        stack = jnp.concatenate(stack, axis=0).astype(BF16)

        def product(which):
            out = None
            for k in reversed(range(3)):
                part = jnp.dot(stack, split[which, k], preferred_element_type=F32)
                for n in reversed(range(3 - k)):
                    block = part[8 * n : 8 * n + 8]
                    out = block if out is None else out + block
            return out

        dip, quad = product(0), product(1)
        low, high = dip[:, :LANES], dip[:, LANES:]
        tab_src[turn, :6, :] = jnp.concatenate(
            [low[0:1], high[0:1], low[2:3], high[2:3], quad[4:5, :LANES], quad[4:5, LANES:]], axis=0
        )
        tab_x[turn].start()
        tab_all[turn, me_m] = tab_src[turn]

    full_row, full_lane = iota((bunches, LANES), 0), iota((bunches, LANES), 1)

    def lay_rows(turn):
        tab_x[turn].arrive()
        total = tab_all[turn, 0, 6:7, :]
        for k in range(1, n_mp):
            total = total + tab_all[turn, k, 6:7, :]
        for p in range(2):
            cent_ref[p, turn : turn + 1, :] = pltpu.roll(total, LANES - (2 + p) * bunches, 1)[:, :bunches]
        total = jnp.broadcast_to(total, (bunches, LANES))
        far = [
            jnp.sum(jnp.where(full_lane == full_row + p * bunches, total, 0.0), axis=1, keepdims=True)
            for p in range(2)
        ]

        def column(k):
            return jnp.concatenate([tab_all[turn, n, k : k + 1, :] for n in range(bunches)], axis=0)

        for k in range(6):
            row = column(k)
            rows_ref[k] = row + far[k // 2] if k < 4 else row

    half = bunches // 2
    first_sums = (lane_sums(0), lane_sums(2))
    owners = bin_block(0, first_ids, phase_ref, 0, half)
    own = jnp.concatenate([own, sum_rows(0, *first_sums)], axis=0)
    hist_src[...] = own
    hist_all[me_b] = own
    owners = owners + bin_block(0, first_ids, phase_ref, half, half)
    pl.semaphore_wait(barrier, n_mp + n_bunch - 2)
    send_all(0, owners[:half])
    sum_x[0].start()
    send_all(0, owners[half:])
    lay_wake()

    loads[5].wait()
    for p in range(2):
        wide = jnp.concatenate([advance_ref[p : p + 1, :], jnp.zeros((1, LANES - bunches), F32)], axis=1)
        wide = jnp.broadcast_to(wide, (bunches, LANES))
        column = jnp.sum(jnp.where(full_row == full_lane, wide, 0.0), axis=1, keepdims=True)
        sin, cos = sin_cos(jnp.broadcast_to(column, (bunches, LANES)))
        rot[2 * p] = cos
        rot[2 * p + 1] = sin

    for k, ref in enumerate((dipole_ref, quad_ref)):
        loads[6 + k].wait()
        rest = jnp.transpose(ref[...])
        for n in range(3):
            piece = rest.astype(BF16)
            split[k, n] = piece
            rest = rest - piece.astype(F32)
    tiles = far_first()
    kick_table(0)
    far_later(tiles)
    loads[8].wait()
    loads[9].wait()
    loads[10].wait()
    lay_rows(0)

    sums = []
    for g in range(bunches // GROUP):
        at = pl.ds(g * GROUP, GROUP)
        rows = [rows_ref[k, at, :] for k in range(6)]
        turn_by = [rot[k, at, :] for k in range(4)]

        def kick(c, acc):
            lanes = pl.ds(pl.multiple_of(c * WIDTH, WIDTH), WIDTH)
            new = turned(first_ids[at, lanes], [phase_ref[k, at, lanes] for k in range(4)], rows, turn_by)
            for k in range(4):
                mid_ref[k, at, lanes] = new[k]
            acc = list(acc)
            for s in range(WIDTH // LANES):
                cut = slice(s * LANES, (s + 1) * LANES)
                acc = [acc[0] + new[0][:, cut], acc[1] + new[2][:, cut]]
            return tuple(acc)

        zero = jnp.zeros((GROUP, LANES), F32)
        sums.append(lax.fori_loop(0, parts // WIDTH, kick, (zero, zero), unroll=8))
    sums = [jnp.concatenate([s[p] for s in sums], axis=0) for p in range(2)]
    rows = sum_rows(1, *sums)
    sum_src[...] = rows
    sum_all[me_b] = rows
    sum_x[1].start()
    first = 0
    for count in BLOCKS:
        send_all(1, bin_block(1, next_ids, mid_ref, first, count))
        first += count
    far_second()
    kick_table(1)
    lay_rows(1)

    for turn in range(TURNS):
        for exchange in (msg_x[turn], tab_x[turn], sum_x[turn]):
            exchange.leave()


def last_kernel(mid_ref, ids_ref, rows_ref, rot, cent_in, out_hbm, cent_hbm, out_ref, cent_ref, sems):
    bunches, parts = mid_ref.shape[1], mid_ref.shape[2]
    cent_ref[...] = cent_in[...]
    copies = [pltpu.make_async_copy(cent_ref, cent_hbm, sems.at[0])]
    copies[0].start()
    span = parts // SPANS
    for g in range(bunches // GROUP):
        at = pl.ds(g * GROUP, GROUP)
        rows = [rows_ref[k, at, :] for k in range(6)]
        turn_by = [rot[k, at, :] for k in range(4)]
        for part in range(SPANS):

            def kick(c, _):
                lanes = pl.ds(pl.multiple_of(part * span + c * WIDTH, WIDTH), WIDTH)
                new = turned(ids_ref[at, lanes], [mid_ref[k, at, lanes] for k in range(4)], rows, turn_by)
                for k in range(4):
                    out_ref[k, at, lanes] = new[k]
                return 0

            lax.fori_loop(0, span // WIDTH, kick, 0, unroll=4)
            block = (slice(None), at, pl.ds(part * span, span))
            copies.append(
                pltpu.make_async_copy(out_ref.at[block], out_hbm.at[block], sems.at[len(copies)])
            )
            copies[-1].start()
    for copy in copies:
        copy.wait()


def body(phase_space, phase_advance, centroid_history, lr_wake, sr_dipole, sr_quad, slice_ids):
    n_bunch, n_mp = lax.axis_size("bunch"), lax.axis_size("mp")
    bunches, parts = phase_space.shape[1:]
    turns_back = centroid_history.shape[1]
    wake_rows = lr_wake.shape[0] // LANES
    vmem, hbm = pl.BlockSpec(memory_space=pltpu.VMEM), pl.BlockSpec(memory_space=pltpu.HBM)
    dma = pltpu.SemaphoreType.DMA

    def held(*shape, dtype=F32):
        return pltpu.VMEM(shape, dtype)

    cent_shape = jax.ShapeDtypeStruct((2, TURNS, bunches), F32)
    state = pl.pallas_call(
        functools.partial(track_kernel, (n_bunch, n_mp)),
        out_shape=(
            jax.ShapeDtypeStruct(phase_space.shape, F32),
            jax.ShapeDtypeStruct((bunches, parts), I32),
            jax.ShapeDtypeStruct((6, bunches, LANES), F32),
            jax.ShapeDtypeStruct((4, bunches, LANES), F32),
            cent_shape,
        ),
        in_specs=[hbm] * 7,
        out_specs=(vmem,) * 5,
        scratch_shapes=[
            held(4, bunches, parts),
            held(bunches, parts, dtype=I32),
            held(2, bunches),
            held(2, bunches, turns_back),
            held(wake_rows, LANES),
            held(SLICES, SLICES),
            held(SLICES, SLICES),
            held(TURNS, bunches, 6, LANES),
            held(TURNS, n_mp, 6, LANES),
            held(2 + 2 * turns_back // n_mp, LANES),
            held(n_bunch, 2 + 2 * turns_back // n_mp, LANES),
            held(2, LANES),
            held(n_bunch, 2, LANES),
            held(TURNS, 7, LANES),
            held(TURNS, n_mp, 7, LANES),
            held(TURNS, 2 * bunches, LANES),
            held(4 + turns_back // n_mp, 2, bunches, LANES),
            held(TURNS, 1, LANES),
            held(2, 3, SLICES, SLICES, dtype=BF16),
            dma((11,)),
            dma((TURNS,)),
            dma((TURNS,)),
            dma((TURNS,)),
            dma((TURNS,)),
            dma((TURNS,)),
            dma((TURNS,)),
        ],
        compiler_params=pltpu.CompilerParams(
            collective_id=0, has_side_effects=True, vmem_limit_bytes=40 << 20
        ),
        cost_estimate=pl.CostEstimate(flops=4 * 65536 * 256, bytes_accessed=3 << 20, transcendentals=0),
        name="track",
    )(
        *(
            pltpu.with_memory_space_constraint(a, pltpu.HBM)
            for a in (
                phase_space,
                phase_advance,
                jnp.transpose(centroid_history, (0, 2, 1)),
                lr_wake.reshape(-1, LANES),
                sr_dipole,
                sr_quad,
                slice_ids,
            )
        )
    )
    return tuple(
        pl.pallas_call(
            last_kernel,
            out_shape=(jax.ShapeDtypeStruct(phase_space.shape, F32), cent_shape),
            in_specs=[vmem] * 5,
            out_specs=(hbm, hbm),
            scratch_shapes=[
                held(*phase_space.shape),
                held(2, TURNS, bunches),
                dma((1 + SPANS * bunches // GROUP,)),
            ],
            compiler_params=pltpu.CompilerParams(vmem_limit_bytes=16 << 20),
            cost_estimate=pl.CostEstimate(flops=100 * 65536, bytes_accessed=1 << 20, transcendentals=0),
            name="last",
        )(*state)
    )


def solution(mesh):
    placed = (
        P(None, "bunch", "mp"),
        P(None, "bunch"),
        P(None, None, "bunch"),
        P(),
        P(),
        P(),
        P(None, "bunch", "mp"),
    )
    return jax.shard_map(
        body,
        mesh=mesh,
        in_specs=placed,
        out_specs=(P(None, "bunch", "mp"), P(None, None, "bunch")),
        check_vma=False,
    )
```

```python
import functools

import jax
import jax.numpy as jnp
from jax import lax
from jax.experimental import pallas as pl
from jax.experimental.pallas import tpu as pltpu
from jax.sharding import PartitionSpec as P

SLICES = 256
TURNS = 2
DETUNE = 0.02
LANES = 128
COARSE, FINE = 8, 32
CHUNK = 512
GROUP = 8
BLOCKS = (8, 8)
WIDTH = 512
SPANS = 2

F32, BF16, I32 = jnp.float32, jnp.bfloat16, jnp.int32
NT = (((1,), (1,)), ((), ()))
HIGHEST = lax.Precision.HIGHEST


def iota(shape, axis):
    return lax.broadcasted_iota(I32, shape, axis)


def gather_lanes(row, index):
    return jnp.take_along_axis(row, index, axis=1, mode="promise_in_bounds")


def added(terms):
    while len(terms) > 1:
        terms = [sum(terms[k + 1 : k + 2], terms[k]) for k in range(0, len(terms), 2)]
    return terms[0]


def two_pieces(v):
    high = v.astype(BF16).astype(F32)
    return high, v - high


def sin_cos(theta):
    n = jnp.round(theta * 0.6366197723675814)
    r = theta - n * 1.5703125
    r = r - n * 4.837512969970703e-4
    r = r - n * 7.549789948768648e-8
    r = jnp.clip(r, -0.8, 0.8)
    q = n.astype(I32)
    z = r * r
    s = r + r * z * (-1.6666654611e-1 + z * (8.3321608736e-3 + z * -1.9515295891e-4))
    c = 1.0 - 0.5 * z + z * z * (
        4.166664568298827e-2 + z * (-1.388731625493765e-3 + z * 2.443315711809948e-5)
    )
    odd = (q & 1) == 1
    sin, cos = jnp.where(odd, c, s), jnp.where(odd, s, c)
    sin = jnp.where((q & 2) == 2, -sin, sin)
    cos = jnp.where(((q + 1) & 2) == 2, -cos, cos)
    return sin, cos


def turned(ids, coords, rows, rot):
    width = ids.shape[1]
    index, upper = ids & (LANES - 1), ids >= LANES

    def looked_up(k):
        pieces = []
        for c in range(width // LANES):
            at = slice(c * LANES, (c + 1) * LANES)
            low, high = gather_lanes(rows[2 * k], index[:, at]), gather_lanes(rows[2 * k + 1], index[:, at])
            pieces.append(jnp.where(upper[:, at], high, low))
        return jnp.concatenate(pieces, axis=1)

    x, mx, y, my = coords
    kx, ky, kq = looked_up(0), looked_up(1), looked_up(2)
    mx = mx + (kx + kq * x)
    my = my + (ky - kq * y)
    action = x * x + mx * mx + y * y + my * my
    sin, cos = sin_cos(DETUNE * action)
    cos_x, sin_x, cos_y, sin_y = (jnp.concatenate([r] * (width // LANES), axis=1) for r in rot)
    x, mx = cos * x + sin * mx, cos * mx - sin * x
    y, my = cos * y + sin * my, cos * my - sin * y
    x, mx = cos_x * x + sin_x * mx, cos_x * mx - sin_x * x
    y, my = cos_y * y + sin_y * my, cos_y * my - sin_y * y
    return x, mx, y, my


def track_kernel(
    rings,
    phase_hbm,
    advance_hbm,
    hist_hbm,
    wake_hbm,
    dipole_hbm,
    quad_hbm,
    ids_hbm,
    mid_ref,
    next_ids,
    rows_ref,
    rot,
    cent_ref,
    phase_ref,
    first_ids,
    advance_ref,
    hist_ref,
    wake_ref,
    dipole_ref,
    quad_ref,
    msg,
    landed,
    hist_src,
    hist_all,
    sum_src,
    sum_all,
    tab_src,
    tab_all,
    ext,
    toep,
    partial,
    split,
    load,
    msg_send,
    msg_recv,
    sum_send,
    sum_recv,
    tab_send,
    tab_recv,
):
    n_bunch, n_mp = rings
    me_b, me_m = lax.axis_index("bunch"), lax.axis_index("mp")
    bunches, parts = mid_ref.shape[1], mid_ref.shape[2]
    turns_back = hist_ref.shape[2]
    share = turns_back // n_mp
    scale = 1.0 / (parts * n_mp)

    def by_reach(n, step):
        return sorted(range(1, n), key=lambda k: -min(k // step, (n - k) // step))

    across, along = by_reach(n_bunch, 1), by_reach(n_mp, 2)
    loads = [
        pltpu.make_async_copy(source, target, load.at[k])
        for k, (source, target) in enumerate(
            (
                (phase_hbm.at[0], phase_ref.at[0]),
                (phase_hbm.at[2], phase_ref.at[2]),
                (ids_hbm.at[0], first_ids),
                (hist_hbm, hist_ref),
                (wake_hbm, wake_ref),
                (advance_hbm, advance_ref),
                (dipole_hbm, dipole_ref),
                (quad_hbm, quad_ref),
                (phase_hbm.at[1], phase_ref.at[1]),
                (phase_hbm.at[3], phase_ref.at[3]),
                (ids_hbm.at[1], next_ids),
            )
        )
    ]
    for copy in loads[:4]:
        copy.start()

    barrier = pltpu.get_barrier_semaphore()
    for k, n in zip(along, across):
        pl.semaphore_signal(barrier, inc=1, device_id={"mp": lax.rem(me_m + k, n_mp)})
        pl.semaphore_signal(barrier, inc=1, device_id={"bunch": lax.rem(me_b + n, n_bunch)})

    for copy in loads[4:]:
        copy.start()

    class Exchange:
        def __init__(self, axis, me, offsets, source, target, send, recv):
            self.axis, self.me, self.offsets = axis, me, offsets
            self.source, self.target, self.send, self.recv = source, target, send, recv

        def start(self):
            for k in self.offsets:
                pltpu.make_async_remote_copy(
                    src_ref=self.source,
                    dst_ref=self.target.at[self.me],
                    send_sem=self.send,
                    recv_sem=self.recv,
                    device_id={self.axis: lax.rem(self.me + k, len(self.offsets) + 1)},
                ).start()

        def all_of_them(self):
            block = self.target.at[pl.ds(0, len(self.offsets))]
            return pltpu.make_async_remote_copy(
                src_ref=block,
                dst_ref=block,
                send_sem=self.send,
                recv_sem=self.recv,
                device_id={self.axis: lax.rem(self.me + 1, len(self.offsets) + 1)},
            )

        def arrive(self):
            self.all_of_them().wait_recv()

        def leave(self):
            self.all_of_them().wait_send()

    sum_x = [
        Exchange("bunch", me_b, across, source, target, sum_send.at[t], sum_recv.at[t])
        for t, (source, target) in enumerate(((hist_src, hist_all), (sum_src, sum_all)))
    ]
    tab_x = [
        Exchange("mp", me_m, along, tab_src.at[t], tab_all.at[t], tab_send.at[t], tab_recv.at[t])
        for t in range(TURNS)
    ]
    msg_x = [
        Exchange("mp", me_m, along, None, landed.at[t], msg_send.at[t], msg_recv.at[t]) for t in range(TURNS)
    ]

    def send_msg(turn, b):
        pltpu.make_async_remote_copy(
            src_ref=msg.at[turn, b],
            dst_ref=landed.at[turn, me_m],
            send_sem=msg_send.at[turn],
            recv_sem=msg_recv.at[turn],
            device_id={"mp": b},
        ).start()

    row8, lane8 = iota((8, LANES), 0), iota((8, LANES), 1)
    place = lax.rem(me_b, 8) * bunches

    def pieces(block):
        parts = []
        for _ in range(3):
            parts.append(block.astype(BF16))
            block = block - parts[-1].astype(F32)
        return jnp.concatenate(parts, axis=1)

    def to_lanes(chosen, block):
        rows = lax.dot_general(
            jnp.concatenate([chosen.astype(BF16)] * 3, axis=1), pieces(block), NT, preferred_element_type=F32
        )
        return jnp.concatenate([rows, jnp.zeros((16, LANES - block.shape[0]), F32)], axis=1)

    def sum_rows(turn, sums_x, sums_y):
        both = to_lanes(jnp.ones((16, LANES), F32), jnp.concatenate([sums_x, sums_y], axis=0) * scale)[:8]
        partial[turn] = pltpu.roll(both, 2 * bunches, 1)[:1]
        x = pltpu.roll(jnp.where(lane8 < bunches, both, 0.0), place, 1)
        y = jnp.where((lane8 >= bunches) & (lane8 < 2 * bunches), both, 0.0)
        y = pltpu.roll(y, lax.rem(place + LANES - bunches, LANES), 1)
        rows = jnp.where(row8 == 0, x, y)[:2]
        return rows

    def lane_sums(p):
        def step(c, acc):
            return acc + phase_ref[p, :, pl.ds(pl.multiple_of(c * LANES, LANES), LANES)]

        return lax.fori_loop(0, parts // LANES, step, jnp.zeros((bunches, LANES), F32), unroll=8)

    loads[3].wait()
    r, c = iota((16, 2 * turns_back), 0), iota((16, 2 * turns_back), 1)
    chosen = jnp.where(c == (r // share) * turns_back + me_m * share + (r & (share - 1)), 1.0, 0.0)
    own = to_lanes(chosen, jnp.concatenate([hist_ref[0], hist_ref[1]], axis=1))[: 2 * share]
    own = pltpu.roll(own, place, 1)

    loads[0].wait()
    loads[1].wait()
    loads[2].wait()

    iota_c = iota((COARSE, CHUNK), 0)
    iota_f = iota((FINE, CHUNK), 0)
    own_lanes = lax.shift_right_logical(lane8, 5) == lax.shift_right_logical(row8, 1)

    def bin_bunch(ids_ref, source, b):
        acc = None
        for c in range(parts // CHUNK):
            at = pl.ds(c * CHUNK, CHUNK)
            ids = ids_ref[pl.ds(b, 1), at]
            x = source[0, pl.ds(b, 1), at]
            y = source[2, pl.ds(b, 1), at]
            coarse = iota_c == ((lax.shift_right_logical(ids, 4) & 6) | lax.shift_right_logical(ids, 7))
            fine = jnp.where(iota_f == (ids & (FINE - 1)), 1.0, 0.0).astype(BF16)
            rows = [jnp.where(coarse, 1.0, 0.0)]
            for v in (*two_pieces(x), *two_pieces(y)):
                rows.append(jnp.where(coarse, jnp.broadcast_to(v, (COARSE, CHUNK)), 0.0))
            weighted = jnp.concatenate(rows, axis=0).astype(BF16)
            part = lax.dot_general(weighted, fine, NT, preferred_element_type=F32)
            acc = part if acc is None else acc + part
        return acc

    def as_tile(acc):
        tiles = []
        for v in (acc[8:16] + acc[16:24], acc[24:32] + acc[32:40], acc[0:8]):
            v = jnp.where(own_lanes, jnp.concatenate([v] * 4, axis=1), 0.0)
            v = v + pltpu.roll(v, 2, 0)
            tiles.append(v + pltpu.roll(v, 4, 0))
        tile = jnp.where(row8 < 2, tiles[0], jnp.where(row8 < 4, tiles[1], tiles[2]))
        return (tile * scale)[:6]

    chips, chip = n_mp // 2, lax.div(me_m, 2)
    core = lax.rem(me_m, 2)

    def owner(k):
        u, side = k // 2, k % 2
        reach = (chips // 2 - (u + 1) // 2) * (2 * (u % 2) - 1)
        there = lax.rem(chip + reach + chips, chips)
        return there * 2 + lax.rem(core + 1 + side, 2)

    def bin_block(turn, ids_ref, source, first, count):
        owners = [owner(first + k) for k in range(count)]
        tiles = [as_tile(bin_bunch(ids_ref, source, b)) for b in owners]
        if first + count == bunches:
            landed[turn, me_m] = tiles[-1]
            owners = owners[:-1]
        for b, tile in zip(owners, tiles):
            msg[turn, b] = tile
        return owners

    def send_all(turn, owners):
        for b in owners:
            send_msg(turn, b)

    def toeplitz_rows(r, half, sub):
        d = me_b * bunches + sub * 8 + row8 - (LANES * half + lane8) - 1
        c = d & (SLICES - 1)
        index = c & (LANES - 1)
        low = jnp.broadcast_to(wake_ref[pl.ds(2 * r, 1), :], (8, LANES))
        high = jnp.broadcast_to(wake_ref[pl.ds(2 * r + 1, 1), :], (8, LANES))
        return jnp.where(c >= LANES, gather_lanes(high, index), gather_lanes(low, index)), d >= 0

    def collected(ref):
        halves = []
        for half in range(2):
            total = ref[8 * half]
            for k in range(1, 8):
                total = total + ref[8 * half + k]
            halves.append(total)
        return halves

    def row_of(tile, k):
        return jnp.broadcast_to(tile[k : k + 1, :], (8, LANES))

    def far_row(turn):
        return to_lanes(jnp.ones((16, LANES), F32), ext[turn])[:1] + partial[turn]

    def lay_wake():
        loads[4].wait()
        kept = jnp.where(me_m == n_mp - 1, 0.0, 1.0)
        first = me_m * share
        for sub in range(2):
            at = pl.ds(8 * sub, 8)
            for half in range(2):
                g0, upper = toeplitz_rows(0, half, sub)
                g1, _ = toeplitz_rows(1, half, sub)
                toep[0, half, at, :] = jnp.where(upper, g0, 0.0)
                toep[1, half, at, :] = jnp.where(upper, g1, g0)
                g = [
                    toeplitz_rows(jnp.minimum(first + k, turns_back), half, sub)[0]
                    for k in range(share + 2)
                ]
                for k in range(share + 1):
                    near = jnp.where(upper, g[k + 1], g[k])
                    toep[2 + k, half, at, :] = near
                toep[2 + share + 1, half, at, :] = near * kept

    def far_first():
        sum_x[0].arrive()
        tiles = collected(hist_all)
        for sub in range(2):
            at = pl.ds(8 * sub, 8)
            for p in range(2):
                total = jnp.zeros((8, LANES), F32)
                for half in range(2):
                    total = total + toep[0, half, at, :] * row_of(tiles[half], 2 * share + p)
                    for k in range(share):
                        total = total + toep[2 + k, half, at, :] * row_of(tiles[half], p * share + k)
                ext[0, pl.ds(p * bunches + 8 * sub, 8), :] = total
        tab_src[0, 6:7, :] = far_row(0)
        return tiles

    def far_later(tiles):
        for sub in range(2):
            at = pl.ds(8 * sub, 8)
            for p in range(2):
                total = jnp.zeros((8, LANES), F32)
                for half in range(2):
                    total = total + toep[1, half, at, :] * row_of(tiles[half], 2 * share + p)
                    for k in range(share):
                        later = toep[3 + k if k < share - 1 else 3 + share, half, at, :]
                        total = total + later * row_of(tiles[half], p * share + k)
                ext[1, pl.ds(p * bunches + 8 * sub, 8), :] = total

    def far_second():
        sum_x[1].arrive()
        cent = collected(sum_all)
        for sub in range(2):
            for p in range(2):
                at = pl.ds(p * bunches + 8 * sub, 8)
                total = ext[1, at, :]
                for half in range(2):
                    total = total + toep[0, half, pl.ds(8 * sub, 8), :] * row_of(cent[half], p)
                ext[1, at, :] = total
        tab_src[1, 6:7, :] = far_row(1)

    def kick_table(turn):
        msg_x[turn].arrive()
        total = added([landed[turn, k] for k in range(n_mp)])
        total = jnp.concatenate([total, jnp.zeros((2, LANES), F32)], axis=0)
        wide = jnp.concatenate([total, pltpu.roll(total, 7, 0)], axis=1)
        stack = []
        for _ in range(3):
            stack.append(wide.astype(BF16).astype(F32))
            wide = wide - stack[-1]
        stack = jnp.concatenate(stack, axis=0).astype(BF16)

        def product(which):
            out = None
            for k in reversed(range(3)):
                part = jnp.dot(stack, split[which, k], preferred_element_type=F32)
                for n in reversed(range(3 - k)):
                    block = part[8 * n : 8 * n + 8]
                    out = block if out is None else out + block
            return out

        dip, quad = product(0), product(1)
        low, high = dip[:, :LANES], dip[:, LANES:]
        tab_src[turn, :6, :] = jnp.concatenate(
            [low[0:1], high[0:1], low[2:3], high[2:3], quad[4:5, :LANES], quad[4:5, LANES:]], axis=0
        )
        tab_x[turn].start()
        tab_all[turn, me_m] = tab_src[turn]

    full_row, full_lane = iota((bunches, LANES), 0), iota((bunches, LANES), 1)

    def lay_rows(turn):
        tab_x[turn].arrive()
        total = added([tab_all[turn, k, 6:7, :] for k in range(n_mp)])
        for p in range(2):
            cent_ref[p, turn : turn + 1, :] = pltpu.roll(total, LANES - (2 + p) * bunches, 1)[:, :bunches]
        total = jnp.broadcast_to(total, (bunches, LANES))
        far = [
            jnp.sum(jnp.where(full_lane == full_row + p * bunches, total, 0.0), axis=1, keepdims=True)
            for p in range(2)
        ]

        def column(k):
            return jnp.concatenate([tab_all[turn, n, k : k + 1, :] for n in range(bunches)], axis=0)

        for k in range(6):
            row = column(k)
            rows_ref[k] = row + far[k // 2] if k < 4 else row

    half = bunches // 2
    first_sums = (lane_sums(0), lane_sums(2))
    owners = bin_block(0, first_ids, phase_ref, 0, half)
    own = jnp.concatenate([own, sum_rows(0, *first_sums)], axis=0)
    hist_src[...] = own
    hist_all[me_b] = own
    owners = owners + bin_block(0, first_ids, phase_ref, half, half)
    pl.semaphore_wait(barrier, n_mp + n_bunch - 2)
    send_all(0, owners[:half])
    sum_x[0].start()
    send_all(0, owners[half:])
    lay_wake()

    loads[5].wait()
    for p in range(2):
        wide = jnp.concatenate([advance_ref[p : p + 1, :], jnp.zeros((1, LANES - bunches), F32)], axis=1)
        wide = jnp.broadcast_to(wide, (bunches, LANES))
        column = jnp.sum(jnp.where(full_row == full_lane, wide, 0.0), axis=1, keepdims=True)
        sin, cos = sin_cos(jnp.broadcast_to(column, (bunches, LANES)))
        rot[2 * p] = cos
        rot[2 * p + 1] = sin

    for k, ref in enumerate((dipole_ref, quad_ref)):
        loads[6 + k].wait()
        rest = jnp.transpose(ref[...])
        for n in range(3):
            piece = rest.astype(BF16)
            split[k, n] = piece
            rest = rest - piece.astype(F32)
    tiles = far_first()
    kick_table(0)
    far_later(tiles)
    loads[8].wait()
    loads[9].wait()
    loads[10].wait()
    lay_rows(0)

    sums = []
    for g in range(bunches // GROUP):
        at = pl.ds(g * GROUP, GROUP)
        rows = [rows_ref[k, at, :] for k in range(6)]
        turn_by = [rot[k, at, :] for k in range(4)]

        def kick(c, acc):
            lanes = pl.ds(pl.multiple_of(c * WIDTH, WIDTH), WIDTH)
            new = turned(first_ids[at, lanes], [phase_ref[k, at, lanes] for k in range(4)], rows, turn_by)
            for k in range(4):
                mid_ref[k, at, lanes] = new[k]
            acc = list(acc)
            for s in range(WIDTH // LANES):
                cut = slice(s * LANES, (s + 1) * LANES)
                acc = [acc[0] + new[0][:, cut], acc[1] + new[2][:, cut]]
            return tuple(acc)

        zero = jnp.zeros((GROUP, LANES), F32)
        sums.append(lax.fori_loop(0, parts // WIDTH, kick, (zero, zero), unroll=8))
    sums = [jnp.concatenate([s[p] for s in sums], axis=0) for p in range(2)]
    rows = sum_rows(1, *sums)
    sum_src[...] = rows
    sum_all[me_b] = rows
    sum_x[1].start()
    first = 0
    for count in BLOCKS:
        send_all(1, bin_block(1, next_ids, mid_ref, first, count))
        first += count
    far_second()
    kick_table(1)
    lay_rows(1)

    for turn in range(TURNS):
        for exchange in (msg_x[turn], tab_x[turn], sum_x[turn]):
            exchange.leave()


def last_kernel(mid_ref, ids_ref, rows_ref, rot, cent_in, out_hbm, cent_hbm, out_ref, cent_ref, sems):
    bunches, parts = mid_ref.shape[1], mid_ref.shape[2]
    cent_ref[...] = cent_in[...]
    copies = [pltpu.make_async_copy(cent_ref, cent_hbm, sems.at[0])]
    copies[0].start()
    span = parts // SPANS
    for g in range(bunches // GROUP):
        at = pl.ds(g * GROUP, GROUP)
        rows = [rows_ref[k, at, :] for k in range(6)]
        turn_by = [rot[k, at, :] for k in range(4)]
        for part in range(SPANS):

            def kick(c, _):
                lanes = pl.ds(pl.multiple_of(part * span + c * WIDTH, WIDTH), WIDTH)
                new = turned(ids_ref[at, lanes], [mid_ref[k, at, lanes] for k in range(4)], rows, turn_by)
                for k in range(4):
                    out_ref[k, at, lanes] = new[k]
                return 0

            lax.fori_loop(0, span // WIDTH, kick, 0, unroll=4)
            block = (slice(None), at, pl.ds(part * span, span))
            copies.append(
                pltpu.make_async_copy(out_ref.at[block], out_hbm.at[block], sems.at[len(copies)])
            )
            copies[-1].start()
    for copy in copies:
        copy.wait()


def body(phase_space, phase_advance, centroid_history, lr_wake, sr_dipole, sr_quad, slice_ids):
    n_bunch, n_mp = lax.axis_size("bunch"), lax.axis_size("mp")
    bunches, parts = phase_space.shape[1:]
    turns_back = centroid_history.shape[1]
    wake_rows = lr_wake.shape[0] // LANES
    vmem, hbm = pl.BlockSpec(memory_space=pltpu.VMEM), pl.BlockSpec(memory_space=pltpu.HBM)
    dma = pltpu.SemaphoreType.DMA

    def held(*shape, dtype=F32):
        return pltpu.VMEM(shape, dtype)

    cent_shape = jax.ShapeDtypeStruct((2, TURNS, bunches), F32)
    state = pl.pallas_call(
        functools.partial(track_kernel, (n_bunch, n_mp)),
        out_shape=(
            jax.ShapeDtypeStruct(phase_space.shape, F32),
            jax.ShapeDtypeStruct((bunches, parts), I32),
            jax.ShapeDtypeStruct((6, bunches, LANES), F32),
            jax.ShapeDtypeStruct((4, bunches, LANES), F32),
            cent_shape,
        ),
        in_specs=[hbm] * 7,
        out_specs=(vmem,) * 5,
        scratch_shapes=[
            held(4, bunches, parts),
            held(bunches, parts, dtype=I32),
            held(2, bunches),
            held(2, bunches, turns_back),
            held(wake_rows, LANES),
            held(SLICES, SLICES),
            held(SLICES, SLICES),
            held(TURNS, bunches, 6, LANES),
            held(TURNS, n_mp, 6, LANES),
            held(2 + 2 * turns_back // n_mp, LANES),
            held(n_bunch, 2 + 2 * turns_back // n_mp, LANES),
            held(2, LANES),
            held(n_bunch, 2, LANES),
            held(TURNS, 7, LANES),
            held(TURNS, n_mp, 7, LANES),
            held(TURNS, 2 * bunches, LANES),
            held(4 + turns_back // n_mp, 2, bunches, LANES),
            held(TURNS, 1, LANES),
            held(2, 3, SLICES, SLICES, dtype=BF16),
            dma((11,)),
            dma((TURNS,)),
            dma((TURNS,)),
            dma((TURNS,)),
            dma((TURNS,)),
            dma((TURNS,)),
            dma((TURNS,)),
        ],
        compiler_params=pltpu.CompilerParams(
            collective_id=0, has_side_effects=True, vmem_limit_bytes=40 << 20
        ),
        cost_estimate=pl.CostEstimate(flops=4 * 65536 * 256, bytes_accessed=3 << 20, transcendentals=0),
        name="track",
    )(
        *(
            pltpu.with_memory_space_constraint(a, pltpu.HBM)
            for a in (
                phase_space,
                phase_advance,
                jnp.transpose(centroid_history, (0, 2, 1)),
                lr_wake.reshape(-1, LANES),
                sr_dipole,
                sr_quad,
                slice_ids,
            )
        )
    )
    return tuple(
        pl.pallas_call(
            last_kernel,
            out_shape=(jax.ShapeDtypeStruct(phase_space.shape, F32), cent_shape),
            in_specs=[vmem] * 5,
            out_specs=(hbm, hbm),
            scratch_shapes=[
                held(*phase_space.shape),
                held(2, TURNS, bunches),
                dma((1 + SPANS * bunches // GROUP,)),
            ],
            compiler_params=pltpu.CompilerParams(vmem_limit_bytes=16 << 20),
            cost_estimate=pl.CostEstimate(flops=100 * 65536, bytes_accessed=1 << 20, transcendentals=0),
            name="last",
        )(*state)
    )


def solution(mesh):
    placed = (
        P(None, "bunch", "mp"),
        P(None, "bunch"),
        P(None, None, "bunch"),
        P(),
        P(),
        P(),
        P(None, "bunch", "mp"),
    )
    return jax.shard_map(
        body,
        mesh=mesh,
        in_specs=placed,
        out_specs=(P(None, "bunch", "mp"), P(None, None, "bunch")),
        check_vma=False,
    )
```
